32 devices in a mesh: fsdp: 8 (over y, x, core), tp: 4 (over z).
Axes of the slice: x: 2, y: 2, z: 4, core: 2. Of those that a mesh axis runs over, the one named last changes fastest.
Arguments:
- roll_rows: bfloat16 [256, 72, 3584], P('fsdp', None, 'tp'), may hold values from -60 to 60
- dest: int32 [256], P('fsdp'), may hold values from 0 to 255, as said below
- lengths: int32 [8, 32], P('fsdp'), may hold values from 1 to 72, 768 in all within a row
- clusters: int32 [256], P('fsdp'), may hold values from 0 to 3
- log_prob_grad: bfloat16 [6144, 3584], P('fsdp', 'tp'), may hold values from -6 to 6
- gain: bfloat16 [3584], replicated, may hold values from 0.5 to 1.5
- w_q: bfloat16 [3584, 2048], P('fsdp', 'tp'), may hold values from -1 to 1
- w_k: bfloat16 [3584, 512], P('fsdp', 'tp'), may hold values from -1 to 1
- w_v: bfloat16 [3584, 512], P('fsdp', 'tp'), may hold values from -0.09375 to 0.09375
- w_o_t: bfloat16 [3584, 2048], P('fsdp', 'tp'), may hold values from -0.125 to 0.125
Outputs:
- input_grad: bfloat16 [6144, 3584], P('fsdp', 'tp')
- grad_q: bfloat16 [3584, 2048], P('fsdp', 'tp')
- grad_k: bfloat16 [3584, 512], P('fsdp', 'tp')
- grad_v: bfloat16 [3584, 512], P('fsdp', 'tp')
- grad_o_t: bfloat16 [3584, 2048], P('fsdp', 'tp')
The draws below stay inside these ranges and needn't reach their ends.
Inputs may be any that keep to these rules, and one draw needn't show every extreme that they name: dest is a permutation; every rollout replica hands exactly 4 completions to every learner, and every learner trains 32 completions. Each learner's 32 lengths sum to 768.
All inputs are finite; a program needn't handle non-finite values.
Results may differ from the reference program's by a relative error of at most 0.03.
Values may be sent and summed in bfloat16 or wider, within the bound.
No kernel may reach another device: no remote copies, remote signals or barrier semaphores. Data moves between devices by JAX's collectives and lax.ppermute only.
A program may use at most 128 MiB of HBM per device.

```python
import math
import jax
import jax.numpy as jnp
import numpy as np
from jax import lax

D = 3584
KEY_VALUE_HEADS = 4
HD = 128
QUERY_HEADS = 16
TOK_DEV = 768
SEQ_DEV = 32
GSIZE = 16
NCLUST = 4
TOKENS = 6144
SEQS = 256
MAXLEN = 72
SEQ_PAIR = 4
QW = 2048
KW = 512
N_FSDP = 8
N_TP = 4


def draw_roll_rows(key, part):
    shape_all = (SEQS, MAXLEN, D)
    row_scale = jnp.exp(jax.random.uniform(jax.random.fold_in(key, 2), (SEQS, MAXLEN, 1), jnp.float32, math.log(0.3), math.log(3.0)))
    col_scale = jnp.exp(jax.random.uniform(jax.random.fold_in(key, 3), (D,), jnp.float32, math.log(0.3), math.log(3.0)))
    noise = jnp.clip(jax.random.normal(jax.random.fold_in(key, 1), shape_all, jnp.float32), -6.0, 6.0)
    values = noise * row_scale * col_scale
    return values.astype(jnp.bfloat16)


def draw_w_q(key, part):
    values = jnp.clip(jax.random.normal(jax.random.fold_in(key, 11), (D, QW), jnp.float32), -6.0, 6.0)
    return (values * D ** (-0.5)).astype(jnp.bfloat16)


def draw_w_k(key, part):
    values = jnp.clip(jax.random.normal(jax.random.fold_in(key, 12), (D, KW), jnp.float32), -6.0, 6.0)
    return (values * D ** (-0.5)).astype(jnp.bfloat16)


def draw_dest(key, part):
    seq_order = jax.random.permutation(jax.random.fold_in(key, 21), SEQ_DEV).astype(jnp.int32)
    residue = seq_order % N_FSDP
    seq_index = jnp.arange(SEQ_DEV, dtype=jnp.int32)
    same_residue = residue[:, None] == residue[None, :]
    rank_of = jnp.sum((same_residue & (seq_index[None, :] < seq_index[:, None])).astype(jnp.int32), axis=1)
    learner = jnp.arange(N_FSDP, dtype=jnp.int32)[:, None]
    replica = (learner + residue[None, :]) % N_FSDP
    local_slot = learner * SEQ_PAIR + rank_of[None, :]
    shuffle_key = jax.random.fold_in(key, 22)
    shuffles = jax.vmap(lambda replica_number: jax.random.permutation(jax.random.fold_in(shuffle_key, replica_number), SEQ_DEV))(jnp.arange(N_FSDP, dtype=jnp.int32)).astype(jnp.int32)
    roll_slot = replica * SEQ_DEV + shuffles[replica, local_slot]
    return jnp.zeros((SEQS,), jnp.int32).at[roll_slot.reshape(SEQS)].set(jnp.arange(SEQS, dtype=jnp.int32))


def plant(values, stream_key, smallest, high):
    place = [jax.random.randint(jax.random.fold_in(stream_key, axis), (), 0, length) for axis, length in enumerate(values.shape)]
    longest = values.shape.index(max(values.shape))
    next_to = place[:longest] + [(place[longest] + 1) % values.shape[longest]] + place[longest + 1:]
    return values.at[tuple(place)].set(smallest).at[tuple(next_to)].set(high)


def level_of(own_key, extent, pieces, smallest, largest):
    level = 1.0
    for dim, shards_of in pieces:
        steps = jax.random.uniform(jax.random.fold_in(jax.random.fold_in(own_key, 6), dim), (shards_of,), jnp.float32, smallest / len(pieces), largest / len(pieces))
        level = level * jnp.repeat(jnp.exp(steps), extent[dim] // shards_of).reshape((-1,) + (1,) * (len(extent) - 1 - dim))
    return level


def rank_table(number_of, lean):
    portions = [(1 << 20) // math.isqrt(grade ** lean) + 1 for grade in range(1, number_of + 1)]
    scale = 1 + sum(portions) // (1 << 30)
    return np.cumsum(np.array([max(1, weight // scale) for weight in portions]))


def skewed_ids(rng, dims, amount, lean):
    grid = rank_table(amount, lean)
    ticket = jax.random.randint(jax.random.fold_in(rng, 1), dims, 0, int(grid[amount - 1]))
    standing = jnp.searchsorted(jnp.asarray(grid, jnp.int32), ticket, side="right")
    return jax.random.permutation(jax.random.fold_in(rng, 2), amount)[standing].astype(jnp.int32)


def split_up(count, total, bound, slope):
    weights = [(1 << 20) // math.isqrt(grade ** slope) + 1 for grade in range(2, count + 1)]
    spare, counts = total - bound - (count - 1), [1] * (count - 1)
    while spare > 0:
        candidates = [i for i in range(count - 1) if counts[i] < bound]
        whole, remaining = sum([weights[i] for i in candidates]), spare
        for i in candidates:
            more = min(bound - counts[i], max(1, remaining * weights[i] // whole), spare)
            counts[i] = counts[i] + more
            spare = spare - more
    return np.array([bound] + counts)


def uneven_parts(own_key, amount, total, limit, skew):
    if amount == 2:
        one = jax.random.randint(own_key, (), max(1, total - limit), min(limit, total - 1) + 1)
        return jnp.stack([one, total - one])
    sizes = jnp.asarray(split_up(amount, total, limit, skew), jnp.int32)
    twos = (amount - 1) // 2
    donor, sink = sizes[1:1 + 2 * twos:2], sizes[2:2 + 2 * twos:2]
    room = jnp.minimum(donor - 1, limit - sink)
    moved = jax.random.randint(jax.random.fold_in(own_key, 1), (twos,), 0, 1 << 20) % (room + 1)
    sizes = sizes.at[1:1 + 2 * twos:2].set(donor - moved).at[2:2 + 2 * twos:2].set(sink + moved)
    return sizes[jax.random.permutation(jax.random.fold_in(own_key, 2), amount)]


def normal_values(rng, shape, scale, most, pieces=(), kind=jnp.bfloat16):
    array = scale * jax.random.normal(rng, shape, jnp.float32)
    if pieces:
        array = array * level_of(rng, shape, pieces, -0.22, 0.18)
    return jnp.clip(array, -most, most).astype(kind)


def setup_inputs(seed: int = 0) -> dict:
    arg_keys = jax.random.split(jax.random.key(seed), 11)
    return {
        "roll_rows": draw_roll_rows(jax.random.fold_in(arg_keys[10], 71), 0),
        "dest": draw_dest(jax.random.fold_in(arg_keys[10], 71), 0),
        "lengths": jax.vmap(lambda own: uneven_parts(own, SEQ_DEV, TOK_DEV, MAXLEN, 2))(jax.random.split(arg_keys[2], N_FSDP)).reshape((N_FSDP, SEQ_DEV)).astype(jnp.int32),
        "clusters": plant(skewed_ids(arg_keys[3], (SEQS,), NCLUST, 2), jax.random.fold_in(arg_keys[3], 3), 0, NCLUST - 1).astype(jnp.int32),
        "log_prob_grad": normal_values(arg_keys[4], (TOKENS, D), 1.0, 6.0, ((0, 8), (1, 4))),
        "gain": jnp.clip(1.0 + 0.1 * jax.random.normal(arg_keys[5], (D,), jnp.float32), 0.5, 1.5).astype(jnp.bfloat16),
        "w_q": draw_w_q(jax.random.fold_in(arg_keys[10], 71), 0),
        "w_k": draw_w_k(jax.random.fold_in(arg_keys[10], 71), 0),
        "w_v": normal_values(arg_keys[8], (D, KW), D ** -0.5, 0.09375, ((0, 8), (1, 4))),
        "w_o_t": normal_values(arg_keys[9], (D, QW), QW ** -0.5, 0.125, ((0, 8), (1, 4))),
    }


ROPE_BASE = 1000000.0
NORM_EPSILON = 1e-06

def wire_round(values):
    return lax.optimization_barrier(values.astype(jnp.bfloat16)).astype(jnp.float32)

def contract_rows(left, right):
    return lax.dot_general(left, right, (((0,), (0,)), ((), ())), preferred_element_type=jnp.float32)

def times_trans(left, right):
    return lax.dot_general(left, right, (((1,), (1,)), ((), ())), preferred_element_type=jnp.float32)

def rotary_tables(position):
    half_width = HD // 2
    frequency = ROPE_BASE ** (-(2.0 * jnp.arange(half_width, dtype=jnp.float32)) / HD)
    angles = position.astype(jnp.float32)[:, None] * frequency[None, :]
    return (jnp.cos(angles)[:, None, :], jnp.sin(angles)[:, None, :])

def rotate(values, rope_cos, rope_sin):
    half_width = values.shape[-1] // 2
    first_half = values[..., :half_width]
    second_half = values[..., half_width:]
    return jnp.concatenate([first_half * rope_cos - second_half * rope_sin, second_half * rope_cos + first_half * rope_sin], axis=-1)

def inverse_rotate(values, rope_cos, rope_sin):
    half_width = values.shape[-1] // 2
    first_half = values[..., :half_width]
    second_half = values[..., half_width:]
    return jnp.concatenate([first_half * rope_cos + second_half * rope_sin, second_half * rope_cos - first_half * rope_sin], axis=-1)

def packed_layout(lengths_row):
    sequence_ends = jnp.cumsum(lengths_row).astype(jnp.int32)
    sequence_starts = sequence_ends - lengths_row
    row_index = jnp.arange(TOK_DEV, dtype=jnp.int32)
    segment = lax.optimization_barrier(jnp.sum((sequence_ends[None, :] <= row_index[:, None]).astype(jnp.int32), axis=1))
    one_hot = segment[:, None] == jnp.arange(SEQ_DEV, dtype=jnp.int32)[None, :]
    position = row_index - lax.optimization_barrier(jnp.sum(jnp.where(one_hot, sequence_starts[None, :], 0), axis=1)).astype(jnp.int32)
    return (segment, position, one_hot)

def group_pass(normed, unit_rows, inverse_norm, gain_float, grad_round, rope_cos, rope_sin, allowed, weight_q, weight_k, weight_v, weight_o):
    row_count = normed.shape[0]
    key_heads = weight_k.shape[1] // HD
    queries_per_group = QUERY_HEADS // KEY_VALUE_HEADS
    query_lin = jnp.dot(normed, weight_q, preferred_element_type=jnp.float32)
    key_lin = jnp.dot(normed, weight_k, preferred_element_type=jnp.float32)
    value_lin = jnp.dot(normed, weight_v, preferred_element_type=jnp.float32)
    query_rot = rotate(query_lin.reshape(row_count, key_heads * queries_per_group, HD), rope_cos, rope_sin).astype(jnp.bfloat16).reshape(row_count, key_heads, queries_per_group, HD)
    key_rot = rotate(key_lin.reshape(row_count, key_heads, HD), rope_cos, rope_sin).astype(jnp.bfloat16)
    value_b = value_lin.reshape(row_count, key_heads, HD).astype(jnp.bfloat16)
    scores = jnp.einsum('ighd,jgd->ghij', query_rot.astype(jnp.float32), key_rot.astype(jnp.float32)) * HD ** (-0.5)
    scores = jnp.where(allowed, scores, -1e+30)
    row_max = lax.optimization_barrier(jnp.max(scores, axis=-1, keepdims=True))
    exp_scores = jnp.where(allowed, jnp.exp(scores - row_max), 0.0)
    attn_prob = exp_scores / lax.optimization_barrier(jnp.sum(exp_scores, axis=-1, keepdims=True))
    attn_prob_b = attn_prob.astype(jnp.bfloat16)
    attn_out = jnp.einsum('ghij,jgd->ighd', attn_prob_b.astype(jnp.float32), value_b.astype(jnp.float32))
    attn_out = attn_out.reshape(row_count, key_heads * queries_per_group * HD).astype(jnp.bfloat16)
    grad_wo = contract_rows(grad_round, attn_out)
    grad_attn = jnp.dot(grad_round, weight_o, preferred_element_type=jnp.float32).astype(jnp.bfloat16)
    grad_attn = grad_attn.reshape(row_count, key_heads, queries_per_group, HD)
    grad_prob = jnp.einsum('ighd,jgd->ghij', grad_attn.astype(jnp.float32), value_b.astype(jnp.float32))
    grad_value_f = jnp.einsum('ghij,ighd->jgd', attn_prob_b.astype(jnp.float32), grad_attn.astype(jnp.float32))
    row_delta = lax.optimization_barrier(jnp.sum(attn_prob * grad_prob, axis=-1, keepdims=True))
    grad_score = (attn_prob * (grad_prob - row_delta) * HD ** (-0.5)).astype(jnp.bfloat16)
    grad_qrot = jnp.einsum('ghij,jgd->ighd', grad_score.astype(jnp.float32), key_rot.astype(jnp.float32))
    grad_qrot = grad_qrot.reshape(row_count, key_heads * queries_per_group, HD)
    grad_krot = jnp.einsum('ghij,ighd->jgd', grad_score.astype(jnp.float32), query_rot.astype(jnp.float32))
    grad_query = inverse_rotate(grad_qrot, rope_cos, rope_sin).astype(jnp.bfloat16).reshape(row_count, -1)
    grad_key = inverse_rotate(grad_krot, rope_cos, rope_sin).astype(jnp.bfloat16).reshape(row_count, -1)
    grad_value = grad_value_f.astype(jnp.bfloat16).reshape(row_count, -1)
    grads = (contract_rows(normed, grad_query), contract_rows(normed, grad_key), contract_rows(normed, grad_value), grad_wo)
    grad_normed = times_trans(grad_query, weight_q) + times_trans(grad_key, weight_k) + times_trans(grad_value, weight_v)
    grad_hat = grad_normed * gain_float
    grad_in = inverse_norm * (grad_hat - unit_rows * lax.optimization_barrier(jnp.mean(grad_hat * unit_rows, axis=1, keepdims=True)))
    return (grad_in, grads)

def reference(roll_rows, dest, lengths, clusters, log_prob_grad, gain, w_q, w_k, w_v, w_o_t):
    slot_of = jnp.zeros((SEQS,), jnp.int32).at[dest].set(jnp.arange(SEQS, dtype=jnp.int32))
    ballots = clusters.reshape(SEQS // GSIZE, GSIZE)
    vote_share = lax.optimization_barrier(jnp.mean((ballots[:, :, None] == ballots[:, None, :]).astype(jnp.float32), axis=2))
    advantage = (vote_share - lax.optimization_barrier(jnp.mean(vote_share, axis=1, keepdims=True))).reshape(SEQS).astype(jnp.bfloat16)
    flat_rows = roll_rows.reshape(SEQS * MAXLEN, D)
    gain_float = gain.astype(jnp.float32)
    q_cols = QW // N_TP
    k_cols = KW // N_TP

    def learner(totals, inputs):
        lengths_row, slots_row, cotangent = inputs
        segment, position, one_hot = packed_layout(lengths_row)
        slot_rows = lax.optimization_barrier(jnp.sum(jnp.where(one_hot, slots_row[None, :], 0), axis=1)).astype(jnp.int32)
        packed = jnp.take(flat_rows, slot_rows * MAXLEN + position, axis=0)
        row_advantage = jnp.take(advantage, slot_rows).astype(jnp.float32)
        inputs_float = packed.astype(jnp.float32)
        inverse_norm = lax.rsqrt(lax.optimization_barrier(jnp.mean(inputs_float * inputs_float, axis=1, keepdims=True)) + NORM_EPSILON)
        unit_rows = inputs_float * inverse_norm
        normed = (unit_rows * gain_float).astype(jnp.bfloat16)
        rope_cos, rope_sin = rotary_tables(position)
        allowed = (segment[:, None] == segment[None, :]) & (position[None, :] <= position[:, None])
        grad_out = row_advantage[:, None] * cotangent.astype(jnp.float32)
        grad_round = grad_out.astype(jnp.bfloat16)
        input_sum = grad_out
        stores = ([], [], [], [])
        for member in range(N_TP):
            q_span = slice(member * q_cols, (member + 1) * q_cols)
            k_span = slice(member * k_cols, (member + 1) * k_cols)
            grad_in, grads = group_pass(normed, unit_rows, inverse_norm, gain_float, grad_round, rope_cos, rope_sin, allowed, w_q[:, q_span], w_k[:, k_span], w_v[:, k_span], w_o_t[:, q_span])
            input_sum = input_sum + wire_round(grad_in)
            for store, term in zip(stores, grads):
                store.append(term)
        learner_terms = tuple((wire_round(jnp.concatenate(store, axis=1)) for store in stores))
        totals = tuple((running + term for running, term in zip(totals, learner_terms)))
        return (totals, input_sum.astype(jnp.bfloat16))
    initial = (jnp.zeros((D, QW), jnp.float32), jnp.zeros((D, KW), jnp.float32), jnp.zeros((D, KW), jnp.float32), jnp.zeros((D, QW), jnp.float32))
    totals, input_rows = lax.scan(learner, initial, (lengths, slot_of.reshape(N_FSDP, SEQ_DEV), log_prob_grad.reshape(N_FSDP, TOK_DEV, D)))
    return (input_rows.reshape(TOKENS, D), totals[0].astype(jnp.bfloat16), totals[1].astype(jnp.bfloat16), totals[2].astype(jnp.bfloat16), totals[3].astype(jnp.bfloat16))
```

```python
import functools

import jax
import jax.numpy as jnp
from jax import lax
from jax.experimental import pallas as pl
from jax.experimental.pallas import tpu as pltpu
from jax.sharding import PartitionSpec as P

KEY_VALUE_HEADS = 4
HD = 128
QUERY_HEADS = 16
GSIZE = 16
ROPE_BASE = 1000000.0
NORM_EPSILON = 1e-06
BLOCK = 128

UP = [(0, 1), (1, 2), (2, 3)]
DOWN = [(1, 0), (2, 1), (3, 2)]
UP_MID = [(1, 2), (2, 3)]
DOWN_MID = [(1, 0), (2, 1)]
TO_ENDS = [(2, 3), (1, 0)]
FROM_ENDS = [(3, 2), (0, 1)]
UP_IN = [(0, 1), (1, 2)]
DOWN_IN = [(3, 2), (2, 1)]


def contract_rows(left, right):
    return lax.dot_general(
        left, right, (((0,), (0,)), ((), ())), preferred_element_type=jnp.float32
    )


def times_trans(left, right):
    return lax.dot_general(
        left, right, (((1,), (1,)), ((), ())), preferred_element_type=jnp.float32
    )


def matmul(left, right):
    return jnp.dot(left, right, preferred_element_type=jnp.float32)


def line_gather(own, z):
    up1 = lax.ppermute(own, "tp", UP)
    down1 = lax.ppermute(own, "tp", DOWN)
    up2 = lax.ppermute(up1, "tp", UP_MID)
    down2 = lax.ppermute(down1, "tp", DOWN_MID)
    far2 = jnp.where(z >= 2, up2, down2)
    far3 = lax.ppermute(far2, "tp", TO_ENDS)
    near = jnp.where(z % 2 == 1, up1, down1)
    other = jnp.where(z == 1, down1, jnp.where(z == 2, up1, far3))
    return [own, near, far2, other]


def line_scatter(parts, z):
    own, near, far2, other = parts
    f32 = jnp.float32
    from_end = lax.ppermute(other, "tp", FROM_ENDS)
    total2 = (far2.astype(f32) + from_end.astype(f32)).astype(jnp.bfloat16)
    up2 = lax.ppermute(total2, "tp", UP_IN)
    down2 = lax.ppermute(total2, "tp", DOWN_IN)
    go_up = jnp.where(z == 1, other, near).astype(f32) + up2.astype(f32)
    go_down = jnp.where(z == 2, other, near).astype(f32) + down2.astype(f32)
    up3 = lax.ppermute(go_up.astype(jnp.bfloat16), "tp", UP)
    down3 = lax.ppermute(go_down.astype(jnp.bfloat16), "tp", DOWN)
    return own.astype(f32) + up3.astype(f32) + down3.astype(f32)


def attention_kernel(
    raw_ref, inv_ref, ga_ref, adv_ref, cos_ref, sin_ref, start_ref,
    dqkv_ref, dscaled_ref, out_ref, mean_ref,
    qkv_b, dk_acc, dv_acc,
):
    rows = raw_ref.shape[0]
    heads = ga_ref.shape[1] // HD
    qw = heads * HD
    scale = HD ** (-0.5)
    bf16 = jnp.bfloat16
    zeros = jnp.zeros((BLOCK, HD), jnp.float32)
    qkv_b[pl.ds(0, BLOCK), :] = jnp.zeros((BLOCK, qkv_b.shape[1]), bf16)
    dk_acc[pl.ds(0, BLOCK), :] = zeros
    dv_acc[pl.ds(0, BLOCK), :] = zeros

    def turn(value, cos, sin):
        return value * cos + pltpu.roll(value, HD // 2, 1) * sin

    def step(block, carry):
        base = pl.multiple_of(block * BLOCK, BLOCK)
        here = pl.ds(base, BLOCK)
        after = pl.ds(base + BLOCK, BLOCK)
        both = pl.ds(base, 2 * BLOCK)
        cos, sin = cos_ref[here, :], sin_ref[here, :]
        inv = inv_ref[here, :]
        for h in range(heads + 1):
            cols = slice(h * HD, (h + 1) * HD)
            qkv_b[after, cols] = turn(raw_ref[here, cols] * inv, cos, sin).astype(bf16)
        cols = slice(qw + HD, qw + 2 * HD)
        qkv_b[after, cols] = (raw_ref[here, cols] * inv).astype(bf16)
        dk_acc[after, :] = zeros
        dv_acc[after, :] = zeros
        adv = adv_ref[here, :]
        qs = jnp.concatenate(
            [qkv_b[after, h * HD : (h + 1) * HD] for h in range(heads)], axis=0
        )
        gs = jnp.concatenate(
            [(ga_ref[here, h * HD : (h + 1) * HD] * adv).astype(bf16) for h in range(heads)], axis=0
        )
        ks = qkv_b[both, qw : qw + HD]
        vs = qkv_b[both, qw + HD : qw + 2 * HD]
        start = start_ref[here, :] - (base - BLOCK)
        col = lax.broadcasted_iota(jnp.int32, (BLOCK, 2 * BLOCK), 1)
        row = lax.broadcasted_iota(jnp.int32, (BLOCK, 2 * BLOCK), 0) + BLOCK
        allowed = (col >= start) & (col <= row)
        bias = jnp.where(allowed, 0.0, -1e30)
        bias = jnp.concatenate([bias] * heads, axis=0)
        scores = times_trans(qs, ks) * scale + bias
        top = jnp.max(scores, axis=-1, keepdims=True)
        weight = jnp.exp(scores - top)
        prob = weight / jnp.sum(weight, axis=-1, keepdims=True)
        prob_b = prob.astype(bf16)
        out = matmul(prob_b, vs)
        grad_prob = times_trans(gs, vs)
        delta = jnp.sum(prob * grad_prob, axis=-1, keepdims=True)
        ds = (prob * (grad_prob - delta) * scale).astype(bf16)
        dq = matmul(ds, ks)
        dk_acc[both, :] += contract_rows(ds, qs)
        dv_acc[both, :] += contract_rows(prob_b, gs)
        partial = jnp.zeros((BLOCK, 1), jnp.float32)
        for h in range(heads):
            cols = slice(h * HD, (h + 1) * HD)
            part = slice(h * BLOCK, (h + 1) * BLOCK)
            out_ref[here, cols] = (out[part, :].astype(bf16).astype(jnp.float32) * adv).astype(bf16)
            grad = turn(dq[part, :], cos, -sin).astype(bf16)
            dqkv_ref[here, cols] = grad
            grad = grad.astype(jnp.float32) * inv
            dscaled_ref[here, cols] = grad.astype(bf16)
            partial += jnp.sum(grad * raw_ref[here, cols], axis=-1, keepdims=True)
        mean_ref[here, :] = partial
        return carry

    lax.fori_loop(0, rows // BLOCK, step, 0)

    def finish(block, carry):
        base = pl.multiple_of(block * BLOCK, BLOCK)
        here = pl.ds(base, BLOCK)
        after = pl.ds(base + BLOCK, BLOCK)
        cos, sin = cos_ref[here, :], sin_ref[here, :]
        inv = inv_ref[here, :]
        total = mean_ref[here, :]
        for place, grad in (
            (qw, turn(dk_acc[after, :], cos, -sin)),
            (qw + HD, dv_acc[after, :]),
        ):
            cols = slice(place, place + HD)
            grad = grad.astype(bf16)
            dqkv_ref[here, cols] = grad
            grad = grad.astype(jnp.float32) * inv
            dscaled_ref[here, cols] = grad.astype(bf16)
            total += jnp.sum(grad * raw_ref[here, cols], axis=-1, keepdims=True)
        mean_ref[here, :] = total
        return carry

    lax.fori_loop(0, rows // BLOCK, finish, 0)


def attention(raw, inv, ga, adv, cos, sin, start):
    rows, width = raw.shape
    qw = ga.shape[1]
    vmem = pl.BlockSpec(memory_space=pltpu.VMEM)
    return pl.pallas_call(
        attention_kernel,
        out_shape=(
            jax.ShapeDtypeStruct((rows, width), jnp.bfloat16),
            jax.ShapeDtypeStruct((rows, width), jnp.bfloat16),
            jax.ShapeDtypeStruct((rows, qw), jnp.bfloat16),
            jax.ShapeDtypeStruct((rows, 1), jnp.float32),
        ),
        in_specs=[vmem] * 7,
        out_specs=[vmem] * 4,
        scratch_shapes=[
            pltpu.VMEM((rows + BLOCK, width), jnp.bfloat16),
            pltpu.VMEM((rows + BLOCK, HD), jnp.float32),
            pltpu.VMEM((rows + BLOCK, HD), jnp.float32),
        ],
        compiler_params=pltpu.CompilerParams(vmem_limit_bytes=40 * 1024 * 1024),
        cost_estimate=pl.CostEstimate(
            flops=rows * 2 * BLOCK * HD * 12 * (qw // HD),
            bytes_accessed=rows * width * 8 + rows * qw * 6,
            transcendentals=rows * 2 * BLOCK * (qw // HD),
        ),
        name="attention",
    )(raw, inv, ga, adv, cos, sin, start)


def per_device(roll_rows, dest, lengths, clusters, log_prob_grad, gain, w_q, w_k, w_v, w_o_t):
    sequence_count = dest.shape[0]
    max_len, local_features = roll_rows.shape[1:]
    row_count = log_prob_grad.shape[0]
    replicas = lax.axis_size("fsdp")
    per_pair = sequence_count // replicas
    me = lax.axis_index("fsdp")
    z = lax.axis_index("tp")
    f32, bf16 = jnp.float32, jnp.bfloat16
    q_cols, k_cols = w_q.shape[1], w_k.shape[1]
    qkv_cols = q_cols + 2 * k_cols
    feature_count = gain.shape[0]

    g_parts = line_gather(log_prob_grad, z)

    slot_ids = jnp.arange(sequence_count, dtype=jnp.int32)
    earlier_dest = dest[None, :] < dest[:, None]
    send_block = jnp.sum(earlier_dest.astype(jnp.int32), axis=1)
    source = jnp.sum(
        jnp.where(send_block[None, :] == slot_ids[:, None], slot_ids[None, :], 0), axis=1
    )
    send_rows = jnp.take(roll_rows, source, axis=0, mode="clip")
    arrived_rows = lax.all_to_all(send_rows, "fsdp", split_axis=0, concat_axis=0, tiled=True)

    meta = lax.all_gather(jnp.stack([dest, clusters]), "fsdp", axis=1, tiled=True)
    all_dest, all_clusters = meta[0], meta[1]
    ballots = all_clusters.reshape(-1, GSIZE)
    vote_share = jnp.mean((ballots[:, :, None] == ballots[:, None, :]).astype(f32), axis=2)
    advantage = (
        (vote_share - jnp.mean(vote_share, axis=1, keepdims=True)).reshape(-1).astype(bf16)
    ).astype(f32)
    mine = (all_dest // sequence_count) == me
    within = all_dest % sequence_count
    of_replica = within.reshape(replicas, sequence_count)
    mine_of = mine.reshape(replicas, sequence_count)
    rank = jnp.sum(
        (mine_of[:, None, :] & (of_replica[:, None, :] < of_replica[:, :, None])).astype(jnp.int32),
        axis=2,
    )
    arrival = (jnp.arange(replicas, dtype=jnp.int32)[:, None] * per_pair + rank).reshape(-1)
    holder = mine[None, :] & (within[None, :] == slot_ids[:, None])
    slot_of = jnp.sum(jnp.where(holder, arrival[None, :], 0), axis=1)
    seq_advantage = jnp.sum(jnp.where(holder, advantage[None, :], 0.0), axis=1)

    lengths_row = lengths.reshape(sequence_count)
    sequence_ends = jnp.cumsum(lengths_row)
    sequence_starts = sequence_ends - lengths_row
    row_index = jnp.arange(row_count, dtype=jnp.int32)
    one_hot = (sequence_ends[None, :] > row_index[:, None]) & (
        sequence_starts[None, :] <= row_index[:, None]
    )
    row_start = jnp.sum(jnp.where(one_hot, sequence_starts[None, :], 0), axis=1)
    position = row_index - row_start
    row_slot = jnp.sum(jnp.where(one_hot, slot_of[None, :], 0), axis=1)
    adv = jnp.sum(jnp.where(one_hot, seq_advantage[None, :], 0.0), axis=1)[:, None]
    half_width = HD // 2
    frequency = ROPE_BASE ** (-(2.0 * jnp.arange(half_width, dtype=f32)) / HD)
    angles = position.astype(f32)[:, None] * frequency[None, :]
    cos, sin = jnp.cos(angles), jnp.sin(angles)
    cos = jnp.concatenate([cos, cos], axis=1)
    sin = jnp.concatenate([-sin, sin], axis=1)

    weights = lax.all_gather(
        jnp.concatenate([w_q, w_k, w_v, w_o_t], axis=1), "fsdp", axis=0, tiled=True
    ).reshape(4, local_features, -1)

    x_own = jnp.take(
        arrived_rows.reshape(sequence_count * max_len, local_features),
        row_slot * max_len + position,
        axis=0,
        mode="clip",
    )
    x_parts = line_gather(x_own, z)

    gain_parts = gain.astype(f32).reshape(4, local_features)
    w_parts = [lax.dynamic_index_in_dim(weights, z ^ k, 0, keepdims=False) for k in range(4)]
    gain_k = [lax.dynamic_index_in_dim(gain_parts, z ^ k, 0, keepdims=False) for k in range(4)]

    ga = sum(matmul(g_parts[k], w_parts[k][:, qkv_cols:]) for k in range(4))
    raw = sum(
        matmul((x_parts[k].astype(f32) * gain_k[k][None, :]).astype(bf16), w_parts[k][:, :qkv_cols])
        for k in range(4)
    )
    squares = sum(
        jnp.sum(jnp.square(x_parts[k].astype(f32)), axis=1, keepdims=True) for k in range(4)
    )
    inv = lax.rsqrt(squares / feature_count + NORM_EPSILON)

    dqkv, dscaled, out_scaled, row_sum = attention(
        raw, inv, ga, adv, cos, sin, row_start[:, None]
    )

    pull = inv * inv * row_sum / feature_count
    dx_parts = [
        (
            inv * (times_trans(dqkv, w_parts[k][:, :qkv_cols]) * gain_k[k][None, :])
            - x_parts[k].astype(f32) * pull
        ).astype(bf16)
        for k in range(4)
    ]
    dx = line_scatter(dx_parts, z)
    input_grad = (adv * log_prob_grad.astype(f32) + dx).astype(bf16)

    terms = jnp.zeros((4, local_features, qkv_cols + q_cols), bf16)
    for k in range(4):
        term = jnp.concatenate(
            [
                contract_rows(x_parts[k], dscaled) * gain_k[k][:, None],
                contract_rows(g_parts[k], out_scaled),
            ],
            axis=1,
        ).astype(bf16)
        terms = lax.dynamic_update_index_in_dim(terms, term, z ^ k, 0)
    summed = lax.psum_scatter(
        terms.reshape(feature_count, qkv_cols + q_cols), "fsdp", scatter_dimension=0, tiled=True
    )
    grad_q = summed[:, :q_cols]
    grad_k = summed[:, q_cols : q_cols + k_cols]
    grad_v = summed[:, q_cols + k_cols : qkv_cols]
    grad_o_t = summed[:, qkv_cols:]
    return (input_grad, grad_q, grad_k, grad_v, grad_o_t)


def solution(mesh):
    in_specs = (
        P("fsdp", None, "tp"),
        P("fsdp"),
        P("fsdp", None),
        P("fsdp"),
        P("fsdp", "tp"),
        P(),
        P("fsdp", "tp"),
        P("fsdp", "tp"),
        P("fsdp", "tp"),
        P("fsdp", "tp"),
    )
    out_specs = (
        P("fsdp", "tp"),
        P("fsdp", "tp"),
        P("fsdp", "tp"),
        P("fsdp", "tp"),
        P("fsdp", "tp"),
    )
    return jax.shard_map(
        per_device, mesh=mesh, in_specs=in_specs, out_specs=out_specs, check_vma=False
    )
```

```python
import functools

import jax
import jax.numpy as jnp
from jax import lax
from jax.experimental import pallas as pl
from jax.experimental.pallas import tpu as pltpu
from jax.sharding import PartitionSpec as P

KEY_VALUE_HEADS = 4
HD = 128
QUERY_HEADS = 16
GSIZE = 16
ROPE_BASE = 1000000.0
NORM_EPSILON = 1e-06
BLOCK = 128

UP = [(0, 1), (1, 2), (2, 3)]
DOWN = [(1, 0), (2, 1), (3, 2)]
UP_MID = [(1, 2), (2, 3)]
DOWN_MID = [(1, 0), (2, 1)]
TO_ENDS = [(2, 3), (1, 0)]
FROM_ENDS = [(3, 2), (0, 1)]
UP_IN = [(0, 1), (1, 2)]
DOWN_IN = [(3, 2), (2, 1)]


def contract_rows(left, right):
    return lax.dot_general(
        left, right, (((0,), (0,)), ((), ())), preferred_element_type=jnp.float32
    )


def times_trans(left, right):
    return lax.dot_general(
        left, right, (((1,), (1,)), ((), ())), preferred_element_type=jnp.float32
    )


def matmul(left, right):
    return jnp.dot(left, right, preferred_element_type=jnp.float32)


def line_gather(own, z):
    up1 = lax.ppermute(own, "tp", UP)
    down1 = lax.ppermute(own, "tp", DOWN)
    up2 = lax.ppermute(up1, "tp", UP_MID)
    down2 = lax.ppermute(down1, "tp", DOWN_MID)
    far2 = jnp.where(z >= 2, up2, down2)
    far3 = lax.ppermute(far2, "tp", TO_ENDS)
    near = jnp.where(z % 2 == 1, up1, down1)
    other = jnp.where(z == 1, down1, jnp.where(z == 2, up1, far3))
    return [own, near, far2, other]


def line_scatter(parts, z):
    own, near, far2, other = parts
    f32 = jnp.float32
    from_end = lax.ppermute(other, "tp", FROM_ENDS)
    total2 = (far2.astype(f32) + from_end.astype(f32)).astype(jnp.bfloat16)
    up2 = lax.ppermute(total2, "tp", UP_IN)
    down2 = lax.ppermute(total2, "tp", DOWN_IN)
    go_up = jnp.where(z == 1, other, near).astype(f32) + up2.astype(f32)
    go_down = jnp.where(z == 2, other, near).astype(f32) + down2.astype(f32)
    up3 = lax.ppermute(go_up.astype(jnp.bfloat16), "tp", UP)
    down3 = lax.ppermute(go_down.astype(jnp.bfloat16), "tp", DOWN)
    return own.astype(f32) + up3.astype(f32) + down3.astype(f32)


def attention_kernel(has_prev, is_last, first, *refs):
    refs = list(refs)
    raw_ref, inv_ref, ga_ref, adv_ref, cos_ref, sin_ref, start_ref = refs[:7]
    refs = refs[7:]
    if has_prev:
        raw_prev, inv_prev, dq_prev, dk_prev, dv_prev = refs[:5]
        refs = refs[5:]
    dqkv_ref, dscaled_ref, mean_ref, out_ref = refs[:4]
    refs = refs[4:]
    if not is_last:
        dq_next, dk_next, dv_next = refs[:3]
        refs = refs[3:]
    qkv_b, dq_b, dk_acc, dv_acc = refs
    rows = raw_ref.shape[0]
    heads = ga_ref.shape[1] // HD
    qw = heads * HD
    scale = HD ** (-0.5)
    f32, bf16 = jnp.float32, jnp.bfloat16
    blocks = rows // BLOCK

    def span(block):
        return slice(block * BLOCK, (block + 1) * BLOCK)

    def turn(value, cos, sin):
        return value * cos + pltpu.roll(value, HD // 2, 1) * sin

    def whole(block):
        return slice(first + block * BLOCK, first + (block + 1) * BLOCK)

    def linear(block, cols):
        if block < 0:
            last = raw_prev.shape[0]
            return raw_prev[last - BLOCK : last, cols] * inv_prev[last - BLOCK : last, :]
        return raw_ref[span(block), cols] * inv_ref[span(block), :]

    def prepare(block, from_head):
        cos, sin = cos_ref[whole(block), :], sin_ref[whole(block), :]
        for h in range(from_head, heads + 1):
            cols = slice(h * HD, (h + 1) * HD)
            qkv_b[span(block + 1), cols] = turn(linear(block, cols), cos, sin).astype(bf16)
        cols = slice(qw + HD, qw + 2 * HD)
        qkv_b[span(block + 1), cols] = linear(block, cols).astype(bf16)

    if has_prev:
        prepare(-1, heads)
        dq_b[span(0), :] = dq_prev[...]
        dk_acc[span(0), :] = dk_prev[...]
        dv_acc[span(0), :] = dv_prev[...]
    else:
        qkv_b[span(0), :] = jnp.zeros((BLOCK, qkv_b.shape[1]), bf16)
        dk_acc[span(0), :] = jnp.zeros((BLOCK, HD), f32)
        dv_acc[span(0), :] = jnp.zeros((BLOCK, HD), f32)

    for block in range(blocks):
        prepare(block, 0)
        adv = adv_ref[whole(block), :]
        here, after = span(block), span(block + 1)
        both = slice(block * BLOCK, (block + 2) * BLOCK)
        qs = jnp.concatenate(
            [qkv_b[after, h * HD : (h + 1) * HD] for h in range(heads)], axis=0
        )
        gs = jnp.concatenate(
            [(ga_ref[here, h * HD : (h + 1) * HD] * adv).astype(bf16) for h in range(heads)], axis=0
        )
        ks = qkv_b[both, qw : qw + HD]
        vs = qkv_b[both, qw + HD : qw + 2 * HD]
        start = start_ref[whole(block), :] - (first + (block - 1) * BLOCK)
        col = lax.broadcasted_iota(jnp.int32, (BLOCK, 2 * BLOCK), 1)
        row = lax.broadcasted_iota(jnp.int32, (BLOCK, 2 * BLOCK), 0) + BLOCK
        bias = jnp.where((col >= start) & (col <= row), 0.0, -1e30)
        bias = jnp.concatenate([bias] * heads, axis=0)
        scores = times_trans(qs, ks) * scale + bias
        top = jnp.max(scores, axis=-1, keepdims=True)
        weight = jnp.exp(scores - top)
        prob = weight / jnp.sum(weight, axis=-1, keepdims=True)
        prob_b = prob.astype(bf16)
        out = matmul(prob_b, vs)
        grad_prob = times_trans(gs, vs)
        delta = jnp.sum(prob * grad_prob, axis=-1, keepdims=True)
        ds = (prob * (grad_prob - delta) * scale).astype(bf16)
        dq = matmul(ds, ks)
        dk_acc[span(block), :] += contract_rows(ds[:, :BLOCK], qs)
        dk_acc[after, :] = contract_rows(ds[:, BLOCK:], qs)
        dv_acc[span(block), :] += contract_rows(prob_b[:, :BLOCK], gs)
        dv_acc[after, :] = contract_rows(prob_b[:, BLOCK:], gs)
        cos, sin = cos_ref[whole(block), :], sin_ref[whole(block), :]
        for h in range(heads):
            cols = slice(h * HD, (h + 1) * HD)
            out_ref[here, cols] = (out[span(h), :].astype(bf16).astype(f32) * adv).astype(bf16)
            dq_b[after, cols] = turn(dq[span(h), :], cos, -sin).astype(bf16)

    begin = -1 if has_prev else 0
    end = blocks if is_last else blocks - 1
    for block in range(begin, end):
        to = span(block - begin)
        cos, sin = cos_ref[whole(block), :], sin_ref[whole(block), :]
        inv = inv_prev[inv_prev.shape[0] - BLOCK :, :] if block < 0 else inv_ref[span(block), :]
        total = jnp.zeros((BLOCK, 1), f32)
        for h in range(heads + 2):
            cols = slice(h * HD, (h + 1) * HD)
            if h < heads:
                grad = dq_b[span(block + 1), cols]
            elif h == heads:
                grad = turn(dk_acc[span(block + 1), :], cos, -sin).astype(bf16)
            else:
                grad = dv_acc[span(block + 1), :].astype(bf16)
            dqkv_ref[to, cols] = grad
            grad = grad.astype(f32)
            dscaled_ref[to, cols] = (grad * inv).astype(bf16)
            total += jnp.sum(grad * linear(block, cols), axis=-1, keepdims=True)
        mean_ref[to, :] = total
    if not is_last:
        dq_next[...] = dq_b[span(blocks), :]
        dk_next[...] = dk_acc[span(blocks), :]
        dv_next[...] = dv_acc[span(blocks), :]


def attention(first, total, raw, inv, ga, adv, cos, sin, start, prev):
    rows, width = raw.shape
    qw = ga.shape[1]
    is_last = first + rows == total
    final = rows + (BLOCK if prev else 0) - (0 if is_last else BLOCK)
    f32, bf16 = jnp.float32, jnp.bfloat16
    out_shape = [
        jax.ShapeDtypeStruct((final, width), bf16),
        jax.ShapeDtypeStruct((final, width), bf16),
        jax.ShapeDtypeStruct((final, 1), f32),
        jax.ShapeDtypeStruct((rows, qw), bf16),
    ]
    if not is_last:
        out_shape += [
            jax.ShapeDtypeStruct((BLOCK, qw), bf16),
            jax.ShapeDtypeStruct((BLOCK, HD), f32),
            jax.ShapeDtypeStruct((BLOCK, HD), f32),
        ]
    operands = [raw, inv, ga, adv, cos, sin, start] + list(prev)
    vmem = pl.BlockSpec(memory_space=pltpu.VMEM)
    return pl.pallas_call(
        functools.partial(attention_kernel, bool(prev), is_last, first),
        out_shape=out_shape,
        in_specs=[vmem] * len(operands),
        out_specs=[vmem] * len(out_shape),
        scratch_shapes=[
            pltpu.VMEM((rows + BLOCK, width), bf16),
            pltpu.VMEM((rows + BLOCK, qw), bf16),
            pltpu.VMEM((rows + BLOCK, HD), f32),
            pltpu.VMEM((rows + BLOCK, HD), f32),
        ],
        compiler_params=pltpu.CompilerParams(vmem_limit_bytes=32 * 1024 * 1024),
        cost_estimate=pl.CostEstimate(
            flops=rows * 2 * BLOCK * HD * 12 * (qw // HD),
            bytes_accessed=rows * width * 8 + rows * qw * 6,
            transcendentals=rows * 2 * BLOCK * (qw // HD),
        ),
        name="attention",
    )(*operands)


def weight_grad_kernel(per_row, place_ref, *refs):
    chunks = 2
    x_refs, g_refs = refs[: 4 * chunks], refs[4 * chunks : 8 * chunks]
    ds_ref, os_ref, gain_ref, keep_ref, send_ref, term = refs[8 * chunks :]
    width = ds_ref.shape[1]
    features = x_refs[0].shape[1]
    step = pl.program_id(0)

    def product(left, k, right):
        total = None
        base = 0
        for c in range(chunks):
            ref = left[k * chunks + c]
            part = contract_rows(ref[...], right[base : base + ref.shape[0], :])
            base += ref.shape[0]
            total = part if total is None else total + part
        return total

    for k in range(4):

        @pl.when(step == k)
        def _():
            term[:, :width] = (product(x_refs, k, ds_ref) * gain_ref[0]).astype(jnp.bfloat16)
            term[:, width:] = product(g_refs, k, os_ref).astype(jnp.bfloat16)

    core = place_ref[4]
    for group in range(features // (2 * per_row)):
        rows = slice(group * per_row, (group + 1) * per_row)
        base = 2 * group * per_row
        keep = pl.multiple_of(base + core * per_row, 16)
        send = pl.multiple_of(base + (1 - core) * per_row, 16)
        keep_ref[rows, :] = term[pl.ds(keep, per_row), :]
        send_ref[rows, :] = term[pl.ds(send, per_row), :]


def weight_grads(places, x_chunks, g_chunks, dscaled, out_scaled, gain, per_row):
    features = gain.shape[1]
    width = dscaled.shape[1] + out_scaled.shape[1]
    operands = [c for k in range(4) for c in (x_chunks[0][k], x_chunks[1][k])]
    operands += [c for k in range(4) for c in (g_chunks[0][k], g_chunks[1][k])]
    operands += [dscaled, out_scaled]
    once = [
        pl.BlockSpec(o.shape, lambda k, place: (0, 0), pipeline_mode=pl.Buffered(1))
        for o in operands
    ]
    out = jax.ShapeDtypeStruct((2 * features, width), jnp.bfloat16)
    return pl.pallas_call(
        functools.partial(weight_grad_kernel, per_row),
        out_shape=[out, out],
        grid_spec=pltpu.PrefetchScalarGridSpec(
            num_scalar_prefetch=1,
            grid=(4,),
            in_specs=once
            + [pl.BlockSpec((1, features, 1), lambda k, place: (place[k], 0, 0))],
            out_specs=[pl.BlockSpec((features // 2, width), lambda k, place: (place[k], 0))] * 2,
            scratch_shapes=[pltpu.VMEM((features, width), jnp.bfloat16)],
        ),
        compiler_params=pltpu.CompilerParams(vmem_limit_bytes=48 * 1024 * 1024),
        cost_estimate=pl.CostEstimate(
            flops=2 * dscaled.shape[0] * 4 * features * width,
            bytes_accessed=4 * features * (4 * dscaled.shape[0] + 2 * width),
            transcendentals=0,
        ),
        name="weight_grads",
    )(places, *operands, gain[:, :, None])


def per_device(roll_rows, dest, lengths, clusters, log_prob_grad, gain, w_q, w_k, w_v, w_o_t):
    sequence_count = dest.shape[0]
    max_len, local_features = roll_rows.shape[1:]
    row_count = log_prob_grad.shape[0]
    replicas = lax.axis_size("fsdp")
    per_pair = sequence_count // replicas
    me = lax.axis_index("fsdp")
    z = lax.axis_index("tp")
    f32, bf16 = jnp.float32, jnp.bfloat16
    q_cols, k_cols = w_q.shape[1], w_k.shape[1]
    qkv_cols = q_cols + 2 * k_cols
    feature_count = gain.shape[0]

    chunks = [slice(0, row_count - 2 * BLOCK), slice(row_count - 2 * BLOCK, row_count)]

    g_chunks = [line_gather(log_prob_grad[c, :], z) for c in chunks]

    slot_ids = jnp.arange(sequence_count, dtype=jnp.int32)
    earlier_dest = dest[None, :] < dest[:, None]
    send_block = jnp.sum(earlier_dest.astype(jnp.int32), axis=1)
    source = jnp.sum(
        jnp.where(send_block[None, :] == slot_ids[:, None], slot_ids[None, :], 0), axis=1
    )
    send_rows = jnp.take(roll_rows, source, axis=0, mode="clip")
    arrived_rows = lax.all_to_all(send_rows, "fsdp", split_axis=0, concat_axis=0, tiled=True)

    ballots = clusters.reshape(sequence_count // GSIZE, GSIZE)
    vote_share = jnp.mean((ballots[:, :, None] == ballots[:, None, :]).astype(f32), axis=2)
    advantage = (vote_share - jnp.mean(vote_share, axis=1, keepdims=True)).reshape(sequence_count)
    tags = jnp.stack([(dest % sequence_count).astype(f32), advantage], axis=1)
    picked = send_block[None, :] == slot_ids[:, None]
    tags = jnp.sum(jnp.where(picked[:, :, None], tags[None, :, :], 0.0), axis=1).astype(bf16)
    tags = lax.all_to_all(tags, "fsdp", split_axis=0, concat_axis=0, tiled=True).astype(f32)
    holder = tags[None, :, 0].astype(jnp.int32) == slot_ids[:, None]
    slot_of = jnp.sum(jnp.where(holder, slot_ids[None, :], 0), axis=1)
    seq_advantage = jnp.sum(jnp.where(holder, tags[None, :, 1], 0.0), axis=1)

    lengths_row = lengths.reshape(sequence_count)
    sequence_ends = jnp.cumsum(lengths_row)
    sequence_starts = sequence_ends - lengths_row
    row_index = jnp.arange(row_count, dtype=jnp.int32)
    one_hot = (sequence_ends[None, :] > row_index[:, None]) & (
        sequence_starts[None, :] <= row_index[:, None]
    )
    row_start = jnp.sum(jnp.where(one_hot, sequence_starts[None, :], 0), axis=1)
    position = row_index - row_start
    row_slot = jnp.sum(jnp.where(one_hot, slot_of[None, :], 0), axis=1)
    adv = jnp.sum(jnp.where(one_hot, seq_advantage[None, :], 0.0), axis=1)[:, None]
    half_width = HD // 2
    frequency = ROPE_BASE ** (-(2.0 * jnp.arange(half_width, dtype=f32)) / HD)
    angles = position.astype(f32)[:, None] * frequency[None, :]
    cos, sin = jnp.cos(angles), jnp.sin(angles)
    cos = jnp.concatenate([cos, cos], axis=1)
    sin = jnp.concatenate([-sin, sin], axis=1)

    weights = lax.all_gather(
        jnp.concatenate([w_q, w_k, w_v, w_o_t], axis=1), "fsdp", axis=0, tiled=True
    ).reshape(4, local_features, -1)

    flat_rows = arrived_rows.reshape(sequence_count * max_len, local_features)
    row_source = row_slot * max_len + position
    x_chunks = [
        line_gather(jnp.take(flat_rows, row_source[c], axis=0, mode="clip"), z) for c in chunks
    ]

    gain_parts = gain.astype(f32).reshape(4, local_features)
    w_parts = [lax.dynamic_index_in_dim(weights, z ^ k, 0, keepdims=False) for k in range(4)]
    gain_k = [lax.dynamic_index_in_dim(gain_parts, z ^ k, 0, keepdims=False) for k in range(4)]

    def project(x_parts, g_parts):
        ga = sum(matmul(g_parts[k], w_parts[k][:, qkv_cols:]) for k in range(4))
        raw = sum(
            matmul(
                (x_parts[k].astype(f32) * gain_k[k][None, :]).astype(bf16),
                w_parts[k][:, :qkv_cols],
            )
            for k in range(4)
        )
        squares = sum(
            jnp.sum(jnp.square(x_parts[k].astype(f32)), axis=1, keepdims=True) for k in range(4)
        )
        return raw, lax.rsqrt(squares / feature_count + NORM_EPSILON), ga

    def input_terms(dqkv, row_sum, inv, x_parts):
        pull = inv * row_sum / feature_count
        return line_scatter(
            [
                (
                    inv * (times_trans(dqkv, w_parts[k][:, :qkv_cols]) * gain_k[k][None, :])
                    - x_parts[k].astype(f32) * (inv * pull)
                ).astype(bf16)
                for k in range(4)
            ],
            z,
        )

    start = row_start[:, None]
    raw1, inv1, ga1 = project(x_chunks[0], g_chunks[0])
    first = chunks[1].start
    dqkv1, dscaled1, sum1, out1, dq1, dk1, dv1 = attention(
        0, row_count, raw1, inv1, ga1, adv, cos, sin, start, ()
    )
    final = dqkv1.shape[0]
    dx1 = input_terms(dqkv1, sum1, inv1[:final], [x[:final] for x in x_chunks[0]])

    raw2, inv2, ga2 = project(x_chunks[1], g_chunks[1])
    dqkv2, dscaled2, sum2, out2 = attention(
        first, row_count, raw2, inv2, ga2, adv, cos, sin, start, (raw1, inv1, dq1, dk1, dv1)
    )
    dx2 = input_terms(
        dqkv2,
        sum2,
        jnp.concatenate([inv1[final:], inv2], axis=0),
        [jnp.concatenate([x[final:], y], axis=0) for x, y in zip(*x_chunks)],
    )
    dx = jnp.concatenate([dx1, dx2], axis=0)
    input_grad = (adv * log_prob_grad.astype(f32) + dx).astype(bf16)

    core = me % 2
    places = jnp.stack([z ^ k for k in range(4)] + [core]).astype(jnp.int32)
    keep, send = weight_grads(
        places,
        x_chunks,
        g_chunks,
        jnp.concatenate([dscaled1, dscaled2], axis=0),
        jnp.concatenate([out1, out2], axis=0),
        gain_parts,
        feature_count // replicas,
    )
    other = lax.ppermute(send, "fsdp", [(i, i ^ 1) for i in range(replicas)])
    pair = (keep.astype(f32) + other.astype(f32)).astype(bf16)
    summed = lax.psum_scatter(
        pair,
        "fsdp",
        scatter_dimension=0,
        axis_index_groups=[list(range(c, replicas, 2)) for c in range(2)],
        tiled=True,
    )
    grad_q = summed[:, :q_cols]
    grad_k = summed[:, q_cols : q_cols + k_cols]
    grad_v = summed[:, q_cols + k_cols : qkv_cols]
    grad_o_t = summed[:, qkv_cols:]
    return (input_grad, grad_q, grad_k, grad_v, grad_o_t)


def solution(mesh):
    in_specs = (
        P("fsdp", None, "tp"),
        P("fsdp"),
        P("fsdp", None),
        P("fsdp"),
        P("fsdp", "tp"),
        P(),
        P("fsdp", "tp"),
        P("fsdp", "tp"),
        P("fsdp", "tp"),
        P("fsdp", "tp"),
    )
    out_specs = (
        P("fsdp", "tp"),
        P("fsdp", "tp"),
        P("fsdp", "tp"),
        P("fsdp", "tp"),
        P("fsdp", "tp"),
    )
    return jax.shard_map(
        per_device, mesh=mesh, in_specs=in_specs, out_specs=out_specs, check_vma=False
    )
```

```python
import functools

import jax
import jax.numpy as jnp
from jax import lax
from jax.experimental import pallas as pl
from jax.experimental.pallas import tpu as pltpu
from jax.sharding import PartitionSpec as P

KEY_VALUE_HEADS = 4
HD = 128
QUERY_HEADS = 16
GSIZE = 16
ROPE_BASE = 1000000.0
NORM_EPSILON = 1e-06
BLOCK = 128

UP = [(0, 1), (1, 2), (2, 3)]
DOWN = [(1, 0), (2, 1), (3, 2)]
UP_MID = [(1, 2), (2, 3)]
DOWN_MID = [(1, 0), (2, 1)]
TO_ENDS = [(2, 3), (1, 0)]
FROM_ENDS = [(3, 2), (0, 1)]
UP_IN = [(0, 1), (1, 2)]
DOWN_IN = [(3, 2), (2, 1)]


def contract_rows(left, right):
    return lax.dot_general(
        left, right, (((0,), (0,)), ((), ())), preferred_element_type=jnp.float32
    )


def times_trans(left, right):
    return lax.dot_general(
        left, right, (((1,), (1,)), ((), ())), preferred_element_type=jnp.float32
    )


def matmul(left, right):
    return jnp.dot(left, right, preferred_element_type=jnp.float32)


def gather_near(own):
    return lax.ppermute(own, "tp", UP), lax.ppermute(own, "tp", DOWN)


def gather_far(step1, z):
    up2 = lax.ppermute(step1[0], "tp", UP_MID)
    down2 = lax.ppermute(step1[1], "tp", DOWN_MID)
    return jnp.where(z >= 2, up2, down2)


def gather_end(far2):
    return lax.ppermute(far2, "tp", TO_ENDS)


def shards(own, step1, far2, far3, z):
    up1, down1 = step1
    near = jnp.where(z % 2 == 1, up1, down1)
    other = jnp.where(z == 1, down1, jnp.where(z == 2, up1, far3))
    return [own, near, far2, other]


def after(value, *earlier):
    return lax.optimization_barrier((value, *earlier))[0]


def scatter_end(parts):
    return lax.ppermute(parts[3], "tp", FROM_ENDS)


def scatter_far(parts, from_end):
    total2 = (parts[2].astype(jnp.float32) + from_end.astype(jnp.float32)).astype(jnp.bfloat16)
    return lax.ppermute(total2, "tp", UP_IN), lax.ppermute(total2, "tp", DOWN_IN)


def scatter_near(parts, step2, z):
    own, near, _, other = parts
    f32 = jnp.float32
    up2, down2 = step2
    go_up = jnp.where(z == 1, other, near).astype(f32) + up2.astype(f32)
    go_down = jnp.where(z == 2, other, near).astype(f32) + down2.astype(f32)
    up3 = lax.ppermute(go_up.astype(jnp.bfloat16), "tp", UP)
    down3 = lax.ppermute(go_down.astype(jnp.bfloat16), "tp", DOWN)
    return own.astype(f32) + up3.astype(f32) + down3.astype(f32)


def attention_kernel(has_prev, is_last, first, feature_count, *refs):
    refs = list(refs)
    raw_ref, inv_ref, ga_ref, adv_ref, cos_ref, sin_ref, start_ref = refs[:7]
    refs = refs[7:]
    if has_prev:
        raw_prev, inv_prev, dq_prev, dk_prev, dv_prev = refs[:5]
        refs = refs[5:]
    dqkv_ref, dscaled_ref, mean_ref, out_ref = refs[:4]
    refs = refs[4:]
    if not is_last:
        dq_next, dk_next, dv_next = refs[:3]
        refs = refs[3:]
    qkv_b, dq_b, dk_acc, dv_acc = refs
    rows = raw_ref.shape[0]
    heads = ga_ref.shape[1] // HD
    qw = heads * HD
    scale = HD ** (-0.5)
    f32, bf16 = jnp.float32, jnp.bfloat16
    blocks = rows // BLOCK

    def span(block):
        return slice(block * BLOCK, (block + 1) * BLOCK)

    def turn(value, cos, sin):
        return value * cos + pltpu.roll(value, HD // 2, 1) * sin

    def whole(block):
        return slice(first + block * BLOCK, first + (block + 1) * BLOCK)

    def linear(block, cols):
        if block < 0:
            last = raw_prev.shape[0]
            return raw_prev[last - BLOCK : last, cols] * inv_prev[last - BLOCK : last, :]
        return raw_ref[span(block), cols] * inv_ref[span(block), :]

    def prepare(block, from_head):
        cos, sin = cos_ref[whole(block), :], sin_ref[whole(block), :]
        for h in range(from_head, heads + 1):
            cols = slice(h * HD, (h + 1) * HD)
            qkv_b[span(block + 1), cols] = turn(linear(block, cols), cos, sin).astype(bf16)
        cols = slice(qw + HD, qw + 2 * HD)
        qkv_b[span(block + 1), cols] = linear(block, cols).astype(bf16)

    if has_prev:
        prepare(-1, heads)
        dq_b[span(0), :] = dq_prev[...]
        dk_acc[span(0), :] = dk_prev[...]
        dv_acc[span(0), :] = dv_prev[...]
    else:
        qkv_b[span(0), :] = jnp.zeros((BLOCK, qkv_b.shape[1]), bf16)
        dk_acc[span(0), :] = jnp.zeros((BLOCK, HD), f32)
        dv_acc[span(0), :] = jnp.zeros((BLOCK, HD), f32)

    for block in range(blocks):
        prepare(block, 0)
        adv = adv_ref[whole(block), :]
        here, after = span(block), span(block + 1)
        both = slice(block * BLOCK, (block + 2) * BLOCK)
        qs = jnp.concatenate(
            [qkv_b[after, h * HD : (h + 1) * HD] for h in range(heads)], axis=0
        )
        gs = jnp.concatenate(
            [(ga_ref[here, h * HD : (h + 1) * HD] * adv).astype(bf16) for h in range(heads)], axis=0
        )
        ks = qkv_b[both, qw : qw + HD]
        vs = qkv_b[both, qw + HD : qw + 2 * HD]
        start = start_ref[whole(block), :] - (first + (block - 1) * BLOCK)
        col = lax.broadcasted_iota(jnp.int32, (BLOCK, 2 * BLOCK), 1)
        row = lax.broadcasted_iota(jnp.int32, (BLOCK, 2 * BLOCK), 0) + BLOCK
        bias = jnp.where((col >= start) & (col <= row), 0.0, -1e30)
        bias = jnp.concatenate([bias] * heads, axis=0)
        scores = times_trans(qs, ks) * scale + bias
        top = jnp.max(scores, axis=-1, keepdims=True)
        weight = jnp.exp(scores - top)
        prob = weight / jnp.sum(weight, axis=-1, keepdims=True)
        prob_b = prob.astype(bf16)
        out = matmul(prob_b, vs)
        grad_prob = times_trans(gs, vs)
        delta = jnp.sum(prob * grad_prob, axis=-1, keepdims=True)
        ds = (prob * (grad_prob - delta) * scale).astype(bf16)
        dq = matmul(ds, ks)
        dk_acc[span(block), :] += contract_rows(ds[:, :BLOCK], qs)
        dk_acc[after, :] = contract_rows(ds[:, BLOCK:], qs)
        dv_acc[span(block), :] += contract_rows(prob_b[:, :BLOCK], gs)
        dv_acc[after, :] = contract_rows(prob_b[:, BLOCK:], gs)
        cos, sin = cos_ref[whole(block), :], sin_ref[whole(block), :]
        for h in range(heads):
            cols = slice(h * HD, (h + 1) * HD)
            out_ref[here, cols] = (out[span(h), :].astype(bf16).astype(f32) * adv).astype(bf16)
            dq_b[after, cols] = turn(dq[span(h), :], cos, -sin).astype(bf16)

    begin = -1 if has_prev else 0
    end = blocks if is_last else blocks - 1
    for block in range(begin, end):
        to = span(block - begin)
        cos, sin = cos_ref[whole(block), :], sin_ref[whole(block), :]
        inv = inv_prev[inv_prev.shape[0] - BLOCK :, :] if block < 0 else inv_ref[span(block), :]
        total = jnp.zeros((BLOCK, 1), f32)
        for h in range(heads + 2):
            cols = slice(h * HD, (h + 1) * HD)
            if h < heads:
                grad = dq_b[span(block + 1), cols]
            elif h == heads:
                grad = turn(dk_acc[span(block + 1), :], cos, -sin).astype(bf16)
            else:
                grad = dv_acc[span(block + 1), :].astype(bf16)
            dqkv_ref[to, cols] = grad
            grad = grad.astype(f32)
            dscaled_ref[to, cols] = (grad * inv).astype(bf16)
            total += jnp.sum(grad * linear(block, cols), axis=-1, keepdims=True)
        mean_ref[to, 0:1] = inv
        mean_ref[to, 1:2] = inv * inv * total * (1.0 / feature_count)
    if not is_last:
        dq_next[...] = dq_b[span(blocks), :]
        dk_next[...] = dk_acc[span(blocks), :]
        dv_next[...] = dv_acc[span(blocks), :]


def attention(first, total, feature_count, raw, inv, ga, adv, cos, sin, start, prev):
    rows, width = raw.shape
    qw = ga.shape[1]
    is_last = first + rows == total
    final = rows + (BLOCK if prev else 0) - (0 if is_last else BLOCK)
    f32, bf16 = jnp.float32, jnp.bfloat16
    out_shape = [
        jax.ShapeDtypeStruct((final, width), bf16),
        jax.ShapeDtypeStruct((final, width), bf16),
        jax.ShapeDtypeStruct((final, 2), f32),
        jax.ShapeDtypeStruct((rows, qw), bf16),
    ]
    if not is_last:
        out_shape += [
            jax.ShapeDtypeStruct((BLOCK, qw), bf16),
            jax.ShapeDtypeStruct((BLOCK, HD), f32),
            jax.ShapeDtypeStruct((BLOCK, HD), f32),
        ]
    operands = [raw, inv, ga, adv, cos, sin, start] + list(prev)
    vmem = pl.BlockSpec(memory_space=pltpu.VMEM)
    return pl.pallas_call(
        functools.partial(attention_kernel, bool(prev), is_last, first, feature_count),
        out_shape=out_shape,
        in_specs=[vmem] * len(operands),
        out_specs=[vmem] * len(out_shape),
        scratch_shapes=[
            pltpu.VMEM((rows + BLOCK, width), bf16),
            pltpu.VMEM((rows + BLOCK, qw), bf16),
            pltpu.VMEM((rows + BLOCK, HD), f32),
            pltpu.VMEM((rows + BLOCK, HD), f32),
        ],
        compiler_params=pltpu.CompilerParams(vmem_limit_bytes=32 * 1024 * 1024),
        cost_estimate=pl.CostEstimate(
            flops=rows * 2 * BLOCK * HD * 12 * (qw // HD),
            bytes_accessed=rows * width * 8 + rows * qw * 6,
            transcendentals=rows * 2 * BLOCK * (qw // HD),
        ),
        name="attention",
    )(*operands)


def input_grad_kernel(skip, *refs):
    dqkv_ref, scale_ref = refs[:2]
    w_refs, gain_refs, rows_refs = refs[2:6], refs[6:10], refs[10:-4]
    out_refs = refs[-4:]
    width = dqkv_ref.shape[1]
    final = dqkv_ref.shape[0]
    pieces = len(rows_refs) // 4
    for k in (3, 2, 1, 0):
        weight = w_refs[k][:, :width]
        gain = gain_refs[k][...]
        for base in range(0, final, BLOCK):
            here = slice(base, base + BLOCK)
            at = base + skip
            rows = rows_refs[k * pieces]
            if at >= rows.shape[0]:
                at -= rows.shape[0]
                rows = rows_refs[k * pieces + 1]
            product = times_trans(dqkv_ref[here, :], weight)
            out_refs[k][here, :] = (
                product * gain * scale_ref[here, 0:1]
                - rows[at : at + BLOCK, :].astype(jnp.float32) * scale_ref[here, 1:2]
            ).astype(jnp.bfloat16)


def input_terms(dqkv, scales, weights, gains, rows, skip):
    final, width = dqkv.shape
    features = weights[0].shape[0]
    operands = [dqkv, scales, *weights, *gains, *[piece for k in range(4) for piece in rows[k]]]
    vmem = pl.BlockSpec(memory_space=pltpu.VMEM)
    return pl.pallas_call(
        functools.partial(input_grad_kernel, skip),
        out_shape=[jax.ShapeDtypeStruct((final, features), jnp.bfloat16)] * 4,
        in_specs=[vmem] * len(operands),
        out_specs=[vmem] * 4,
        compiler_params=pltpu.CompilerParams(vmem_limit_bytes=40 * 1024 * 1024),
        cost_estimate=pl.CostEstimate(
            flops=8 * final * width * features,
            bytes_accessed=16 * final * features + 8 * features * width,
            transcendentals=0,
        ),
        name="input_terms",
    )(*operands)


def weight_grad_kernel(per_row, place_ref, *refs):
    right_ref, gain_ref, keep_ref, send_ref, term = refs[-5:]
    left_refs = refs[:-5]
    features = left_refs[0].shape[1]
    step = pl.program_id(0)
    for k in range(4):

        @pl.when(step == k)
        def _():
            total, base = None, 0
            for ref in left_refs[k * len(left_refs) // 4 : (k + 1) * len(left_refs) // 4]:
                part = contract_rows(ref[...], right_ref[base : base + ref.shape[0], :])
                base += ref.shape[0]
                total = part if total is None else total + part
            term[...] = (total * gain_ref[0]).astype(jnp.bfloat16)

    core = place_ref[4]
    for group in range(features // (2 * per_row)):
        rows = slice(group * per_row, (group + 1) * per_row)
        base = 2 * group * per_row
        keep = pl.multiple_of(base + core * per_row, 16)
        send = pl.multiple_of(base + (1 - core) * per_row, 16)
        keep_ref[rows, :] = term[pl.ds(keep, per_row), :]
        send_ref[rows, :] = term[pl.ds(send, per_row), :]


def weight_grads(places, left_chunks, right, gain, per_row):
    features = gain.shape[1]
    width = right.shape[1]
    operands = [chunk[k] for k in range(4) for chunk in left_chunks] + [right]
    once = [
        pl.BlockSpec(o.shape, lambda k, place: (0, 0), pipeline_mode=pl.Buffered(1))
        for o in operands
    ]
    out = jax.ShapeDtypeStruct((2 * features, width), jnp.bfloat16)
    return pl.pallas_call(
        functools.partial(weight_grad_kernel, per_row),
        out_shape=[out, out],
        grid_spec=pltpu.PrefetchScalarGridSpec(
            num_scalar_prefetch=1,
            grid=(4,),
            in_specs=once
            + [pl.BlockSpec((1, features, 1), lambda k, place: (place[k], 0, 0))],
            out_specs=[pl.BlockSpec((features // 2, width), lambda k, place: (place[k], 0))] * 2,
            scratch_shapes=[pltpu.VMEM((features, width), jnp.bfloat16)],
        ),
        compiler_params=pltpu.CompilerParams(vmem_limit_bytes=40 * 1024 * 1024),
        cost_estimate=pl.CostEstimate(
            flops=2 * right.shape[0] * 4 * features * width,
            bytes_accessed=4 * features * (2 * right.shape[0] + 2 * width),
            transcendentals=0,
        ),
        name="weight_grads",
    )(places, *operands, gain[:, :, None])


def per_device(roll_rows, dest, lengths, clusters, log_prob_grad, gain, w_q, w_k, w_v, w_o_t):
    sequence_count = dest.shape[0]
    max_len, local_features = roll_rows.shape[1:]
    row_count = log_prob_grad.shape[0]
    replicas = lax.axis_size("fsdp")
    per_pair = sequence_count // replicas
    me = lax.axis_index("fsdp")
    z = lax.axis_index("tp")
    f32, bf16 = jnp.float32, jnp.bfloat16
    q_cols, k_cols = w_q.shape[1], w_k.shape[1]
    qkv_cols = q_cols + 2 * k_cols
    feature_count = gain.shape[0]

    core = me % 2
    same_core = [list(range(c, replicas, 2)) for c in range(2)]
    other_core = [(i, i ^ 1) for i in range(replicas)]

    g_slices = [slice(0, row_count - 2 * BLOCK), slice(row_count - 2 * BLOCK, row_count)]
    g_own = [log_prob_grad[c, :] for c in g_slices]
    g_step1 = [gather_near(g) for g in g_own]
    g_far2 = [gather_far(step1, z) for step1 in g_step1]
    g_far3 = [gather_end(after(g_far2[0], g_step1[1][0])), gather_end(g_far2[1])]
    g_chunks = [shards(*parts, z) for parts in zip(g_own, g_step1, g_far2, g_far3)]
    tick = lax.ppermute(gain[: 8 * HD], "tp", UP)

    slot_ids = jnp.arange(sequence_count, dtype=jnp.int32)
    earlier_dest = dest[None, :] < dest[:, None]
    send_block = jnp.sum(earlier_dest.astype(jnp.int32), axis=1)
    source = jnp.sum(
        jnp.where(send_block[None, :] == slot_ids[:, None], slot_ids[None, :], 0), axis=1
    )
    send_rows = jnp.take(roll_rows, after(source, tick), axis=0, mode="clip")
    arrived_rows = lax.all_to_all(send_rows, "fsdp", split_axis=0, concat_axis=0, tiled=True)

    ballots = clusters.reshape(sequence_count // GSIZE, GSIZE)
    vote_share = jnp.mean((ballots[:, :, None] == ballots[:, None, :]).astype(f32), axis=2)
    advantage = (vote_share - jnp.mean(vote_share, axis=1, keepdims=True)).reshape(sequence_count)
    tags = jnp.stack([(dest % sequence_count).astype(f32), advantage], axis=1)
    picked = send_block[None, :] == slot_ids[:, None]
    tags = jnp.sum(jnp.where(picked[:, :, None], tags[None, :, :], 0.0), axis=1).astype(bf16)
    tags = lax.all_to_all(tags, "fsdp", split_axis=0, concat_axis=0, tiled=True).astype(f32)
    holder = tags[None, :, 0].astype(jnp.int32) == slot_ids[:, None]
    slot_of = jnp.sum(jnp.where(holder, slot_ids[None, :], 0), axis=1)
    seq_advantage = jnp.sum(jnp.where(holder, tags[None, :, 1], 0.0), axis=1)

    lengths_row = lengths.reshape(sequence_count)
    sequence_ends = jnp.cumsum(lengths_row)
    sequence_starts = sequence_ends - lengths_row
    row_index = jnp.arange(row_count, dtype=jnp.int32)
    one_hot = (sequence_ends[None, :] > row_index[:, None]) & (
        sequence_starts[None, :] <= row_index[:, None]
    )
    row_start = jnp.sum(jnp.where(one_hot, sequence_starts[None, :], 0), axis=1)
    position = row_index - row_start
    row_slot = jnp.sum(jnp.where(one_hot, slot_of[None, :], 0), axis=1)
    adv = jnp.sum(jnp.where(one_hot, seq_advantage[None, :], 0.0), axis=1)[:, None]
    half_width = HD // 2
    frequency = ROPE_BASE ** (-(2.0 * jnp.arange(half_width, dtype=f32)) / HD)
    angles = position.astype(f32)[:, None] * frequency[None, :]
    cos, sin = jnp.cos(angles), jnp.sin(angles)
    cos = jnp.concatenate([cos, cos], axis=1)
    sin = jnp.concatenate([-sin, sin], axis=1)

    own_rows = lax.all_gather(
        jnp.concatenate([w_q, w_k, w_v, w_o_t], axis=1),
        "fsdp",
        axis=0,
        axis_index_groups=same_core,
    )
    other_rows = lax.ppermute(own_rows, "fsdp", other_core)
    per_row = own_rows.shape[1]
    gain_parts = gain.astype(f32).reshape(4, 1, local_features)
    w_parts, gain_k = [], []
    for k in range(4):
        pair = [
            lax.dynamic_index_in_dim(r.reshape(4, -1, per_row, r.shape[2]), z ^ k, 0, keepdims=False)
            for r in (own_rows, other_rows)
        ]
        swapped = core == 1
        w_parts.append(
            jnp.stack(
                [jnp.where(swapped, pair[1], pair[0]), jnp.where(swapped, pair[0], pair[1])], axis=1
            ).reshape(local_features, -1)
        )
        gain_k.append(lax.dynamic_index_in_dim(gain_parts, z ^ k, 0, keepdims=False))

    arrived_rows = after(arrived_rows, g_far3[0], g_far2[1])
    x_all = jnp.take(
        arrived_rows.reshape(sequence_count * max_len, local_features),
        row_slot * max_len + position,
        axis=0,
        mode="clip",
    )
    size = 2 * BLOCK
    count = row_count // size
    x_own = [x_all[i * size : (i + 1) * size, :] for i in range(count)]
    start = row_start[:, None]
    ga = jnp.concatenate(
        [sum(matmul(g[k], w_parts[k][:, qkv_cols:]) for k in range(4)) for g in g_chunks], axis=0
    )

    def project(x_parts):
        raw = sum(
            matmul((x_parts[k].astype(f32) * gain_k[k]).astype(bf16), w_parts[k][:, :qkv_cols])
            for k in range(4)
        )
        squares = sum(
            jnp.sum(jnp.square(x_parts[k].astype(f32)), axis=1, keepdims=True) for k in range(4)
        )
        return raw, lax.rsqrt(squares / feature_count + NORM_EPSILON)

    def backward(i, raw, inv, prev):
        base = i * size
        dqkv, scaled, scales, out, *carry = attention(
            base, row_count, feature_count, raw, inv, ga[base : base + size],
            adv, cos, sin, start, prev,
        )
        near = x_chunks[max(i - 1, 0) : i + 1]
        terms = input_terms(
            dqkv,
            scales,
            w_parts,
            gain_k,
            [[piece[k] for piece in near] for k in range(4)],
            BLOCK if i else 0,
        )
        return terms, scaled, out, (raw, inv, *carry)

    x_chunks = []
    x1 = [gather_near(x_own[0])]
    x1.append(gather_near(after(x_own[1], x1[0][0])))
    x2 = [gather_far((after(x1[0][0], g_far3[1]), x1[0][1]), z)]
    x1.append(gather_near(after(x_own[2], x1[1][0], x2[0])))
    x3 = [gather_end(x2[0])]
    x2.append(gather_far(x1[1], z))
    x_chunks.append(shards(x_own[0], x1[0], x2[0], x3[0], z))
    x3.append(gather_end(after(x2[1], x3[0], w_parts[0])))
    raw, inv = project(x_chunks[0])
    x2.append(gather_far((after(x1[2][0], raw), x1[2][1]), z))
    terms0, scaled0, out0, prev = backward(0, raw, inv, ())
    x3.append(gather_end(after(x2[2], x3[1], terms0[3])))
    end0 = scatter_end(terms0)
    step0 = scatter_far(terms0, end0)
    dx0 = scatter_near(terms0, step0, z)

    x_chunks.append(shards(x_own[1], x1[1], x2[1], x3[1], z))
    raw, inv = project(x_chunks[1])
    terms1, scaled1, out1, prev = backward(1, after(raw, end0), inv, prev)
    end1 = scatter_end([*terms1[:3], after(terms1[3], *step0)])
    step1 = scatter_far(terms1, after(end1, dx0))
    dx1 = scatter_near(terms1, step1, z)

    x_chunks.append(shards(x_own[2], x1[2], x2[2], x3[2], z))
    raw, inv = project(x_chunks[2])
    terms2, scaled2, out2, prev = backward(2, after(raw, end1), inv, prev)
    end2 = scatter_end([*terms2[:3], after(terms2[3], *step1)])
    step2 = scatter_far(terms2, after(end2, dx1))
    dx2 = scatter_near(terms2, step2, z)
    dx = jnp.concatenate([dx0, dx1, dx2], axis=0)
    input_grad = (adv * log_prob_grad.astype(f32) + dx).astype(bf16)

    places = jnp.stack([z ^ k for k in range(4)] + [core]).astype(jnp.int32)

    def reduced(chunks, right, gain_rows):
        keep, send = weight_grads(places, chunks, right, gain_rows, per_row)
        other = lax.ppermute(send, "fsdp", other_core)
        pair = (keep.astype(f32) + other.astype(f32)).astype(bf16)
        return keep, lax.psum_scatter(
            pair, "fsdp", scatter_dimension=0, axis_index_groups=same_core, tiled=True
        )

    ones = jnp.ones((4, local_features), f32)
    out = after(jnp.concatenate([out0, out1, out2], axis=0), terms2[3])
    keep, grad_o_t = reduced(g_chunks, out, ones)
    scaled = after(jnp.concatenate([scaled0, scaled1, scaled2], axis=0), end2, keep)
    _, summed = reduced(x_chunks, scaled, gain_parts[:, 0, :])
    grad_q = summed[:, :q_cols]
    grad_k = summed[:, q_cols : q_cols + k_cols]
    grad_v = summed[:, q_cols + k_cols :]
    return (input_grad, grad_q, grad_k, grad_v, grad_o_t)


def solution(mesh):
    in_specs = (
        P("fsdp", None, "tp"),
        P("fsdp"),
        P("fsdp", None),
        P("fsdp"),
        P("fsdp", "tp"),
        P(),
        P("fsdp", "tp"),
        P("fsdp", "tp"),
        P("fsdp", "tp"),
        P("fsdp", "tp"),
    )
    out_specs = (
        P("fsdp", "tp"),
        P("fsdp", "tp"),
        P("fsdp", "tp"),
        P("fsdp", "tp"),
        P("fsdp", "tp"),
    )
    return jax.shard_map(
        per_device, mesh=mesh, in_specs=in_specs, out_specs=out_specs, check_vma=False
    )
```

```python
import functools

import jax
import jax.numpy as jnp
from jax import lax
from jax.experimental import pallas as pl
from jax.experimental.pallas import tpu as pltpu
from jax.sharding import PartitionSpec as P

KEY_VALUE_HEADS = 4
HD = 128
QUERY_HEADS = 16
GSIZE = 16
ROPE_BASE = 1000000.0
NORM_EPSILON = 1e-06
BLOCK = 128

UP = [(0, 1), (1, 2), (2, 3)]
DOWN = [(1, 0), (2, 1), (3, 2)]
UP_MID = [(1, 2), (2, 3)]
DOWN_MID = [(1, 0), (2, 1)]
TO_ENDS = [(2, 3), (1, 0)]
FROM_ENDS = [(3, 2), (0, 1)]
UP_IN = [(0, 1), (1, 2)]
DOWN_IN = [(3, 2), (2, 1)]


def contract_rows(left, right):
    return lax.dot_general(
        left, right, (((0,), (0,)), ((), ())), preferred_element_type=jnp.float32
    )


def times_trans(left, right):
    return lax.dot_general(
        left, right, (((1,), (1,)), ((), ())), preferred_element_type=jnp.float32
    )


def matmul(left, right):
    return jnp.dot(left, right, preferred_element_type=jnp.float32)


def gather_near(own):
    return lax.ppermute(own, "tp", UP), lax.ppermute(own, "tp", DOWN)


def gather_far(step1, z):
    up2 = lax.ppermute(step1[0], "tp", UP_MID)
    down2 = lax.ppermute(step1[1], "tp", DOWN_MID)
    return jnp.where(z >= 2, up2, down2)


def gather_end(far2):
    return lax.ppermute(far2, "tp", TO_ENDS)


def shards(own, step1, far2, far3, z):
    up1, down1 = step1
    near = jnp.where(z % 2 == 1, up1, down1)
    other = jnp.where(z == 1, down1, jnp.where(z == 2, up1, far3))
    return [own, near, far2, other]


def after(value, *earlier):
    return lax.optimization_barrier((value, *earlier))[0]


def scatter_end(parts):
    return lax.ppermute(parts[3], "tp", FROM_ENDS)


def scatter_far(parts, from_end):
    total2 = (parts[2].astype(jnp.float32) + from_end.astype(jnp.float32)).astype(jnp.bfloat16)
    return lax.ppermute(total2, "tp", UP_IN), lax.ppermute(total2, "tp", DOWN_IN)


def scatter_near(parts, step2, z):
    own, near, _, other = parts
    f32 = jnp.float32
    up2, down2 = step2
    go_up = jnp.where(z == 1, other, near).astype(f32) + up2.astype(f32)
    go_down = jnp.where(z == 2, other, near).astype(f32) + down2.astype(f32)
    up3 = lax.ppermute(go_up.astype(jnp.bfloat16), "tp", UP)
    down3 = lax.ppermute(go_down.astype(jnp.bfloat16), "tp", DOWN)
    return own.astype(f32) + up3.astype(f32) + down3.astype(f32)


def attention_kernel(has_prev, is_last, first, feature_count, *refs):
    refs = list(refs)
    raw_ref, inv_ref, ga_ref, adv_ref, cos_ref, sin_ref, start_ref = refs[:7]
    refs = refs[7:]
    if has_prev:
        raw_prev, inv_prev, dq_prev, dk_prev, dv_prev = refs[:5]
        refs = refs[5:]
    dqkv_ref, dscaled_ref, mean_ref, out_ref = refs[:4]
    refs = refs[4:]
    if not is_last:
        dq_next, dk_next, dv_next = refs[:3]
        refs = refs[3:]
    qkv_b, dq_b, dk_acc, dv_acc = refs
    rows = raw_ref.shape[0]
    heads = ga_ref.shape[1] // HD
    qw = heads * HD
    scale = HD ** (-0.5)
    f32, bf16 = jnp.float32, jnp.bfloat16
    blocks = rows // BLOCK

    def span(block):
        return slice(block * BLOCK, (block + 1) * BLOCK)

    def turn(value, cos, sin):
        return value * cos + pltpu.roll(value, HD // 2, 1) * sin

    def whole(block):
        return slice(first + block * BLOCK, first + (block + 1) * BLOCK)

    def linear(block, cols):
        if block < 0:
            last = raw_prev.shape[0]
            return raw_prev[last - BLOCK : last, cols] * inv_prev[last - BLOCK : last, :]
        return raw_ref[span(block), cols] * inv_ref[span(block), :]

    def prepare(block, from_head):
        cos, sin = cos_ref[whole(block), :], sin_ref[whole(block), :]
        for h in range(from_head, heads + 1):
            cols = slice(h * HD, (h + 1) * HD)
            qkv_b[span(block + 1), cols] = turn(linear(block, cols), cos, sin).astype(bf16)
        cols = slice(qw + HD, qw + 2 * HD)
        qkv_b[span(block + 1), cols] = linear(block, cols).astype(bf16)

    if has_prev:
        prepare(-1, heads)
        dq_b[span(0), :] = dq_prev[...]
        dk_acc[span(0), :] = dk_prev[...]
        dv_acc[span(0), :] = dv_prev[...]
    else:
        qkv_b[span(0), :] = jnp.zeros((BLOCK, qkv_b.shape[1]), bf16)
        dk_acc[span(0), :] = jnp.zeros((BLOCK, HD), f32)
        dv_acc[span(0), :] = jnp.zeros((BLOCK, HD), f32)

    for block in range(blocks):
        prepare(block, 0)
        adv = adv_ref[whole(block), :]
        here, after = span(block), span(block + 1)
        both = slice(block * BLOCK, (block + 2) * BLOCK)
        qs = jnp.concatenate(
            [qkv_b[after, h * HD : (h + 1) * HD] for h in range(heads)], axis=0
        )
        gs = jnp.concatenate(
            [(ga_ref[here, h * HD : (h + 1) * HD] * adv).astype(bf16) for h in range(heads)], axis=0
        )
        ks = qkv_b[both, qw : qw + HD]
        vs = qkv_b[both, qw + HD : qw + 2 * HD]
        start = start_ref[whole(block), :] - (first + (block - 1) * BLOCK)
        col = lax.broadcasted_iota(jnp.int32, (BLOCK, 2 * BLOCK), 1)
        row = lax.broadcasted_iota(jnp.int32, (BLOCK, 2 * BLOCK), 0) + BLOCK
        bias = jnp.where((col >= start) & (col <= row), 0.0, -1e30)
        bias = jnp.concatenate([bias] * heads, axis=0)
        scores = times_trans(qs, ks) * scale + bias
        top = jnp.max(scores, axis=-1, keepdims=True)
        weight = jnp.exp(scores - top)
        prob = weight / jnp.sum(weight, axis=-1, keepdims=True)
        prob_b = prob.astype(bf16)
        out = matmul(prob_b, vs)
        grad_prob = times_trans(gs, vs)
        delta = jnp.sum(prob * grad_prob, axis=-1, keepdims=True)
        ds = (prob * (grad_prob - delta) * scale).astype(bf16)
        dq = matmul(ds, ks)
        dk_acc[span(block), :] += contract_rows(ds[:, :BLOCK], qs)
        dk_acc[after, :] = contract_rows(ds[:, BLOCK:], qs)
        dv_acc[span(block), :] += contract_rows(prob_b[:, :BLOCK], gs)
        dv_acc[after, :] = contract_rows(prob_b[:, BLOCK:], gs)
        cos, sin = cos_ref[whole(block), :], sin_ref[whole(block), :]
        for h in range(heads):
            cols = slice(h * HD, (h + 1) * HD)
            out_ref[here, cols] = (out[span(h), :].astype(bf16).astype(f32) * adv).astype(bf16)
            dq_b[after, cols] = turn(dq[span(h), :], cos, -sin).astype(bf16)

    begin = -1 if has_prev else 0
    end = blocks if is_last else blocks - 1
    for block in range(begin, end):
        to = span(block - begin)
        cos, sin = cos_ref[whole(block), :], sin_ref[whole(block), :]
        inv = inv_prev[inv_prev.shape[0] - BLOCK :, :] if block < 0 else inv_ref[span(block), :]
        total = jnp.zeros((BLOCK, 1), f32)
        for h in range(heads + 2):
            cols = slice(h * HD, (h + 1) * HD)
            if h < heads:
                grad = dq_b[span(block + 1), cols]
            elif h == heads:
                grad = turn(dk_acc[span(block + 1), :], cos, -sin).astype(bf16)
            else:
                grad = dv_acc[span(block + 1), :].astype(bf16)
            dqkv_ref[to, cols] = grad
            grad = grad.astype(f32)
            dscaled_ref[to, cols] = (grad * inv).astype(bf16)
            total += jnp.sum(grad * linear(block, cols), axis=-1, keepdims=True)
        mean_ref[to, 0:1] = inv
        mean_ref[to, 1:2] = inv * inv * total * (1.0 / feature_count)
    if not is_last:
        dq_next[...] = dq_b[span(blocks), :]
        dk_next[...] = dk_acc[span(blocks), :]
        dv_next[...] = dv_acc[span(blocks), :]


def attention(first, total, feature_count, raw, inv, ga, adv, cos, sin, start, prev):
    rows, width = raw.shape
    qw = ga.shape[1]
    is_last = first + rows == total
    final = rows + (BLOCK if prev else 0) - (0 if is_last else BLOCK)
    f32, bf16 = jnp.float32, jnp.bfloat16
    out_shape = [
        jax.ShapeDtypeStruct((final, width), bf16),
        jax.ShapeDtypeStruct((final, width), bf16),
        jax.ShapeDtypeStruct((final, 2), f32),
        jax.ShapeDtypeStruct((rows, qw), bf16),
    ]
    if not is_last:
        out_shape += [
            jax.ShapeDtypeStruct((BLOCK, qw), bf16),
            jax.ShapeDtypeStruct((BLOCK, HD), f32),
            jax.ShapeDtypeStruct((BLOCK, HD), f32),
        ]
    operands = [raw, inv, ga, adv, cos, sin, start] + list(prev)
    vmem = pl.BlockSpec(memory_space=pltpu.VMEM)
    return pl.pallas_call(
        functools.partial(attention_kernel, bool(prev), is_last, first, feature_count),
        out_shape=out_shape,
        in_specs=[vmem] * len(operands),
        out_specs=[vmem] * len(out_shape),
        scratch_shapes=[
            pltpu.VMEM((rows + BLOCK, width), bf16),
            pltpu.VMEM((rows + BLOCK, qw), bf16),
            pltpu.VMEM((rows + BLOCK, HD), f32),
            pltpu.VMEM((rows + BLOCK, HD), f32),
        ],
        compiler_params=pltpu.CompilerParams(vmem_limit_bytes=32 * 1024 * 1024),
        cost_estimate=pl.CostEstimate(
            flops=rows * 2 * BLOCK * HD * 12 * (qw // HD),
            bytes_accessed=rows * width * 8 + rows * qw * 6,
            transcendentals=rows * 2 * BLOCK * (qw // HD),
        ),
        name="attention",
    )(*operands)


def weight_grad_kernel(x_count, *refs):
    x_refs = refs[:x_count]
    g_ref, scaled_ref, out_ref, gain_ref, term_ref = refs[x_count:]
    width = scaled_ref.shape[1]
    total, base = None, 0
    for ref in x_refs:
        part = contract_rows(ref[...], scaled_ref[base : base + ref.shape[0], :])
        base += ref.shape[0]
        total = part if total is None else total + part
    term_ref[:, :width] = (total * gain_ref[0]).astype(jnp.bfloat16)
    term_ref[:, width:] = contract_rows(g_ref[...], out_ref[...]).astype(jnp.bfloat16)


def weight_grads(x_chunks, g_rows, scaled, out, gain):
    features = gain.shape[1]
    width = scaled.shape[1] + out.shape[1]
    return pl.pallas_call(
        functools.partial(weight_grad_kernel, len(x_chunks)),
        out_shape=jax.ShapeDtypeStruct((4 * features, width), jnp.bfloat16),
        grid=(4,),
        in_specs=[
            pl.BlockSpec((rows.shape[0], features), lambda j: (0, j)) for rows in (*x_chunks, g_rows)
        ]
        + [
            pl.BlockSpec(o.shape, lambda j: (0, 0), pipeline_mode=pl.Buffered(1))
            for o in (scaled, out)
        ]
        + [pl.BlockSpec((1, features, 1), lambda j: (j, 0, 0))],
        out_specs=pl.BlockSpec((features, width), lambda j: (j, 0)),
        compiler_params=pltpu.CompilerParams(vmem_limit_bytes=40 * 1024 * 1024),
        cost_estimate=pl.CostEstimate(
            flops=2 * scaled.shape[0] * 4 * features * width,
            bytes_accessed=4 * features * (4 * scaled.shape[0] + 2 * width),
            transcendentals=0,
        ),
        name="weight_grads",
    )(*x_chunks, g_rows, scaled, out, gain[:, :, None])


def per_device(roll_rows, dest, lengths, clusters, log_prob_grad, gain, w_q, w_k, w_v, w_o_t):
    sequence_count = dest.shape[0]
    max_len, local_features = roll_rows.shape[1:]
    row_count = log_prob_grad.shape[0]
    replicas = lax.axis_size("fsdp")
    per_pair = sequence_count // replicas
    me = lax.axis_index("fsdp")
    z = lax.axis_index("tp")
    f32, bf16 = jnp.float32, jnp.bfloat16
    q_cols, k_cols = w_q.shape[1], w_k.shape[1]
    qkv_cols = q_cols + 2 * k_cols
    feature_count = gain.shape[0]

    g_rows = lax.all_gather(log_prob_grad, "tp", axis=1, tiled=True)

    slot_ids = jnp.arange(sequence_count, dtype=jnp.int32)
    earlier_dest = dest[None, :] < dest[:, None]
    send_block = jnp.sum(earlier_dest.astype(jnp.int32), axis=1)
    source = jnp.sum(
        jnp.where(send_block[None, :] == slot_ids[:, None], slot_ids[None, :], 0), axis=1
    )
    send_rows = jnp.take(roll_rows, source, axis=0, mode="clip")
    arrived_rows = lax.all_to_all(send_rows, "fsdp", split_axis=0, concat_axis=0, tiled=True)

    ballots = clusters.reshape(sequence_count // GSIZE, GSIZE)
    vote_share = jnp.mean((ballots[:, :, None] == ballots[:, None, :]).astype(f32), axis=2)
    advantage = (vote_share - jnp.mean(vote_share, axis=1, keepdims=True)).reshape(sequence_count)
    tags = jnp.stack([(dest % sequence_count).astype(f32), advantage], axis=1)
    picked = send_block[None, :] == slot_ids[:, None]
    tags = jnp.sum(jnp.where(picked[:, :, None], tags[None, :, :], 0.0), axis=1).astype(bf16)
    tags = lax.all_to_all(tags, "fsdp", split_axis=0, concat_axis=0, tiled=True).astype(f32)
    holder = tags[None, :, 0].astype(jnp.int32) == slot_ids[:, None]
    slot_of = jnp.sum(jnp.where(holder, slot_ids[None, :], 0), axis=1)
    seq_advantage = jnp.sum(jnp.where(holder, tags[None, :, 1], 0.0), axis=1)

    lengths_row = lengths.reshape(sequence_count)
    sequence_ends = jnp.cumsum(lengths_row)
    sequence_starts = sequence_ends - lengths_row
    row_index = jnp.arange(row_count, dtype=jnp.int32)
    one_hot = (sequence_ends[None, :] > row_index[:, None]) & (
        sequence_starts[None, :] <= row_index[:, None]
    )
    row_start = jnp.sum(jnp.where(one_hot, sequence_starts[None, :], 0), axis=1)
    position = row_index - row_start
    row_slot = jnp.sum(jnp.where(one_hot, slot_of[None, :], 0), axis=1)
    adv = jnp.sum(jnp.where(one_hot, seq_advantage[None, :], 0.0), axis=1)[:, None]
    half_width = HD // 2
    frequency = ROPE_BASE ** (-(2.0 * jnp.arange(half_width, dtype=f32)) / HD)
    angles = position.astype(f32)[:, None] * frequency[None, :]
    cos, sin = jnp.cos(angles), jnp.sin(angles)
    cos = jnp.concatenate([cos, cos], axis=1)
    sin = jnp.concatenate([-sin, sin], axis=1)

    x_own = jnp.take(
        arrived_rows.reshape(sequence_count * max_len, local_features),
        row_slot * max_len + position,
        axis=0,
        mode="clip",
    )
    bounds = [0, row_count - 2 * BLOCK, row_count]
    x_head, x_tail = x_own[: bounds[1], :], x_own[bounds[1] :, :]
    tail_near = gather_near(x_tail)
    head_near = gather_near(after(x_head, tail_near[0]))
    tail_far2 = gather_far((after(tail_near[0], g_rows), tail_near[1]), z)
    head_far2 = gather_far((after(head_near[0], tail_far2), head_near[1]), z)
    tail_end = gather_end(after(tail_far2, *head_near))
    tail_shards = shards(x_tail, tail_near, tail_far2, tail_end, z)

    bits = list(range(1, replicas.bit_length() - 1)) + [0]
    blocks = jnp.concatenate([w_q, w_k, w_v, w_o_t], axis=1)[None]
    waits = [(send_rows,), (arrived_rows,), (tail_far2, *head_near)]
    for t, bit in enumerate(bits):
        there = [(i, i ^ (1 << bit)) for i in range(replicas)]
        sent = after(blocks, *waits[min(t, 2)])
        blocks = jnp.concatenate([blocks, lax.ppermute(sent, "fsdp", there)], axis=0)
    apart = jnp.arange(replicas, dtype=jnp.int32) ^ me
    block_of = sum(((apart >> bit) & 1) << t for t, bit in enumerate(bits))
    weights = jnp.take(blocks, block_of, axis=0, mode="clip").reshape(feature_count, -1)
    w_qkv = weights[:, :qkv_cols]
    w_shards = w_qkv.reshape(4, local_features, qkv_cols)
    gain_f = gain.astype(f32)
    gain_shards = gain_f.reshape(4, 1, local_features)
    w_k_parts = [lax.dynamic_index_in_dim(w_shards, z ^ k, 0, keepdims=False) for k in range(4)]
    gain_k = [lax.dynamic_index_in_dim(gain_shards, z ^ k, 0, keepdims=False) for k in range(4)]

    def in_order(parts):
        whole = jnp.zeros((parts[0].shape[0], feature_count), bf16)
        for k in range(4):
            whole = lax.dynamic_update_slice_in_dim(whole, parts[k], (z ^ k) * local_features, 1)
        return whole

    ga = matmul(g_rows, weights[:, qkv_cols:])
    start = row_start[:, None]

    def product(k, x):
        raw = matmul((x.astype(f32) * gain_k[k]).astype(bf16), w_k_parts[k])
        return raw, jnp.sum(jnp.square(x.astype(f32)), axis=1, keepdims=True)

    def project(parts):
        raws, squares = zip(*[product(k, x) for k, x in enumerate(parts)])
        return sum(raws), sum(squares)

    def inverse_norm(squares):
        return lax.rsqrt(squares / feature_count + NORM_EPSILON)

    def backward(i, raw, inv, prev):
        here = slice(bounds[i], bounds[i + 1])
        return attention(
            here.start, row_count, feature_count, raw, inv, ga[here], adv, cos, sin, start, prev
        )

    def input_terms(dqkv, scales, x):
        terms = (
            scales[:, 0:1] * (times_trans(dqkv, w_qkv) * gain_f[None, :])
            - x.astype(f32) * scales[:, 1:2]
        ).astype(bf16)
        return [
            lax.dynamic_slice_in_dim(terms, (z ^ k) * local_features, local_features, 1)
            for k in range(4)
        ]

    raw1, squares1 = project(tail_shards)
    x_last = in_order(tail_shards)
    head_end = gather_end(after(head_far2, tail_end, ga, raw1))
    head_shards = shards(x_head, head_near, head_far2, head_end, z)
    raw0, squares0 = project(head_shards)
    x_first = in_order(head_shards)
    x_chunks = [x_first, x_last]
    inv0, inv1 = inverse_norm(squares0), inverse_norm(squares1)
    dqkv0, scaled0, scales0, out0, *carry = backward(0, raw0, inv0, ())
    final = dqkv0.shape[0]
    terms0 = input_terms(dqkv0, scales0, x_first[:final])
    end0 = scatter_end(terms0)
    step0 = scatter_far(terms0, end0)
    dx0 = scatter_near(terms0, step0, z)

    dqkv1, scaled1, scales1, out1 = backward(
        1, after(raw1, terms0[3]), inv1, (raw0, inv0, *carry)
    )
    weight_terms = weight_grads(
        x_chunks,
        g_rows,
        after(jnp.concatenate([scaled0, scaled1], axis=0), end0),
        jnp.concatenate([out0, out1], axis=0),
        gain_f.reshape(4, local_features),
    )
    summed = lax.psum_scatter(weight_terms, "fsdp", scatter_dimension=0, tiled=True)

    terms1 = input_terms(
        after(dqkv1, weight_terms), scales1, jnp.concatenate([x_first[final:], x_last], axis=0)
    )
    end1 = scatter_end([*terms1[:3], after(terms1[3], end0)])
    step1 = scatter_far(terms1, after(end1, *step0))
    dx1 = scatter_near(terms1, (after(step1[0], dx0), step1[1]), z)
    dx = jnp.concatenate([dx0, dx1], axis=0)
    input_grad = (adv * log_prob_grad.astype(f32) + dx).astype(bf16)
    grad_q = summed[:, :q_cols]
    grad_k = summed[:, q_cols : q_cols + k_cols]
    grad_v = summed[:, q_cols + k_cols : qkv_cols]
    grad_o_t = summed[:, qkv_cols:]
    return (input_grad, grad_q, grad_k, grad_v, grad_o_t)


def solution(mesh):
    in_specs = (
        P("fsdp", None, "tp"),
        P("fsdp"),
        P("fsdp", None),
        P("fsdp"),
        P("fsdp", "tp"),
        P(),
        P("fsdp", "tp"),
        P("fsdp", "tp"),
        P("fsdp", "tp"),
        P("fsdp", "tp"),
    )
    out_specs = (
        P("fsdp", "tp"),
        P("fsdp", "tp"),
        P("fsdp", "tp"),
        P("fsdp", "tp"),
        P("fsdp", "tp"),
    )
    return jax.shard_map(
        per_device, mesh=mesh, in_specs=in_specs, out_specs=out_specs, check_vma=False
    )
```

```python
import functools

import jax
import jax.numpy as jnp
from jax import lax
from jax.experimental import pallas as pl
from jax.experimental.pallas import tpu as pltpu
from jax.sharding import PartitionSpec as P

KEY_VALUE_HEADS = 4
HD = 128
QUERY_HEADS = 16
GSIZE = 16
ROPE_BASE = 1000000.0
NORM_EPSILON = 1e-06
BLOCK = 128

UP = [(0, 1), (1, 2), (2, 3)]
DOWN = [(1, 0), (2, 1), (3, 2)]
UP_MID = [(1, 2), (2, 3)]
DOWN_MID = [(1, 0), (2, 1)]
TO_ENDS = [(2, 3), (1, 0)]
FROM_ENDS = [(3, 2), (0, 1)]
UP_IN = [(0, 1), (1, 2)]
DOWN_IN = [(3, 2), (2, 1)]


def contract_rows(left, right):
    return lax.dot_general(
        left, right, (((0,), (0,)), ((), ())), preferred_element_type=jnp.float32
    )


def times_trans(left, right):
    return lax.dot_general(
        left, right, (((1,), (1,)), ((), ())), preferred_element_type=jnp.float32
    )


def matmul(left, right):
    return jnp.dot(left, right, preferred_element_type=jnp.float32)


def gather_near(own):
    return lax.ppermute(own, "tp", UP), lax.ppermute(own, "tp", DOWN)


def gather_far(step1, z):
    up2 = lax.ppermute(step1[0], "tp", UP_MID)
    down2 = lax.ppermute(step1[1], "tp", DOWN_MID)
    return jnp.where(z >= 2, up2, down2)


def gather_end(far2):
    return lax.ppermute(far2, "tp", TO_ENDS)


def shards(own, step1, far2, far3, z):
    up1, down1 = step1
    near = jnp.where(z % 2 == 1, up1, down1)
    other = jnp.where(z == 1, down1, jnp.where(z == 2, up1, far3))
    return [own, near, far2, other]


def after(value, *earlier):
    return lax.optimization_barrier((value, *earlier))[0]


def scatter_end(parts):
    return lax.ppermute(parts[3], "tp", FROM_ENDS)


def scatter_far(parts, from_end):
    total2 = (parts[2].astype(jnp.float32) + from_end.astype(jnp.float32)).astype(jnp.bfloat16)
    return lax.ppermute(total2, "tp", UP_IN), lax.ppermute(total2, "tp", DOWN_IN)


def scatter_near(parts, step2, z):
    own, near, _, other = parts
    f32 = jnp.float32
    up2, down2 = step2
    go_up = jnp.where(z == 1, other, near).astype(f32) + up2.astype(f32)
    go_down = jnp.where(z == 2, other, near).astype(f32) + down2.astype(f32)
    up3 = lax.ppermute(go_up.astype(jnp.bfloat16), "tp", UP)
    down3 = lax.ppermute(go_down.astype(jnp.bfloat16), "tp", DOWN)
    return own.astype(f32) + up3.astype(f32) + down3.astype(f32)


def attention_kernel(has_prev, is_last, first, feature_count, *refs):
    refs = list(refs)
    raw_ref, inv_ref, ga_ref, adv_ref, cos_ref, sin_ref, start_ref = refs[:7]
    refs = refs[7:]
    if has_prev:
        raw_prev, inv_prev, dq_prev, dk_prev, dv_prev = refs[:5]
        refs = refs[5:]
    dqkv_ref, dscaled_ref, mean_ref, out_ref = refs[:4]
    refs = refs[4:]
    if not is_last:
        dq_next, dk_next, dv_next = refs[:3]
        refs = refs[3:]
    qkv_b, dq_b, dk_acc, dv_acc = refs
    rows = raw_ref.shape[0]
    heads = ga_ref.shape[1] // HD
    qw = heads * HD
    scale = HD ** (-0.5)
    f32, bf16 = jnp.float32, jnp.bfloat16
    blocks = rows // BLOCK

    def span(block):
        return slice(block * BLOCK, (block + 1) * BLOCK)

    def turn(value, cos, sin):
        return value * cos + pltpu.roll(value, HD // 2, 1) * sin

    def whole(block):
        return slice(first + block * BLOCK, first + (block + 1) * BLOCK)

    def linear(block, cols):
        if block < 0:
            last = raw_prev.shape[0]
            return raw_prev[last - BLOCK : last, cols] * inv_prev[last - BLOCK : last, :]
        return raw_ref[span(block), cols] * inv_ref[span(block), :]

    def prepare(block, from_head):
        cos, sin = cos_ref[whole(block), :], sin_ref[whole(block), :]
        for h in range(from_head, heads + 1):
            cols = slice(h * HD, (h + 1) * HD)
            qkv_b[span(block + 1), cols] = turn(linear(block, cols), cos, sin).astype(bf16)
        cols = slice(qw + HD, qw + 2 * HD)
        qkv_b[span(block + 1), cols] = linear(block, cols).astype(bf16)

    if has_prev:
        prepare(-1, heads)
        dq_b[span(0), :] = dq_prev[...]
        dk_acc[span(0), :] = dk_prev[...]
        dv_acc[span(0), :] = dv_prev[...]
    else:
        qkv_b[span(0), :] = jnp.zeros((BLOCK, qkv_b.shape[1]), bf16)
        dk_acc[span(0), :] = jnp.zeros((BLOCK, HD), f32)
        dv_acc[span(0), :] = jnp.zeros((BLOCK, HD), f32)

    for block in range(blocks):
        prepare(block, 0)
        adv = adv_ref[whole(block), :]
        here, after = span(block), span(block + 1)
        both = slice(block * BLOCK, (block + 2) * BLOCK)
        qs = jnp.concatenate(
            [qkv_b[after, h * HD : (h + 1) * HD] for h in range(heads)], axis=0
        )
        gs = jnp.concatenate(
            [(ga_ref[here, h * HD : (h + 1) * HD] * adv).astype(bf16) for h in range(heads)], axis=0
        )
        ks = qkv_b[both, qw : qw + HD]
        vs = qkv_b[both, qw + HD : qw + 2 * HD]
        start = start_ref[whole(block), :] - (first + (block - 1) * BLOCK)
        col = lax.broadcasted_iota(jnp.int32, (BLOCK, 2 * BLOCK), 1)
        row = lax.broadcasted_iota(jnp.int32, (BLOCK, 2 * BLOCK), 0) + BLOCK
        bias = jnp.where((col >= start) & (col <= row), 0.0, -1e30)
        bias = jnp.concatenate([bias] * heads, axis=0)
        scores = times_trans(qs, ks) * scale + bias
        top = jnp.max(scores, axis=-1, keepdims=True)
        weight = jnp.exp(scores - top)
        prob = weight / jnp.sum(weight, axis=-1, keepdims=True)
        prob_b = prob.astype(bf16)
        out = matmul(prob_b, vs)
        grad_prob = times_trans(gs, vs)
        delta = jnp.sum(prob * grad_prob, axis=-1, keepdims=True)
        ds = (prob * (grad_prob - delta) * scale).astype(bf16)
        dq = matmul(ds, ks)
        dk_acc[span(block), :] += contract_rows(ds[:, :BLOCK], qs)
        dk_acc[after, :] = contract_rows(ds[:, BLOCK:], qs)
        dv_acc[span(block), :] += contract_rows(prob_b[:, :BLOCK], gs)
        dv_acc[after, :] = contract_rows(prob_b[:, BLOCK:], gs)
        cos, sin = cos_ref[whole(block), :], sin_ref[whole(block), :]
        for h in range(heads):
            cols = slice(h * HD, (h + 1) * HD)
            out_ref[here, cols] = (out[span(h), :].astype(bf16).astype(f32) * adv).astype(bf16)
            dq_b[after, cols] = turn(dq[span(h), :], cos, -sin).astype(bf16)

    begin = -1 if has_prev else 0
    end = blocks if is_last else blocks - 1
    for block in range(begin, end):
        to = span(block - begin)
        cos, sin = cos_ref[whole(block), :], sin_ref[whole(block), :]
        inv = inv_prev[inv_prev.shape[0] - BLOCK :, :] if block < 0 else inv_ref[span(block), :]
        total = jnp.zeros((BLOCK, 1), f32)
        for h in range(heads + 2):
            cols = slice(h * HD, (h + 1) * HD)
            if h < heads:
                grad = dq_b[span(block + 1), cols]
            elif h == heads:
                grad = turn(dk_acc[span(block + 1), :], cos, -sin).astype(bf16)
            else:
                grad = dv_acc[span(block + 1), :].astype(bf16)
            dqkv_ref[to, cols] = grad
            grad = grad.astype(f32)
            dscaled_ref[to, cols] = (grad * inv).astype(bf16)
            total += jnp.sum(grad * linear(block, cols), axis=-1, keepdims=True)
        mean_ref[to, 0:1] = inv
        mean_ref[to, 1:2] = inv * inv * total * (1.0 / feature_count)
    if not is_last:
        dq_next[...] = dq_b[span(blocks), :]
        dk_next[...] = dk_acc[span(blocks), :]
        dv_next[...] = dv_acc[span(blocks), :]


def attention(first, total, feature_count, raw, inv, ga, adv, cos, sin, start, prev):
    rows, width = raw.shape
    qw = ga.shape[1]
    is_last = first + rows == total
    final = rows + (BLOCK if prev else 0) - (0 if is_last else BLOCK)
    f32, bf16 = jnp.float32, jnp.bfloat16
    out_shape = [
        jax.ShapeDtypeStruct((final, width), bf16),
        jax.ShapeDtypeStruct((final, width), bf16),
        jax.ShapeDtypeStruct((final, 2), f32),
        jax.ShapeDtypeStruct((rows, qw), bf16),
    ]
    if not is_last:
        out_shape += [
            jax.ShapeDtypeStruct((BLOCK, qw), bf16),
            jax.ShapeDtypeStruct((BLOCK, HD), f32),
            jax.ShapeDtypeStruct((BLOCK, HD), f32),
        ]
    operands = [raw, inv, ga, adv, cos, sin, start] + list(prev)
    vmem = pl.BlockSpec(memory_space=pltpu.VMEM)
    return pl.pallas_call(
        functools.partial(attention_kernel, bool(prev), is_last, first, feature_count),
        out_shape=out_shape,
        in_specs=[vmem] * len(operands),
        out_specs=[vmem] * len(out_shape),
        scratch_shapes=[
            pltpu.VMEM((rows + BLOCK, width), bf16),
            pltpu.VMEM((rows + BLOCK, qw), bf16),
            pltpu.VMEM((rows + BLOCK, HD), f32),
            pltpu.VMEM((rows + BLOCK, HD), f32),
        ],
        compiler_params=pltpu.CompilerParams(vmem_limit_bytes=32 * 1024 * 1024),
        cost_estimate=pl.CostEstimate(
            flops=rows * 2 * BLOCK * HD * 12 * (qw // HD),
            bytes_accessed=rows * width * 8 + rows * qw * 6,
            transcendentals=rows * 2 * BLOCK * (qw // HD),
        ),
        name="attention",
    )(*operands)


def weight_grad_kernel(x_count, place_ref, *refs):
    x_refs = refs[: 4 * x_count]
    g_ref, scaled_ref, out_ref, gain_ref, term_ref = refs[4 * x_count :]
    width = scaled_ref.shape[1]
    term_ref[:, width:] = contract_rows(g_ref[...], out_ref[...]).astype(jnp.bfloat16)
    for k in range(4):

        @pl.when(place_ref[pl.program_id(0)] == k)
        def _():
            total, base = None, 0
            for ref in x_refs[k * x_count : (k + 1) * x_count]:
                part = contract_rows(ref[...], scaled_ref[base : base + ref.shape[0], :])
                base += ref.shape[0]
                total = part if total is None else total + part
            term_ref[:, :width] = (total * gain_ref[0]).astype(jnp.bfloat16)


def weight_grads(places, x_chunks, g_rows, scaled, out, gain):
    features = gain.shape[1]
    width = scaled.shape[1] + out.shape[1]
    x_parts = [chunk[k] for k in range(4) for chunk in x_chunks]

    def once(o):
        return pl.BlockSpec(o.shape, lambda j, place: (0, 0), pipeline_mode=pl.Buffered(1))

    return pl.pallas_call(
        functools.partial(weight_grad_kernel, len(x_chunks)),
        out_shape=jax.ShapeDtypeStruct((4 * features, width), jnp.bfloat16),
        grid_spec=pltpu.PrefetchScalarGridSpec(
            num_scalar_prefetch=1,
            grid=(4,),
            in_specs=[once(x) for x in x_parts]
            + [pl.BlockSpec((g_rows.shape[0], features), lambda j, place: (0, j))]
            + [once(scaled), once(out)]
            + [pl.BlockSpec((1, features, 1), lambda j, place: (j, 0, 0))],
            out_specs=pl.BlockSpec((features, width), lambda j, place: (j, 0)),
        ),
        compiler_params=pltpu.CompilerParams(vmem_limit_bytes=40 * 1024 * 1024),
        cost_estimate=pl.CostEstimate(
            flops=2 * scaled.shape[0] * 4 * features * width,
            bytes_accessed=4 * features * (4 * scaled.shape[0] + 2 * width),
            transcendentals=0,
        ),
        name="weight_grads",
    )(places, *x_parts, g_rows, scaled, out, gain[:, :, None])


def per_device(roll_rows, dest, lengths, clusters, log_prob_grad, gain, w_q, w_k, w_v, w_o_t):
    sequence_count = dest.shape[0]
    max_len, local_features = roll_rows.shape[1:]
    row_count = log_prob_grad.shape[0]
    replicas = lax.axis_size("fsdp")
    per_pair = sequence_count // replicas
    me = lax.axis_index("fsdp")
    z = lax.axis_index("tp")
    f32, bf16 = jnp.float32, jnp.bfloat16
    q_cols, k_cols = w_q.shape[1], w_k.shape[1]
    qkv_cols = q_cols + 2 * k_cols
    feature_count = gain.shape[0]

    g_rows = lax.all_gather(log_prob_grad, "tp", axis=1, tiled=True)

    slot_ids = jnp.arange(sequence_count, dtype=jnp.int32)
    earlier_dest = dest[None, :] < dest[:, None]
    send_block = jnp.sum(earlier_dest.astype(jnp.int32), axis=1)
    source = jnp.sum(
        jnp.where(send_block[None, :] == slot_ids[:, None], slot_ids[None, :], 0), axis=1
    )
    send_rows = jnp.take(roll_rows, source, axis=0, mode="clip")
    arrived_rows = lax.all_to_all(send_rows, "fsdp", split_axis=0, concat_axis=0, tiled=True)

    ballots = clusters.reshape(sequence_count // GSIZE, GSIZE)
    vote_share = jnp.mean((ballots[:, :, None] == ballots[:, None, :]).astype(f32), axis=2)
    advantage = (vote_share - jnp.mean(vote_share, axis=1, keepdims=True)).reshape(sequence_count)
    tags = jnp.stack([(dest % sequence_count).astype(f32), advantage], axis=1)
    picked = send_block[None, :] == slot_ids[:, None]
    tags = jnp.sum(jnp.where(picked[:, :, None], tags[None, :, :], 0.0), axis=1).astype(bf16)
    tags = lax.all_to_all(tags, "fsdp", split_axis=0, concat_axis=0, tiled=True).astype(f32)
    holder = tags[None, :, 0].astype(jnp.int32) == slot_ids[:, None]
    slot_of = jnp.sum(jnp.where(holder, slot_ids[None, :], 0), axis=1)
    seq_advantage = jnp.sum(jnp.where(holder, tags[None, :, 1], 0.0), axis=1)

    lengths_row = lengths.reshape(sequence_count)
    sequence_ends = jnp.cumsum(lengths_row)
    sequence_starts = sequence_ends - lengths_row
    row_index = jnp.arange(row_count, dtype=jnp.int32)
    one_hot = (sequence_ends[None, :] > row_index[:, None]) & (
        sequence_starts[None, :] <= row_index[:, None]
    )
    row_start = jnp.sum(jnp.where(one_hot, sequence_starts[None, :], 0), axis=1)
    position = row_index - row_start
    row_slot = jnp.sum(jnp.where(one_hot, slot_of[None, :], 0), axis=1)
    adv = jnp.sum(jnp.where(one_hot, seq_advantage[None, :], 0.0), axis=1)[:, None]
    half_width = HD // 2
    frequency = ROPE_BASE ** (-(2.0 * jnp.arange(half_width, dtype=f32)) / HD)
    angles = position.astype(f32)[:, None] * frequency[None, :]
    cos, sin = jnp.cos(angles), jnp.sin(angles)
    cos = jnp.concatenate([cos, cos], axis=1)
    sin = jnp.concatenate([-sin, sin], axis=1)

    x_own = jnp.take(
        arrived_rows.reshape(sequence_count * max_len, local_features),
        row_slot * max_len + position,
        axis=0,
        mode="clip",
    )
    bounds = [0, row_count - 2 * BLOCK, row_count]
    x_head, x_tail = x_own[: bounds[1], :], x_own[bounds[1] :, :]
    tail_near = gather_near(x_tail)
    head_near = gather_near(after(x_head, tail_near[0]))
    tail_far2 = gather_far((after(tail_near[0], g_rows), tail_near[1]), z)
    head_far2 = gather_far((after(head_near[0], tail_far2), head_near[1]), z)
    tail_end = gather_end(after(tail_far2, *head_near))
    tail_shards = shards(x_tail, tail_near, tail_far2, tail_end, z)

    w_qkv = lax.all_gather(
        jnp.concatenate([w_q, w_k, w_v], axis=1), "fsdp", axis=0, tiled=True
    )
    w_o = lax.all_gather(w_o_t, "fsdp", axis=0, tiled=True)
    gain_f = gain.astype(f32)
    w_shards = w_qkv.reshape(4, local_features, qkv_cols)
    gain_shards = gain_f.reshape(4, 1, local_features)
    w_k_parts = [lax.dynamic_index_in_dim(w_shards, z ^ k, 0, keepdims=False) for k in range(4)]
    gain_k = [lax.dynamic_index_in_dim(gain_shards, z ^ k, 0, keepdims=False) for k in range(4)]
    ga = matmul(g_rows, w_o)
    start = row_start[:, None]

    def product(k, x):
        raw = matmul((x.astype(f32) * gain_k[k]).astype(bf16), w_k_parts[k])
        return raw, jnp.sum(jnp.square(x.astype(f32)), axis=1, keepdims=True)

    def project(parts):
        raws, squares = zip(*[product(k, x) for k, x in enumerate(parts)])
        return sum(raws), sum(squares)

    def inverse_norm(squares):
        return lax.rsqrt(squares / feature_count + NORM_EPSILON)

    def backward(i, raw, inv, prev):
        here = slice(bounds[i], bounds[i + 1])
        return attention(
            here.start, row_count, feature_count, raw, inv, ga[here], adv, cos, sin, start, prev
        )

    def input_terms(dqkv, scales, parts):
        return [
            (
                scales[:, 0:1] * (times_trans(dqkv, w_k_parts[k]) * gain_k[k])
                - parts[k].astype(f32) * scales[:, 1:2]
            ).astype(bf16)
            for k in range(4)
        ]

    raw1, squares1 = project(tail_shards)
    head_end = gather_end(after(head_far2, tail_end, raw1))
    head_shards = shards(x_head, head_near, head_far2, head_end, z)
    raw0, squares0 = project(head_shards)
    x_chunks = [head_shards, tail_shards]
    inv0, inv1 = inverse_norm(squares0), inverse_norm(squares1)
    dqkv0, scaled0, scales0, out0, *carry = backward(0, raw0, inv0, ())
    final = dqkv0.shape[0]
    terms0 = input_terms(dqkv0, scales0, [x[:final] for x in head_shards])
    end0 = scatter_end(terms0)
    step0 = scatter_far(terms0, end0)
    dx0 = scatter_near(terms0, step0, z)

    dqkv1, scaled1, scales1, out1 = backward(
        1, after(raw1, terms0[3]), inv1, (raw0, inv0, *carry)
    )
    places = jnp.stack([z ^ j for j in range(4)]).astype(jnp.int32)
    weight_terms = weight_grads(
        places,
        x_chunks,
        g_rows,
        after(jnp.concatenate([scaled0, scaled1], axis=0), end0),
        jnp.concatenate([out0, out1], axis=0),
        gain_f.reshape(4, local_features),
    )
    summed = lax.psum_scatter(weight_terms, "fsdp", scatter_dimension=0, tiled=True)

    terms1 = input_terms(
        after(dqkv1, weight_terms),
        scales1,
        [jnp.concatenate([x[final:], y], axis=0) for x, y in zip(*x_chunks)],
    )
    end1 = scatter_end([*terms1[:3], after(terms1[3], end0)])
    step1 = scatter_far(terms1, after(end1, *step0))
    dx1 = scatter_near(terms1, (after(step1[0], dx0), step1[1]), z)
    dx = jnp.concatenate([dx0, dx1], axis=0)
    input_grad = (adv * log_prob_grad.astype(f32) + dx).astype(bf16)
    grad_q = summed[:, :q_cols]
    grad_k = summed[:, q_cols : q_cols + k_cols]
    grad_v = summed[:, q_cols + k_cols : qkv_cols]
    grad_o_t = summed[:, qkv_cols:]
    return (input_grad, grad_q, grad_k, grad_v, grad_o_t)


def solution(mesh):
    in_specs = (
        P("fsdp", None, "tp"),
        P("fsdp"),
        P("fsdp", None),
        P("fsdp"),
        P("fsdp", "tp"),
        P(),
        P("fsdp", "tp"),
        P("fsdp", "tp"),
        P("fsdp", "tp"),
        P("fsdp", "tp"),
    )
    out_specs = (
        P("fsdp", "tp"),
        P("fsdp", "tp"),
        P("fsdp", "tp"),
        P("fsdp", "tp"),
        P("fsdp", "tp"),
    )
    return jax.shard_map(
        per_device, mesh=mesh, in_specs=in_specs, out_specs=out_specs, check_vma=False
    )
```

```python
import functools

import jax
import jax.numpy as jnp
from jax import lax
from jax.experimental import pallas as pl
from jax.experimental.pallas import tpu as pltpu
from jax.sharding import PartitionSpec as P

KEY_VALUE_HEADS = 4
HD = 128
QUERY_HEADS = 16
GSIZE = 16
ROPE_BASE = 1000000.0
NORM_EPSILON = 1e-06
BLOCK = 128

UP = [(0, 1), (1, 2), (2, 3)]
DOWN = [(1, 0), (2, 1), (3, 2)]
UP_MID = [(1, 2), (2, 3)]
DOWN_MID = [(1, 0), (2, 1)]
TO_ENDS = [(2, 3), (1, 0)]
FROM_ENDS = [(3, 2), (0, 1)]
UP_IN = [(0, 1), (1, 2)]
DOWN_IN = [(3, 2), (2, 1)]


def contract_rows(left, right):
    return lax.dot_general(
        left, right, (((0,), (0,)), ((), ())), preferred_element_type=jnp.float32
    )


def times_trans(left, right):
    return lax.dot_general(
        left, right, (((1,), (1,)), ((), ())), preferred_element_type=jnp.float32
    )


def matmul(left, right):
    return jnp.dot(left, right, preferred_element_type=jnp.float32)


def gather_near(own):
    return lax.ppermute(own, "tp", UP), lax.ppermute(own, "tp", DOWN)


def gather_far(step1, z):
    up2 = lax.ppermute(step1[0], "tp", UP_MID)
    down2 = lax.ppermute(step1[1], "tp", DOWN_MID)
    return jnp.where(z >= 2, up2, down2)


def gather_end(far2):
    return lax.ppermute(far2, "tp", TO_ENDS)


def shards(own, step1, far2, far3, z):
    up1, down1 = step1
    near = jnp.where(z % 2 == 1, up1, down1)
    other = jnp.where(z == 1, down1, jnp.where(z == 2, up1, far3))
    return [own, near, far2, other]


def after(value, *earlier):
    return lax.optimization_barrier((value, *earlier))[0]


def scatter_end(parts):
    return lax.ppermute(parts[3], "tp", FROM_ENDS)


def scatter_far(parts, from_end):
    total2 = (parts[2].astype(jnp.float32) + from_end.astype(jnp.float32)).astype(jnp.bfloat16)
    return lax.ppermute(total2, "tp", UP_IN), lax.ppermute(total2, "tp", DOWN_IN)


def scatter_near(parts, step2, z):
    own, near, _, other = parts
    f32 = jnp.float32
    up2, down2 = step2
    go_up = jnp.where(z == 1, other, near).astype(f32) + up2.astype(f32)
    go_down = jnp.where(z == 2, other, near).astype(f32) + down2.astype(f32)
    up3 = lax.ppermute(go_up.astype(jnp.bfloat16), "tp", UP)
    down3 = lax.ppermute(go_down.astype(jnp.bfloat16), "tp", DOWN)
    return own.astype(f32) + up3.astype(f32) + down3.astype(f32)


def attention_kernel(has_prev, is_last, first, feature_count, *refs):
    refs = list(refs)
    raw_ref, inv_ref, ga_ref, adv_ref, cos_ref, sin_ref, start_ref = refs[:7]
    refs = refs[7:]
    if has_prev:
        lin_prev, inv_prev, dq_prev, dk_prev, dv_prev = refs[:5]
        refs = refs[5:]
    dqkv_ref, dscaled_ref, mean_ref, out_ref = refs[:4]
    refs = refs[4:]
    if not is_last:
        lin_next, inv_next, dq_next, dk_next, dv_next = refs[:5]
        refs = refs[5:]
    qkv_b, dq_b, dk_acc, dv_acc = refs
    rows = raw_ref.shape[0]
    heads = ga_ref.shape[1] // HD
    qw = heads * HD
    scale = HD ** (-0.5)
    f32, bf16 = jnp.float32, jnp.bfloat16
    blocks = rows // BLOCK

    def span(block):
        return slice(block * BLOCK, (block + 1) * BLOCK)

    def turn(value, cos, sin):
        return value * cos + pltpu.roll(value, HD // 2, 1) * sin

    def whole(block):
        return slice(first + block * BLOCK, first + (block + 1) * BLOCK)

    def linear(block, cols):
        if block < 0:
            return lin_prev[:, cols]
        return raw_ref[span(block), cols] * inv_ref[span(block), :]

    def prepare(block, from_head):
        cos, sin = cos_ref[whole(block), :], sin_ref[whole(block), :]
        for h in range(from_head, heads + 1):
            cols = slice(h * HD, (h + 1) * HD)
            qkv_b[span(block + 1), cols] = turn(linear(block, cols), cos, sin).astype(bf16)
        cols = slice(qw + HD, qw + 2 * HD)
        qkv_b[span(block + 1), cols] = linear(block, cols).astype(bf16)

    if has_prev:
        prepare(-1, heads)
        dq_b[span(0), :] = dq_prev[...]
        dk_acc[span(0), :] = dk_prev[...]
        dv_acc[span(0), :] = dv_prev[...]
    else:
        qkv_b[span(0), :] = jnp.zeros((BLOCK, qkv_b.shape[1]), bf16)
        dk_acc[span(0), :] = jnp.zeros((BLOCK, HD), f32)
        dv_acc[span(0), :] = jnp.zeros((BLOCK, HD), f32)

    for block in range(blocks):
        prepare(block, 0)
        adv = adv_ref[whole(block), :]
        here, after = span(block), span(block + 1)
        both = slice(block * BLOCK, (block + 2) * BLOCK)
        qs = jnp.concatenate(
            [qkv_b[after, h * HD : (h + 1) * HD] for h in range(heads)], axis=0
        )
        gs = jnp.concatenate(
            [(ga_ref[whole(block), h * HD : (h + 1) * HD] * adv).astype(bf16) for h in range(heads)], axis=0
        )
        ks = qkv_b[both, qw : qw + HD]
        vs = qkv_b[both, qw + HD : qw + 2 * HD]
        start = start_ref[whole(block), :] - (first + (block - 1) * BLOCK)
        col = lax.broadcasted_iota(jnp.int32, (BLOCK, 2 * BLOCK), 1)
        row = lax.broadcasted_iota(jnp.int32, (BLOCK, 2 * BLOCK), 0) + BLOCK
        bias = jnp.where((col >= start) & (col <= row), 0.0, -1e30)
        bias = jnp.concatenate([bias] * heads, axis=0)
        scores = times_trans(qs, ks) * scale + bias
        top = jnp.max(scores, axis=-1, keepdims=True)
        weight = jnp.exp(scores - top)
        prob = weight / jnp.sum(weight, axis=-1, keepdims=True)
        prob_b = prob.astype(bf16)
        out = matmul(prob_b, vs)
        grad_prob = times_trans(gs, vs)
        delta = jnp.sum(prob * grad_prob, axis=-1, keepdims=True)
        ds = (prob * (grad_prob - delta) * scale).astype(bf16)
        dq = matmul(ds, ks)
        dk_acc[span(block), :] += contract_rows(ds[:, :BLOCK], qs)
        dk_acc[after, :] = contract_rows(ds[:, BLOCK:], qs)
        dv_acc[span(block), :] += contract_rows(prob_b[:, :BLOCK], gs)
        dv_acc[after, :] = contract_rows(prob_b[:, BLOCK:], gs)
        cos, sin = cos_ref[whole(block), :], sin_ref[whole(block), :]
        for h in range(heads):
            cols = slice(h * HD, (h + 1) * HD)
            out_ref[here, cols] = (out[span(h), :].astype(bf16).astype(f32) * adv).astype(bf16)
            dq_b[after, cols] = turn(dq[span(h), :], cos, -sin).astype(bf16)

    begin = -1 if has_prev else 0
    end = blocks if is_last else blocks - 1
    for block in range(begin, end):
        to = span(block - begin)
        cos, sin = cos_ref[whole(block), :], sin_ref[whole(block), :]
        inv = inv_prev[...] if block < 0 else inv_ref[span(block), :]
        total = jnp.zeros((BLOCK, 1), f32)
        for h in range(heads + 2):
            cols = slice(h * HD, (h + 1) * HD)
            if h < heads:
                grad = dq_b[span(block + 1), cols]
            elif h == heads:
                grad = turn(dk_acc[span(block + 1), :], cos, -sin).astype(bf16)
            else:
                grad = dv_acc[span(block + 1), :].astype(bf16)
            dqkv_ref[to, cols] = grad
            grad = grad.astype(f32)
            dscaled_ref[to, cols] = (grad * inv).astype(bf16)
            total += jnp.sum(grad * linear(block, cols), axis=-1, keepdims=True)
        mean_ref[to, 0:1] = inv
        mean_ref[to, 1:2] = inv * inv * total * (1.0 / feature_count)
    if not is_last:
        inv_next[...] = inv_ref[span(blocks - 1), :]
        lin_next[...] = raw_ref[span(blocks - 1), :] * inv_next[...]
        dq_next[...] = dq_b[span(blocks), :]
        dk_next[...] = dk_acc[span(blocks), :]
        dv_next[...] = dv_acc[span(blocks), :]


def attention(first, total, feature_count, raw, inv, ga, adv, cos, sin, start, prev):
    rows, width = raw.shape
    qw = ga.shape[1]
    is_last = first + rows == total
    final = rows + (BLOCK if prev else 0) - (0 if is_last else BLOCK)
    f32, bf16 = jnp.float32, jnp.bfloat16
    out_shape = [
        jax.ShapeDtypeStruct((final, width), bf16),
        jax.ShapeDtypeStruct((final, width), bf16),
        jax.ShapeDtypeStruct((final, 2), f32),
        jax.ShapeDtypeStruct((rows, qw), bf16),
    ]
    if not is_last:
        out_shape += [
            jax.ShapeDtypeStruct((BLOCK, width), f32),
            jax.ShapeDtypeStruct((BLOCK, 1), f32),
            jax.ShapeDtypeStruct((BLOCK, qw), bf16),
            jax.ShapeDtypeStruct((BLOCK, HD), f32),
            jax.ShapeDtypeStruct((BLOCK, HD), f32),
        ]
    operands = [raw, inv, ga, adv, cos, sin, start] + list(prev)
    vmem = pl.BlockSpec(memory_space=pltpu.VMEM)
    return pl.pallas_call(
        functools.partial(attention_kernel, bool(prev), is_last, first, feature_count),
        out_shape=out_shape,
        in_specs=[vmem] * len(operands),
        out_specs=[vmem] * len(out_shape),
        scratch_shapes=[
            pltpu.VMEM((rows + BLOCK, width), bf16),
            pltpu.VMEM((rows + BLOCK, qw), bf16),
            pltpu.VMEM((rows + BLOCK, HD), f32),
            pltpu.VMEM((rows + BLOCK, HD), f32),
        ],
        compiler_params=pltpu.CompilerParams(vmem_limit_bytes=32 * 1024 * 1024),
        cost_estimate=pl.CostEstimate(
            flops=rows * 2 * BLOCK * HD * 12 * (qw // HD),
            bytes_accessed=rows * width * 8 + rows * qw * 6,
            transcendentals=rows * 2 * BLOCK * (qw // HD),
        ),
        name="attention",
    )(*operands)


def project_kernel(count, feature_count, *refs):
    x_refs, w_refs = refs[:count], refs[count : 2 * count]
    raw_ref, square_ref = refs[-2:]
    raw, squares = None, None
    if len(refs) > 2 * count + 2:
        raw, squares = refs[2 * count][...], refs[2 * count + 1][...]
    for x_ref, w_ref in zip(x_refs, w_refs):
        part = matmul(x_ref[...], w_ref[...])
        raw = part if raw is None else raw + part
        wide = x_ref[...].astype(jnp.float32)
        part = jnp.sum(wide * wide, axis=1, keepdims=True)
        squares = part if squares is None else squares + part
    raw_ref[...] = raw
    if feature_count:
        squares = lax.rsqrt(squares / feature_count + NORM_EPSILON)
    square_ref[...] = squares


def project(parts, weights, prior, feature_count):
    rows, width = parts[0].shape[0], weights[0].shape[1]
    operands = [*parts, *weights, *prior]
    vmem = pl.BlockSpec(memory_space=pltpu.VMEM)
    return pl.pallas_call(
        functools.partial(project_kernel, len(parts), feature_count),
        out_shape=[
            jax.ShapeDtypeStruct((rows, width), jnp.float32),
            jax.ShapeDtypeStruct((rows, 1), jnp.float32),
        ],
        in_specs=[vmem] * len(operands),
        out_specs=[vmem] * 2,
        compiler_params=pltpu.CompilerParams(vmem_limit_bytes=32 * 1024 * 1024),
        cost_estimate=pl.CostEstimate(
            flops=2 * len(parts) * rows * width * parts[0].shape[1],
            bytes_accessed=2 * len(parts) * parts[0].shape[1] * (rows + width) + 8 * rows * width,
            transcendentals=rows,
        ),
        name="project",
    )(*operands)


def weight_grad_kernel(x_count, place_ref, *refs):
    x_refs = refs[: 4 * x_count]
    g_ref, scaled_ref, out_ref, gain_ref, term_ref = refs[4 * x_count :]
    width = scaled_ref.shape[1]
    gain = gain_ref[0]
    gain = jnp.transpose(jnp.broadcast_to(gain, (HD, gain.shape[1])))[:, 0:1]
    term_ref[:, width:] = contract_rows(g_ref[...], out_ref[...]).astype(jnp.bfloat16)
    for k in range(4):

        @pl.when(place_ref[pl.program_id(0)] == k)
        def _():
            total, base = None, 0
            for ref in x_refs[k * x_count : (k + 1) * x_count]:
                part = contract_rows(ref[...], scaled_ref[base : base + ref.shape[0], :])
                base += ref.shape[0]
                total = part if total is None else total + part
            term_ref[:, :width] = (total * gain).astype(jnp.bfloat16)


def weight_grads(places, x_chunks, g_rows, scaled, out, gain):
    features = gain.shape[2]
    width = scaled.shape[1] + out.shape[1]
    x_parts = [chunk[k] for k in range(4) for chunk in x_chunks]

    def once(o):
        return pl.BlockSpec(o.shape, lambda j, place: (0, 0), pipeline_mode=pl.Buffered(1))

    return pl.pallas_call(
        functools.partial(weight_grad_kernel, len(x_chunks)),
        out_shape=jax.ShapeDtypeStruct((4 * features, width), jnp.bfloat16),
        grid_spec=pltpu.PrefetchScalarGridSpec(
            num_scalar_prefetch=1,
            grid=(4,),
            in_specs=[once(x) for x in x_parts]
            + [pl.BlockSpec((g_rows.shape[0], features), lambda j, place: (0, j))]
            + [once(scaled), once(out)]
            + [pl.BlockSpec((1, 1, features), lambda j, place: (j, 0, 0))],
            out_specs=pl.BlockSpec((features, width), lambda j, place: (j, 0)),
        ),
        compiler_params=pltpu.CompilerParams(vmem_limit_bytes=40 * 1024 * 1024),
        cost_estimate=pl.CostEstimate(
            flops=2 * scaled.shape[0] * 4 * features * width,
            bytes_accessed=4 * features * (4 * scaled.shape[0] + 2 * width),
            transcendentals=0,
        ),
        name="weight_grads",
    )(places, *x_parts, g_rows, scaled, out, gain)


def per_device(roll_rows, dest, lengths, clusters, log_prob_grad, gain, w_q, w_k, w_v, w_o_t):
    sequence_count = dest.shape[0]
    max_len, local_features = roll_rows.shape[1:]
    row_count = log_prob_grad.shape[0]
    replicas = lax.axis_size("fsdp")
    per_pair = sequence_count // replicas
    me = lax.axis_index("fsdp")
    z = lax.axis_index("tp")
    f32, bf16 = jnp.float32, jnp.bfloat16
    q_cols, k_cols = w_q.shape[1], w_k.shape[1]
    qkv_cols = q_cols + 2 * k_cols
    feature_count = gain.shape[0]

    g_rows = lax.all_gather(log_prob_grad, "tp", axis=1, tiled=True)

    slot_ids = jnp.arange(sequence_count, dtype=jnp.int32)
    earlier_dest = dest[None, :] < dest[:, None]
    send_block = jnp.sum(earlier_dest.astype(jnp.int32), axis=1)
    source = jnp.sum(
        jnp.where(send_block[None, :] == slot_ids[:, None], slot_ids[None, :], 0), axis=1
    )
    send_rows = jnp.take(roll_rows, source, axis=0, mode="clip")
    arrived_rows = lax.all_to_all(send_rows, "fsdp", split_axis=0, concat_axis=0, tiled=True)

    ballots = clusters.reshape(sequence_count // GSIZE, GSIZE)
    vote_share = jnp.mean((ballots[:, :, None] == ballots[:, None, :]).astype(f32), axis=2)
    advantage = (vote_share - jnp.mean(vote_share, axis=1, keepdims=True)).reshape(sequence_count)
    tags = jnp.stack([(dest % sequence_count).astype(f32), advantage], axis=1)
    picked = send_block[None, :] == slot_ids[:, None]
    tags = jnp.sum(jnp.where(picked[:, :, None], tags[None, :, :], 0.0), axis=1).astype(bf16)
    tags = lax.all_to_all(tags, "fsdp", split_axis=0, concat_axis=0, tiled=True).astype(f32)
    holder = tags[None, :, 0].astype(jnp.int32) == slot_ids[:, None]
    slot_of = jnp.sum(jnp.where(holder, slot_ids[None, :], 0), axis=1)
    seq_advantage = jnp.sum(jnp.where(holder, tags[None, :, 1], 0.0), axis=1)

    lengths_row = lengths.reshape(sequence_count)
    sequence_ends = jnp.cumsum(lengths_row)
    sequence_starts = sequence_ends - lengths_row
    row_index = jnp.arange(row_count, dtype=jnp.int32)
    one_hot = (sequence_ends[None, :] > row_index[:, None]) & (
        sequence_starts[None, :] <= row_index[:, None]
    )
    row_start = jnp.sum(jnp.where(one_hot, sequence_starts[None, :], 0), axis=1)
    position = row_index - row_start
    row_slot = jnp.sum(jnp.where(one_hot, slot_of[None, :], 0), axis=1)
    adv = jnp.sum(jnp.where(one_hot, seq_advantage[None, :], 0.0), axis=1)[:, None]
    half_width = HD // 2
    frequency = ROPE_BASE ** (-(2.0 * jnp.arange(half_width, dtype=f32)) / HD)
    angles = position.astype(f32)[:, None] * frequency[None, :]
    cos, sin = jnp.cos(angles), jnp.sin(angles)
    cos = jnp.concatenate([cos, cos], axis=1)
    sin = jnp.concatenate([-sin, sin], axis=1)

    start = row_start[:, None]
    arrived_rows = after(arrived_rows, cos, sin, start, adv)
    x_own = jnp.take(
        arrived_rows.reshape(sequence_count * max_len, local_features),
        row_slot * max_len + position,
        axis=0,
        mode="clip",
    )
    bounds = [0, row_count - 2 * BLOCK, row_count]
    x_head, x_tail = x_own[: bounds[1], :], x_own[bounds[1] :, :]
    tail_near = gather_near(x_tail)
    head_near = gather_near(after(x_head, tail_near[0]))
    tail_far2 = gather_far((after(tail_near[0], g_rows), tail_near[1]), z)
    head_far2 = gather_far((after(head_near[0], tail_far2), head_near[1]), z)
    tail_end = gather_end(after(tail_far2, *head_near))
    tail_shards = shards(x_tail, tail_near, tail_far2, tail_end, z)

    w_qkv = lax.all_gather(
        jnp.concatenate([w_q, w_k, w_v], axis=1), "fsdp", axis=0, tiled=True
    )
    w_o = lax.all_gather(w_o_t, "fsdp", axis=0, tiled=True)
    gain_f = gain.astype(f32)
    gain_shards = gain_f.reshape(4, 1, local_features)
    w_shards = (w_qkv.astype(f32) * gain_f[:, None]).astype(bf16)
    w_shards = w_shards.reshape(4, local_features, qkv_cols)
    w_k_parts = [lax.dynamic_index_in_dim(w_shards, z ^ k, 0, keepdims=False) for k in range(4)]

    def backward(i, raw, inv, prev):
        return attention(
            bounds[i], row_count, feature_count, raw, inv, ga, adv, cos, sin, start, prev
        )

    def input_terms(dqkv, scales, parts):
        return [
            (
                scales[:, 0:1] * times_trans(dqkv, w_k_parts[k])
                - parts[k].astype(f32) * scales[:, 1:2]
            ).astype(bf16)
            for k in range(4)
        ]

    raw1, inv1 = project(tail_shards, w_k_parts, (), feature_count)
    head_near_shard = jnp.where(z % 2 == 1, head_near[0], head_near[1])
    early = project([x_head, head_near_shard, head_far2], w_k_parts[:3], (), 0)
    head_end = gather_end(after(head_far2, tail_end, raw1, early[0]))
    head_shards = shards(x_head, head_near, head_far2, head_end, z)
    x_chunks = [head_shards, tail_shards]
    ga = matmul(g_rows, after(w_o, early[0]))
    raw0, inv0 = project(head_shards[3:], w_k_parts[3:], early, feature_count)
    dqkv0, scaled0, scales0, out0, *carry = backward(0, raw0, inv0, ())
    final = dqkv0.shape[0]
    terms0 = input_terms(dqkv0, scales0, [x[:final] for x in head_shards])
    end0 = scatter_end(terms0)
    step0 = scatter_far(terms0, end0)
    dx0 = scatter_near(terms0, step0, z)

    dqkv1, scaled1, scales1, out1 = backward(
        1, after(raw1, terms0[3]), inv1, carry
    )
    places = jnp.stack([z ^ j for j in range(4)]).astype(jnp.int32)
    weight_terms = weight_grads(
        places,
        x_chunks,
        g_rows,
        after(jnp.concatenate([scaled0, scaled1], axis=0), end0),
        jnp.concatenate([out0, out1], axis=0),
        gain_shards,
    )
    summed = lax.psum_scatter(weight_terms, "fsdp", scatter_dimension=0, tiled=True)

    terms1 = input_terms(
        after(dqkv1, weight_terms),
        scales1,
        [jnp.concatenate([x[final:], y], axis=0) for x, y in zip(*x_chunks)],
    )
    end1 = scatter_end([*terms1[:3], after(terms1[3], end0)])
    step1 = scatter_far(terms1, after(end1, *step0))
    dx1 = scatter_near(terms1, (after(step1[0], dx0), step1[1]), z)
    dx = jnp.concatenate([dx0, dx1], axis=0)
    input_grad = (adv * log_prob_grad.astype(f32) + dx).astype(bf16)
    grad_q = summed[:, :q_cols]
    grad_k = summed[:, q_cols : q_cols + k_cols]
    grad_v = summed[:, q_cols + k_cols : qkv_cols]
    grad_o_t = summed[:, qkv_cols:]
    return (input_grad, grad_q, grad_k, grad_v, grad_o_t)


def solution(mesh):
    in_specs = (
        P("fsdp", None, "tp"),
        P("fsdp"),
        P("fsdp", None),
        P("fsdp"),
        P("fsdp", "tp"),
        P(),
        P("fsdp", "tp"),
        P("fsdp", "tp"),
        P("fsdp", "tp"),
        P("fsdp", "tp"),
    )
    out_specs = (
        P("fsdp", "tp"),
        P("fsdp", "tp"),
        P("fsdp", "tp"),
        P("fsdp", "tp"),
        P("fsdp", "tp"),
    )
    return jax.shard_map(
        per_device, mesh=mesh, in_specs=in_specs, out_specs=out_specs, check_vma=False
    )
```

```python
import functools

import jax
import jax.numpy as jnp
from jax import lax
from jax.experimental import pallas as pl
from jax.experimental.pallas import tpu as pltpu
from jax.sharding import PartitionSpec as P

KEY_VALUE_HEADS = 4
HD = 128
QUERY_HEADS = 16
GSIZE = 16
ROPE_BASE = 1000000.0
NORM_EPSILON = 1e-06
BLOCK = 128

UP = [(0, 1), (1, 2), (2, 3)]
DOWN = [(1, 0), (2, 1), (3, 2)]
UP_MID = [(1, 2), (2, 3)]
DOWN_MID = [(1, 0), (2, 1)]
TO_ENDS = [(2, 3), (1, 0)]
FROM_ENDS = [(3, 2), (0, 1)]
UP_IN = [(0, 1), (1, 2)]
DOWN_IN = [(3, 2), (2, 1)]


def contract_rows(left, right):
    return lax.dot_general(
        left, right, (((0,), (0,)), ((), ())), preferred_element_type=jnp.float32
    )


def times_trans(left, right):
    return lax.dot_general(
        left, right, (((1,), (1,)), ((), ())), preferred_element_type=jnp.float32
    )


def matmul(left, right):
    return jnp.dot(left, right, preferred_element_type=jnp.float32)


def gather_near(own):
    return lax.ppermute(own, "tp", UP), lax.ppermute(own, "tp", DOWN)


def gather_far(step1, z):
    up2 = lax.ppermute(step1[0], "tp", UP_MID)
    down2 = lax.ppermute(step1[1], "tp", DOWN_MID)
    return jnp.where(z >= 2, up2, down2)


def gather_end(far2):
    return lax.ppermute(far2, "tp", TO_ENDS)


def shards(own, step1, far2, far3, z):
    up1, down1 = step1
    near = jnp.where(z % 2 == 1, up1, down1)
    other = jnp.where(z == 1, down1, jnp.where(z == 2, up1, far3))
    return [own, near, far2, other]


def after(value, *earlier):
    return lax.optimization_barrier((value, *earlier))[0]


def scatter_end(parts):
    return lax.ppermute(parts[3], "tp", FROM_ENDS)


def far_total(parts, from_end):
    return (parts[2].astype(jnp.float32) + from_end.astype(jnp.float32)).astype(jnp.bfloat16)


def scatter_far(total2):
    return lax.ppermute(total2, "tp", UP_IN), lax.ppermute(total2, "tp", DOWN_IN)


def scatter_near(parts, step2, z):
    own, near, _, other = parts
    f32 = jnp.float32
    up2, down2 = step2
    go_up = jnp.where(z == 1, other, near).astype(f32) + up2.astype(f32)
    go_down = jnp.where(z == 2, other, near).astype(f32) + down2.astype(f32)
    up3 = lax.ppermute(go_up.astype(jnp.bfloat16), "tp", UP)
    down3 = lax.ppermute(go_down.astype(jnp.bfloat16), "tp", DOWN)
    return own.astype(f32) + up3.astype(f32) + down3.astype(f32)


def attention_kernel(has_prev, is_last, first, feature_count, *refs):
    refs = list(refs)
    raw_ref, inv_ref, ga_ref, adv_ref, cos_ref, sin_ref, start_ref = refs[:7]
    refs = refs[7:]
    if has_prev:
        lin_prev, inv_prev, dq_prev, dk_prev, dv_prev = refs[:5]
        refs = refs[5:]
    dqkv_ref, dscaled_ref, mean_ref, out_ref = refs[:4]
    refs = refs[4:]
    if not is_last:
        lin_next, inv_next, dq_next, dk_next, dv_next = refs[:5]
        refs = refs[5:]
    qkv_b, dq_b, dk_acc, dv_acc = refs
    rows = raw_ref.shape[0]
    heads = ga_ref.shape[1] // HD
    qw = heads * HD
    scale = HD ** (-0.5)
    f32, bf16 = jnp.float32, jnp.bfloat16
    blocks = rows // BLOCK

    def span(block):
        return slice(block * BLOCK, (block + 1) * BLOCK)

    def turn(value, cos, sin):
        return value * cos + pltpu.roll(value, HD // 2, 1) * sin

    def whole(block):
        return slice(first + block * BLOCK, first + (block + 1) * BLOCK)

    def linear(block, cols):
        if block < 0:
            return lin_prev[:, cols]
        return raw_ref[span(block), cols] * inv_ref[span(block), :]

    def prepare(block, from_head):
        cos, sin = cos_ref[whole(block), :], sin_ref[whole(block), :]
        for h in range(from_head, heads + 1):
            cols = slice(h * HD, (h + 1) * HD)
            qkv_b[span(block + 1), cols] = turn(linear(block, cols), cos, sin).astype(bf16)
        cols = slice(qw + HD, qw + 2 * HD)
        qkv_b[span(block + 1), cols] = linear(block, cols).astype(bf16)

    if has_prev:
        prepare(-1, heads)
        dq_b[span(0), :] = dq_prev[...]
        dk_acc[span(0), :] = dk_prev[...]
        dv_acc[span(0), :] = dv_prev[...]
    else:
        qkv_b[span(0), :] = jnp.zeros((BLOCK, qkv_b.shape[1]), bf16)
        dk_acc[span(0), :] = jnp.zeros((BLOCK, HD), f32)
        dv_acc[span(0), :] = jnp.zeros((BLOCK, HD), f32)

    for block in range(blocks):
        prepare(block, 0)
        adv = adv_ref[whole(block), :]
        here, after = span(block), span(block + 1)
        both = slice(block * BLOCK, (block + 2) * BLOCK)
        qs = jnp.concatenate(
            [qkv_b[after, h * HD : (h + 1) * HD] for h in range(heads)], axis=0
        )
        gs = jnp.concatenate(
            [(ga_ref[here, h * HD : (h + 1) * HD] * adv).astype(bf16) for h in range(heads)], axis=0
        )
        ks = qkv_b[both, qw : qw + HD]
        vs = qkv_b[both, qw + HD : qw + 2 * HD]
        start = start_ref[whole(block), :] - (first + (block - 1) * BLOCK)
        col = lax.broadcasted_iota(jnp.int32, (BLOCK, 2 * BLOCK), 1)
        row = lax.broadcasted_iota(jnp.int32, (BLOCK, 2 * BLOCK), 0) + BLOCK
        bias = jnp.where((col >= start) & (col <= row), 0.0, -1e30)
        bias = jnp.concatenate([bias] * heads, axis=0)
        scores = times_trans(qs, ks) * scale + bias
        top = jnp.max(scores, axis=-1, keepdims=True)
        weight = jnp.exp(scores - top)
        prob = weight / jnp.sum(weight, axis=-1, keepdims=True)
        prob_b = prob.astype(bf16)
        out = matmul(prob_b, vs)
        grad_prob = times_trans(gs, vs)
        delta = jnp.sum(prob * grad_prob, axis=-1, keepdims=True)
        ds = (prob * (grad_prob - delta) * scale).astype(bf16)
        dq = matmul(ds, ks)
        dk_acc[span(block), :] += contract_rows(ds[:, :BLOCK], qs)
        dk_acc[after, :] = contract_rows(ds[:, BLOCK:], qs)
        dv_acc[span(block), :] += contract_rows(prob_b[:, :BLOCK], gs)
        dv_acc[after, :] = contract_rows(prob_b[:, BLOCK:], gs)
        cos, sin = cos_ref[whole(block), :], sin_ref[whole(block), :]
        for h in range(heads):
            cols = slice(h * HD, (h + 1) * HD)
            out_ref[here, cols] = (out[span(h), :].astype(bf16).astype(f32) * adv).astype(bf16)
            dq_b[after, cols] = turn(dq[span(h), :], cos, -sin).astype(bf16)

    begin = -1 if has_prev else 0
    end = blocks if is_last else blocks - 1
    for block in range(begin, end):
        to = span(block - begin)
        cos, sin = cos_ref[whole(block), :], sin_ref[whole(block), :]
        inv = inv_prev[...] if block < 0 else inv_ref[span(block), :]
        total = jnp.zeros((BLOCK, 1), f32)
        for h in range(heads + 2):
            cols = slice(h * HD, (h + 1) * HD)
            if h < heads:
                grad = dq_b[span(block + 1), cols]
            elif h == heads:
                grad = turn(dk_acc[span(block + 1), :], cos, -sin).astype(bf16)
            else:
                grad = dv_acc[span(block + 1), :].astype(bf16)
            dqkv_ref[to, cols] = grad
            grad = grad.astype(f32)
            dscaled_ref[to, cols] = (grad * inv).astype(bf16)
            total += jnp.sum(grad * linear(block, cols), axis=-1, keepdims=True)
        mean_ref[to, 0:1] = inv
        mean_ref[to, 1:2] = inv * inv * total * (1.0 / feature_count)
    if not is_last:
        inv_next[...] = inv_ref[span(blocks - 1), :]
        lin_next[...] = raw_ref[span(blocks - 1), :] * inv_next[...]
        dq_next[...] = dq_b[span(blocks), :]
        dk_next[...] = dk_acc[span(blocks), :]
        dv_next[...] = dv_acc[span(blocks), :]


def attention(first, total, feature_count, raw, inv, ga, adv, cos, sin, start, prev):
    rows, width = raw.shape
    qw = ga.shape[1]
    is_last = first + rows == total
    final = rows + (BLOCK if prev else 0) - (0 if is_last else BLOCK)
    f32, bf16 = jnp.float32, jnp.bfloat16
    out_shape = [
        jax.ShapeDtypeStruct((final, width), bf16),
        jax.ShapeDtypeStruct((final, width), bf16),
        jax.ShapeDtypeStruct((final, 2), f32),
        jax.ShapeDtypeStruct((rows, qw), bf16),
    ]
    if not is_last:
        out_shape += [
            jax.ShapeDtypeStruct((BLOCK, width), f32),
            jax.ShapeDtypeStruct((BLOCK, 1), f32),
            jax.ShapeDtypeStruct((BLOCK, qw), bf16),
            jax.ShapeDtypeStruct((BLOCK, HD), f32),
            jax.ShapeDtypeStruct((BLOCK, HD), f32),
        ]
    operands = [raw, inv, ga, adv, cos, sin, start] + list(prev)
    vmem = pl.BlockSpec(memory_space=pltpu.VMEM)
    return pl.pallas_call(
        functools.partial(attention_kernel, bool(prev), is_last, first, feature_count),
        out_shape=out_shape,
        in_specs=[vmem] * len(operands),
        out_specs=[vmem] * len(out_shape),
        scratch_shapes=[
            pltpu.VMEM((rows + BLOCK, width), bf16),
            pltpu.VMEM((rows + BLOCK, qw), bf16),
            pltpu.VMEM((rows + BLOCK, HD), f32),
            pltpu.VMEM((rows + BLOCK, HD), f32),
        ],
        compiler_params=pltpu.CompilerParams(vmem_limit_bytes=32 * 1024 * 1024),
        cost_estimate=pl.CostEstimate(
            flops=rows * 2 * BLOCK * HD * 12 * (qw // HD),
            bytes_accessed=rows * width * 8 + rows * qw * 6,
            transcendentals=rows * 2 * BLOCK * (qw // HD),
        ),
        name="attention",
    )(*operands)


def project_kernel(count, feature_count, *refs):
    x_refs, w_refs = refs[:count], refs[count : 2 * count]
    raw_ref, square_ref = refs[-2:]
    raw, squares = None, None
    if len(refs) > 2 * count + 2:
        raw, squares = refs[2 * count][...], refs[2 * count + 1][...]
    for x_ref, w_ref in zip(x_refs, w_refs):
        part = matmul(x_ref[...], w_ref[...])
        raw = part if raw is None else raw + part
        wide = x_ref[...].astype(jnp.float32)
        part = jnp.sum(wide * wide, axis=1, keepdims=True)
        squares = part if squares is None else squares + part
    raw_ref[...] = raw
    if feature_count:
        squares = lax.rsqrt(squares / feature_count + NORM_EPSILON)
    square_ref[...] = squares


def project(parts, weights, prior, feature_count):
    rows, width = parts[0].shape[0], weights[0].shape[1]
    operands = [*parts, *weights, *prior]
    vmem = pl.BlockSpec(memory_space=pltpu.VMEM)
    return pl.pallas_call(
        functools.partial(project_kernel, len(parts), feature_count),
        out_shape=[
            jax.ShapeDtypeStruct((rows, width), jnp.float32),
            jax.ShapeDtypeStruct((rows, 1), jnp.float32),
        ],
        in_specs=[vmem] * len(operands),
        out_specs=[vmem] * 2,
        compiler_params=pltpu.CompilerParams(vmem_limit_bytes=32 * 1024 * 1024),
        cost_estimate=pl.CostEstimate(
            flops=2 * len(parts) * rows * width * parts[0].shape[1],
            bytes_accessed=2 * len(parts) * parts[0].shape[1] * (rows + width) + 8 * rows * width,
            transcendentals=rows,
        ),
        name="project",
    )(*operands)


def weight_grad_kernel(place_ref, *refs):
    heads, tails, g_tails = refs[:4], refs[4:8], refs[8:12]
    g_ref, scaled_ref, out_ref, gain_ref, term_ref = refs[12:]
    width = scaled_ref.shape[1]
    gain = gain_ref[0]
    gain = jnp.transpose(jnp.broadcast_to(gain, (HD, gain.shape[1])))[:, 0:1]
    first = g_ref.shape[0]
    for k in range(4):

        @pl.when(place_ref[pl.program_id(0)] == k)
        def _():
            total = contract_rows(heads[k][...], scaled_ref[:first, :])
            total += contract_rows(tails[k][...], scaled_ref[first:, :])
            term_ref[:, :width] = (total * gain).astype(jnp.bfloat16)
            total = contract_rows(g_ref[...], out_ref[:first, :])
            total += contract_rows(g_tails[k][...], out_ref[first:, :])
            term_ref[:, width:] = total.astype(jnp.bfloat16)


def weight_grads(places, heads, tails, g_tails, g_rows, scaled, out, gain):
    features = gain.shape[2]
    width = scaled.shape[1] + out.shape[1]
    vmem = pl.BlockSpec(memory_space=pltpu.VMEM)
    return pl.pallas_call(
        weight_grad_kernel,
        out_shape=jax.ShapeDtypeStruct((4 * features, width), jnp.bfloat16),
        grid_spec=pltpu.PrefetchScalarGridSpec(
            num_scalar_prefetch=1,
            grid=(4,),
            in_specs=[vmem] * 12
            + [pl.BlockSpec((g_rows.shape[0], features), lambda j, place: (0, j))]
            + [vmem] * 2
            + [pl.BlockSpec((1, 1, features), lambda j, place: (j, 0, 0))],
            out_specs=pl.BlockSpec((features, width), lambda j, place: (j, 0)),
        ),
        compiler_params=pltpu.CompilerParams(vmem_limit_bytes=40 * 1024 * 1024),
        cost_estimate=pl.CostEstimate(
            flops=2 * scaled.shape[0] * 4 * features * width,
            bytes_accessed=4 * features * (4 * scaled.shape[0] + 2 * width),
            transcendentals=0,
        ),
        name="weight_grads",
    )(places, *heads, *tails, *g_tails, g_rows, scaled, out, gain)


def per_device(roll_rows, dest, lengths, clusters, log_prob_grad, gain, w_q, w_k, w_v, w_o_t):
    sequence_count = dest.shape[0]
    max_len, local_features = roll_rows.shape[1:]
    row_count = log_prob_grad.shape[0]
    replicas = lax.axis_size("fsdp")
    per_pair = sequence_count // replicas
    me = lax.axis_index("fsdp")
    z = lax.axis_index("tp")
    f32, bf16 = jnp.float32, jnp.bfloat16
    q_cols, k_cols = w_q.shape[1], w_k.shape[1]
    qkv_cols = q_cols + 2 * k_cols
    feature_count = gain.shape[0]

    bounds = [0, row_count - 2 * BLOCK, row_count]
    g_rows = lax.all_gather(log_prob_grad[: bounds[1], :], "tp", axis=1, tiled=True)
    g_tail = log_prob_grad[bounds[1] :, :]
    g_near = gather_near(g_tail)
    g_far2 = gather_far(g_near, z)
    g_end = gather_end(g_far2)
    g_shards = shards(g_tail, g_near, g_far2, g_end, z)

    slot_ids = jnp.arange(sequence_count, dtype=jnp.int32)
    earlier_dest = dest[None, :] < dest[:, None]
    send_block = jnp.sum(earlier_dest.astype(jnp.int32), axis=1)
    source = jnp.sum(
        jnp.where(send_block[None, :] == slot_ids[:, None], slot_ids[None, :], 0), axis=1
    )
    send_rows = jnp.take(roll_rows, source, axis=0, mode="clip")
    arrived_rows = lax.all_to_all(send_rows, "fsdp", split_axis=0, concat_axis=0, tiled=True)

    ballots = clusters.reshape(sequence_count // GSIZE, GSIZE)
    vote_share = jnp.mean((ballots[:, :, None] == ballots[:, None, :]).astype(f32), axis=2)
    advantage = (vote_share - jnp.mean(vote_share, axis=1, keepdims=True)).reshape(sequence_count)
    tags = jnp.stack([(dest % sequence_count).astype(f32), advantage], axis=1)
    picked = send_block[None, :] == slot_ids[:, None]
    tags = jnp.sum(jnp.where(picked[:, :, None], tags[None, :, :], 0.0), axis=1).astype(bf16)
    tags = lax.all_to_all(tags, "fsdp", split_axis=0, concat_axis=0, tiled=True).astype(f32)
    holder = tags[None, :, 0].astype(jnp.int32) == slot_ids[:, None]
    slot_of = jnp.sum(jnp.where(holder, slot_ids[None, :], 0), axis=1)
    seq_advantage = jnp.sum(jnp.where(holder, tags[None, :, 1], 0.0), axis=1)

    lengths_row = lengths.reshape(sequence_count)
    sequence_ends = jnp.cumsum(lengths_row)
    sequence_starts = sequence_ends - lengths_row
    row_index = jnp.arange(row_count, dtype=jnp.int32)
    one_hot = (sequence_ends[None, :] > row_index[:, None]) & (
        sequence_starts[None, :] <= row_index[:, None]
    )
    row_start = jnp.sum(jnp.where(one_hot, sequence_starts[None, :], 0), axis=1)
    position = row_index - row_start
    row_slot = jnp.sum(jnp.where(one_hot, slot_of[None, :], 0), axis=1)
    adv = jnp.sum(jnp.where(one_hot, seq_advantage[None, :], 0.0), axis=1)[:, None]
    half_width = HD // 2
    frequency = ROPE_BASE ** (-(2.0 * jnp.arange(half_width, dtype=f32)) / HD)
    angles = position.astype(f32)[:, None] * frequency[None, :]
    cos, sin = jnp.cos(angles), jnp.sin(angles)
    cos = jnp.concatenate([cos, cos], axis=1)
    sin = jnp.concatenate([-sin, sin], axis=1)

    start = row_start[:, None]
    arrived_rows = after(arrived_rows, cos, sin, start, adv, g_far2)
    x_own = jnp.take(
        arrived_rows.reshape(sequence_count * max_len, local_features),
        row_slot * max_len + position,
        axis=0,
        mode="clip",
    )
    x_head, x_tail = x_own[: bounds[1], :], x_own[bounds[1] :, :]
    tail_near = gather_near(x_tail)
    head_near = gather_near(after(x_head, tail_near[0], g_end))
    tail_far2 = gather_far((after(tail_near[0], g_rows), tail_near[1]), z)
    head_far2 = gather_far((after(head_near[0], tail_far2), head_near[1]), z)
    tail_end = gather_end(after(tail_far2, *head_near))
    tail_shards = shards(x_tail, tail_near, tail_far2, tail_end, z)

    w_qkv = lax.all_gather(
        jnp.concatenate([w_q, w_k, w_v], axis=1), "fsdp", axis=0, tiled=True
    )
    w_o = lax.all_gather(w_o_t, "fsdp", axis=0, tiled=True)
    gain_f = gain.astype(f32)
    gain_shards = gain_f.reshape(4, 1, local_features)
    w_shards = (w_qkv.astype(f32) * gain_f[:, None]).astype(bf16)
    w_shards = w_shards.reshape(4, local_features, qkv_cols)
    w_k_parts = [lax.dynamic_index_in_dim(w_shards, z ^ k, 0, keepdims=False) for k in range(4)]

    def backward(i, raw, inv, prev):
        return attention(
            bounds[i], row_count, feature_count, raw, inv, ga[i], adv, cos, sin, start, prev
        )

    def input_terms(dqkv, scales, parts):
        return [
            (
                scales[:, 0:1] * times_trans(dqkv, w_k_parts[k])
                - parts[k].astype(f32) * scales[:, 1:2]
            ).astype(bf16)
            for k in range(4)
        ]

    raw1, inv1 = project(tail_shards, w_k_parts, (), feature_count)
    head_near_shard = jnp.where(z % 2 == 1, head_near[0], head_near[1])
    early = project([x_head, head_near_shard, head_far2], w_k_parts[:3], (), 0)
    head_end = gather_end(after(head_far2, tail_end, raw1, early[0]))
    head_shards = shards(x_head, head_near, head_far2, head_end, z)
    x_chunks = [head_shards, tail_shards]
    w_o = after(w_o, early[0])
    o_shards = w_o.reshape(4, local_features, q_cols)
    ga = [
        matmul(g_rows, w_o),
        sum(
            matmul(g_shards[k], lax.dynamic_index_in_dim(o_shards, z ^ k, 0, keepdims=False))
            for k in range(4)
        ),
    ]
    raw0, inv0 = project(head_shards[3:], w_k_parts[3:], early, feature_count)
    dqkv0, scaled0, scales0, out0, *carry = backward(0, raw0, inv0, ())
    final = dqkv0.shape[0]
    terms0 = input_terms(dqkv0, scales0, [x[:final] for x in head_shards])
    end0 = scatter_end(terms0)
    total0 = far_total(terms0, end0)
    step0 = scatter_far(total0)
    dx0 = scatter_near(terms0, step0, z)

    dqkv1, scaled1, scales1, out1 = backward(
        1, after(raw1, terms0[3]), inv1, carry
    )
    places = jnp.stack([z ^ j for j in range(4)]).astype(jnp.int32)
    weight_terms = weight_grads(
        places,
        head_shards,
        tail_shards,
        g_shards,
        g_rows,
        after(jnp.concatenate([scaled0, scaled1], axis=0), total0),
        jnp.concatenate([out0, out1], axis=0),
        gain_shards,
    )
    summed = lax.psum_scatter(weight_terms, "fsdp", scatter_dimension=0, tiled=True)

    terms1 = input_terms(
        after(dqkv1, weight_terms),
        scales1,
        [jnp.concatenate([x[final:], y], axis=0) for x, y in zip(*x_chunks)],
    )
    end1 = scatter_end([*terms1[:3], after(terms1[3], end0)])
    step1 = scatter_far(far_total(terms1, after(end1, *step0)))
    dx1 = scatter_near(terms1, (after(step1[0], dx0), step1[1]), z)
    dx = jnp.concatenate([dx0, dx1], axis=0)
    input_grad = (adv * log_prob_grad.astype(f32) + dx).astype(bf16)
    grad_q = summed[:, :q_cols]
    grad_k = summed[:, q_cols : q_cols + k_cols]
    grad_v = summed[:, q_cols + k_cols : qkv_cols]
    grad_o_t = summed[:, qkv_cols:]
    return (input_grad, grad_q, grad_k, grad_v, grad_o_t)


def solution(mesh):
    in_specs = (
        P("fsdp", None, "tp"),
        P("fsdp"),
        P("fsdp", None),
        P("fsdp"),
        P("fsdp", "tp"),
        P(),
        P("fsdp", "tp"),
        P("fsdp", "tp"),
        P("fsdp", "tp"),
        P("fsdp", "tp"),
    )
    out_specs = (
        P("fsdp", "tp"),
        P("fsdp", "tp"),
        P("fsdp", "tp"),
        P("fsdp", "tp"),
        P("fsdp", "tp"),
    )
    return jax.shard_map(
        per_device, mesh=mesh, in_specs=in_specs, out_specs=out_specs, check_vma=False
    )
```

```python
import functools

import jax
import jax.numpy as jnp
from jax import lax
from jax.experimental import pallas as pl
from jax.experimental.pallas import tpu as pltpu
from jax.sharding import PartitionSpec as P

KEY_VALUE_HEADS = 4
HD = 128
QUERY_HEADS = 16
GSIZE = 16
ROPE_BASE = 1000000.0
NORM_EPSILON = 1e-06
BLOCK = 128

UP = [(0, 1), (1, 2), (2, 3)]
DOWN = [(1, 0), (2, 1), (3, 2)]
UP_MID = [(1, 2), (2, 3)]
DOWN_MID = [(1, 0), (2, 1)]
TO_ENDS = [(2, 3), (1, 0)]
FROM_ENDS = [(3, 2), (0, 1)]
UP_IN = [(0, 1), (1, 2)]
DOWN_IN = [(3, 2), (2, 1)]


def contract_rows(left, right):
    return lax.dot_general(
        left, right, (((0,), (0,)), ((), ())), preferred_element_type=jnp.float32
    )


def times_trans(left, right):
    return lax.dot_general(
        left, right, (((1,), (1,)), ((), ())), preferred_element_type=jnp.float32
    )


def matmul(left, right):
    return jnp.dot(left, right, preferred_element_type=jnp.float32)


def gather_near(own):
    return lax.ppermute(own, "tp", UP), lax.ppermute(own, "tp", DOWN)


def gather_far(step1, z):
    up2 = lax.ppermute(step1[0], "tp", UP_MID)
    down2 = lax.ppermute(step1[1], "tp", DOWN_MID)
    return jnp.where(z >= 2, up2, down2)


def gather_end(far2):
    return lax.ppermute(far2, "tp", TO_ENDS)


def shards(own, step1, far2, far3, z):
    up1, down1 = step1
    near = jnp.where(z % 2 == 1, up1, down1)
    other = jnp.where(z == 1, down1, jnp.where(z == 2, up1, far3))
    return [own, near, far2, other]


def after(value, *earlier):
    return lax.optimization_barrier((value, *earlier))[0]


def scatter_end(parts):
    return lax.ppermute(parts[3], "tp", FROM_ENDS)


def far_total(parts, from_end):
    return (parts[2].astype(jnp.float32) + from_end.astype(jnp.float32)).astype(jnp.bfloat16)


def scatter_far(total2):
    return lax.ppermute(total2, "tp", UP_IN), lax.ppermute(total2, "tp", DOWN_IN)


def scatter_near(parts, step2, z):
    own, near, _, other = parts
    f32 = jnp.float32
    up2, down2 = step2
    go_up = jnp.where(z == 1, other, near).astype(f32) + up2.astype(f32)
    go_down = jnp.where(z == 2, other, near).astype(f32) + down2.astype(f32)
    up3 = lax.ppermute(go_up.astype(jnp.bfloat16), "tp", UP)
    down3 = lax.ppermute(go_down.astype(jnp.bfloat16), "tp", DOWN)
    return own.astype(f32) + up3.astype(f32) + down3.astype(f32)


def attention_kernel(has_prev, is_last, first, feature_count, *refs):
    refs = list(refs)
    raw_ref, inv_ref, ga_ref, adv_ref, cos_ref, sin_ref, start_ref = refs[:7]
    refs = refs[7:]
    if has_prev:
        lin_prev, inv_prev, dq_prev, dk_prev, dv_prev = refs[:5]
        refs = refs[5:]
    dqkv_ref, dscaled_ref, mean_ref, out_ref = refs[:4]
    refs = refs[4:]
    if not is_last:
        lin_next, inv_next, dq_next, dk_next, dv_next = refs[:5]
        refs = refs[5:]
    qkv_b, dq_b, dk_acc, dv_acc = refs
    rows = raw_ref.shape[0]
    heads = ga_ref.shape[1] // HD
    qw = heads * HD
    scale = HD ** (-0.5)
    f32, bf16 = jnp.float32, jnp.bfloat16
    blocks = rows // BLOCK

    def span(block):
        return slice(block * BLOCK, (block + 1) * BLOCK)

    def turn(value, cos, sin):
        return value * cos + pltpu.roll(value, HD // 2, 1) * sin

    def whole(block):
        return slice(first + block * BLOCK, first + (block + 1) * BLOCK)

    def linear(block, cols):
        if block < 0:
            return lin_prev[:, cols]
        return raw_ref[span(block), cols] * inv_ref[span(block), :]

    def prepare(block, from_head):
        cos, sin = cos_ref[whole(block), :], sin_ref[whole(block), :]
        for h in range(from_head, heads + 1):
            cols = slice(h * HD, (h + 1) * HD)
            qkv_b[span(block + 1), cols] = turn(linear(block, cols), cos, sin).astype(bf16)
        cols = slice(qw + HD, qw + 2 * HD)
        qkv_b[span(block + 1), cols] = linear(block, cols).astype(bf16)

    if has_prev:
        prepare(-1, heads)
        dq_b[span(0), :] = dq_prev[...]
        dk_acc[span(0), :] = dk_prev[...]
        dv_acc[span(0), :] = dv_prev[...]
    else:
        qkv_b[span(0), :] = jnp.zeros((BLOCK, qkv_b.shape[1]), bf16)
        dk_acc[span(0), :] = jnp.zeros((BLOCK, HD), f32)
        dv_acc[span(0), :] = jnp.zeros((BLOCK, HD), f32)

    for block in range(blocks):
        prepare(block, 0)
        adv = adv_ref[whole(block), :]
        here, after = span(block), span(block + 1)
        both = slice(block * BLOCK, (block + 2) * BLOCK)
        qs = jnp.concatenate(
            [qkv_b[after, h * HD : (h + 1) * HD] for h in range(heads)], axis=0
        )
        gs = jnp.concatenate(
            [(ga_ref[here, h * HD : (h + 1) * HD] * adv).astype(bf16) for h in range(heads)], axis=0
        )
        ks = qkv_b[both, qw : qw + HD]
        vs = qkv_b[both, qw + HD : qw + 2 * HD]
        start = start_ref[whole(block), :] - (first + (block - 1) * BLOCK)
        col = lax.broadcasted_iota(jnp.int32, (BLOCK, 2 * BLOCK), 1)
        row = lax.broadcasted_iota(jnp.int32, (BLOCK, 2 * BLOCK), 0) + BLOCK
        bias = jnp.where((col >= start) & (col <= row), 0.0, -1e30)
        bias = jnp.concatenate([bias] * heads, axis=0)
        scores = times_trans(qs, ks) * scale + bias
        top = jnp.max(scores, axis=-1, keepdims=True)
        weight = jnp.exp(scores - top)
        prob = weight / jnp.sum(weight, axis=-1, keepdims=True)
        prob_b = prob.astype(bf16)
        out = matmul(prob_b, vs)
        grad_prob = times_trans(gs, vs)
        delta = jnp.sum(prob * grad_prob, axis=-1, keepdims=True)
        ds = (prob * (grad_prob - delta) * scale).astype(bf16)
        dq = matmul(ds, ks)
        dk_acc[span(block), :] += contract_rows(ds[:, :BLOCK], qs)
        dk_acc[after, :] = contract_rows(ds[:, BLOCK:], qs)
        dv_acc[span(block), :] += contract_rows(prob_b[:, :BLOCK], gs)
        dv_acc[after, :] = contract_rows(prob_b[:, BLOCK:], gs)
        cos, sin = cos_ref[whole(block), :], sin_ref[whole(block), :]
        for h in range(heads):
            cols = slice(h * HD, (h + 1) * HD)
            out_ref[here, cols] = (out[span(h), :].astype(bf16).astype(f32) * adv).astype(bf16)
            dq_b[after, cols] = turn(dq[span(h), :], cos, -sin).astype(bf16)

    begin = -1 if has_prev else 0
    end = blocks if is_last else blocks - 1
    for block in range(begin, end):
        to = span(block - begin)
        cos, sin = cos_ref[whole(block), :], sin_ref[whole(block), :]
        inv = inv_prev[...] if block < 0 else inv_ref[span(block), :]
        total = jnp.zeros((BLOCK, 1), f32)
        for h in range(heads + 2):
            cols = slice(h * HD, (h + 1) * HD)
            if h < heads:
                grad = dq_b[span(block + 1), cols]
            elif h == heads:
                grad = turn(dk_acc[span(block + 1), :], cos, -sin).astype(bf16)
            else:
                grad = dv_acc[span(block + 1), :].astype(bf16)
            dqkv_ref[to, cols] = grad
            grad = grad.astype(f32)
            dscaled_ref[to, cols] = (grad * inv).astype(bf16)
            total += jnp.sum(grad * linear(block, cols), axis=-1, keepdims=True)
        mean_ref[to, 0:1] = inv
        mean_ref[to, 1:2] = inv * inv * total * (1.0 / feature_count)
    if not is_last:
        inv_next[...] = inv_ref[span(blocks - 1), :]
        lin_next[...] = raw_ref[span(blocks - 1), :] * inv_next[...]
        dq_next[...] = dq_b[span(blocks), :]
        dk_next[...] = dk_acc[span(blocks), :]
        dv_next[...] = dv_acc[span(blocks), :]


def attention(first, total, feature_count, raw, inv, ga, adv, cos, sin, start, prev):
    rows, width = raw.shape
    qw = ga.shape[1]
    is_last = first + rows == total
    final = rows + (BLOCK if prev else 0) - (0 if is_last else BLOCK)
    f32, bf16 = jnp.float32, jnp.bfloat16
    out_shape = [
        jax.ShapeDtypeStruct((final, width), bf16),
        jax.ShapeDtypeStruct((final, width), bf16),
        jax.ShapeDtypeStruct((final, 2), f32),
        jax.ShapeDtypeStruct((rows, qw), bf16),
    ]
    if not is_last:
        out_shape += [
            jax.ShapeDtypeStruct((BLOCK, width), f32),
            jax.ShapeDtypeStruct((BLOCK, 1), f32),
            jax.ShapeDtypeStruct((BLOCK, qw), bf16),
            jax.ShapeDtypeStruct((BLOCK, HD), f32),
            jax.ShapeDtypeStruct((BLOCK, HD), f32),
        ]
    operands = [raw, inv, ga, adv, cos, sin, start] + list(prev)
    vmem = pl.BlockSpec(memory_space=pltpu.VMEM)
    return pl.pallas_call(
        functools.partial(attention_kernel, bool(prev), is_last, first, feature_count),
        out_shape=out_shape,
        in_specs=[vmem] * len(operands),
        out_specs=[vmem] * len(out_shape),
        scratch_shapes=[
            pltpu.VMEM((rows + BLOCK, width), bf16),
            pltpu.VMEM((rows + BLOCK, qw), bf16),
            pltpu.VMEM((rows + BLOCK, HD), f32),
            pltpu.VMEM((rows + BLOCK, HD), f32),
        ],
        compiler_params=pltpu.CompilerParams(vmem_limit_bytes=12 * 1024 * 1024),
        cost_estimate=pl.CostEstimate(
            flops=rows * 2 * BLOCK * HD * 12 * (qw // HD),
            bytes_accessed=rows * width * 8 + rows * qw * 6,
            transcendentals=rows * 2 * BLOCK * (qw // HD),
        ),
        name="attention",
    )(*operands)


def project_kernel(count, feature_count, *refs):
    x_refs, w_refs = refs[:count], refs[count : 2 * count]
    raw_ref, square_ref = refs[-2:]
    raw, squares = None, None
    if len(refs) > 2 * count + 2:
        raw, squares = refs[2 * count][...], refs[2 * count + 1][...]
    for x_ref, w_ref in zip(x_refs, w_refs):
        part = matmul(x_ref[...], w_ref[...])
        raw = part if raw is None else raw + part
        wide = x_ref[...].astype(jnp.float32)
        part = jnp.sum(wide * wide, axis=1, keepdims=True)
        squares = part if squares is None else squares + part
    raw_ref[...] = raw
    if feature_count:
        squares = lax.rsqrt(squares / feature_count + NORM_EPSILON)
    square_ref[...] = squares


def project(parts, weights, prior, feature_count):
    rows, width = parts[0].shape[0], weights[0].shape[1]
    operands = [*parts, *weights, *prior]
    vmem = pl.BlockSpec(memory_space=pltpu.VMEM)
    return pl.pallas_call(
        functools.partial(project_kernel, len(parts), feature_count),
        out_shape=[
            jax.ShapeDtypeStruct((rows, width), jnp.float32),
            jax.ShapeDtypeStruct((rows, 1), jnp.float32),
        ],
        in_specs=[vmem] * len(operands),
        out_specs=[vmem] * 2,
        compiler_params=pltpu.CompilerParams(vmem_limit_bytes=12 * 1024 * 1024),
        cost_estimate=pl.CostEstimate(
            flops=2 * len(parts) * rows * width * parts[0].shape[1],
            bytes_accessed=2 * len(parts) * parts[0].shape[1] * (rows + width) + 8 * rows * width,
            transcendentals=rows,
        ),
        name="project",
    )(*operands)


def weight_grad_kernel(place_ref, *refs):
    heads, tails, g_tails = refs[:4], refs[4:8], refs[8:12]
    g_ref, scaled_ref, out_ref, gain_ref, term_ref = refs[12:]
    width = scaled_ref.shape[1]
    gain = gain_ref[0]
    gain = jnp.transpose(jnp.broadcast_to(gain, (HD, gain.shape[1])))[:, 0:1]
    first = g_ref.shape[0]
    for k in range(4):

        @pl.when(place_ref[pl.program_id(0)] == k)
        def _():
            total = contract_rows(heads[k][...], scaled_ref[:first, :])
            total += contract_rows(tails[k][...], scaled_ref[first:, :])
            term_ref[:, :width] = (total * gain).astype(jnp.bfloat16)
            total = contract_rows(g_ref[...], out_ref[:first, :])
            total += contract_rows(g_tails[k][...], out_ref[first:, :])
            term_ref[:, width:] = total.astype(jnp.bfloat16)


def weight_grads(places, heads, tails, g_tails, g_rows, scaled, out, gain):
    features = gain.shape[2]
    width = scaled.shape[1] + out.shape[1]
    vmem = pl.BlockSpec(memory_space=pltpu.VMEM)
    return pl.pallas_call(
        weight_grad_kernel,
        out_shape=jax.ShapeDtypeStruct((4 * features, width), jnp.bfloat16),
        grid_spec=pltpu.PrefetchScalarGridSpec(
            num_scalar_prefetch=1,
            grid=(4,),
            in_specs=[vmem] * 12
            + [pl.BlockSpec((g_rows.shape[0], features), lambda j, place: (0, j))]
            + [vmem] * 2
            + [pl.BlockSpec((1, 1, features), lambda j, place: (j, 0, 0))],
            out_specs=pl.BlockSpec((features, width), lambda j, place: (j, 0)),
        ),
        compiler_params=pltpu.CompilerParams(vmem_limit_bytes=20 * 1024 * 1024),
        cost_estimate=pl.CostEstimate(
            flops=2 * scaled.shape[0] * 4 * features * width,
            bytes_accessed=4 * features * (4 * scaled.shape[0] + 2 * width),
            transcendentals=0,
        ),
        name="weight_grads",
    )(places, *heads, *tails, *g_tails, g_rows, scaled, out, gain)


def per_device(roll_rows, dest, lengths, clusters, log_prob_grad, gain, w_q, w_k, w_v, w_o_t):
    sequence_count = dest.shape[0]
    max_len, local_features = roll_rows.shape[1:]
    row_count = log_prob_grad.shape[0]
    replicas = lax.axis_size("fsdp")
    per_pair = sequence_count // replicas
    me = lax.axis_index("fsdp")
    z = lax.axis_index("tp")
    f32, bf16 = jnp.float32, jnp.bfloat16
    q_cols, k_cols = w_q.shape[1], w_k.shape[1]
    qkv_cols = q_cols + 2 * k_cols
    feature_count = gain.shape[0]

    bounds = [0, row_count - 2 * BLOCK, row_count]
    g_rows = lax.all_gather(log_prob_grad[: bounds[1], :], "tp", axis=1, tiled=True)
    g_tail = log_prob_grad[bounds[1] :, :]
    g_near = gather_near(g_tail)
    g_far2 = gather_far(g_near, z)
    g_end = gather_end(g_far2)
    g_shards = shards(g_tail, g_near, g_far2, g_end, z)

    slot_ids = jnp.arange(sequence_count, dtype=jnp.int32)
    earlier_dest = dest[None, :] < dest[:, None]
    send_block = jnp.sum(earlier_dest.astype(jnp.int32), axis=1)
    source = jnp.sum(
        jnp.where(send_block[None, :] == slot_ids[:, None], slot_ids[None, :], 0), axis=1
    )
    send_rows = jnp.take(roll_rows, source, axis=0, mode="clip")
    arrived_rows = lax.all_to_all(send_rows, "fsdp", split_axis=0, concat_axis=0, tiled=True)

    ballots = clusters.reshape(sequence_count // GSIZE, GSIZE)
    vote_share = jnp.mean((ballots[:, :, None] == ballots[:, None, :]).astype(f32), axis=2)
    advantage = (vote_share - jnp.mean(vote_share, axis=1, keepdims=True)).reshape(sequence_count)
    tags = jnp.stack([(dest % sequence_count).astype(f32), advantage], axis=1)
    picked = send_block[None, :] == slot_ids[:, None]
    tags = jnp.sum(jnp.where(picked[:, :, None], tags[None, :, :], 0.0), axis=1).astype(bf16)
    tags = lax.all_to_all(tags, "fsdp", split_axis=0, concat_axis=0, tiled=True).astype(f32)
    holder = tags[None, :, 0].astype(jnp.int32) == slot_ids[:, None]
    slot_of = jnp.sum(jnp.where(holder, slot_ids[None, :], 0), axis=1)
    seq_advantage = jnp.sum(jnp.where(holder, tags[None, :, 1], 0.0), axis=1)

    lengths_row = lengths.reshape(sequence_count)
    sequence_ends = jnp.cumsum(lengths_row)
    sequence_starts = sequence_ends - lengths_row
    row_index = jnp.arange(row_count, dtype=jnp.int32)
    one_hot = (sequence_ends[None, :] > row_index[:, None]) & (
        sequence_starts[None, :] <= row_index[:, None]
    )
    row_start = jnp.sum(jnp.where(one_hot, sequence_starts[None, :], 0), axis=1)
    position = row_index - row_start
    row_slot = jnp.sum(jnp.where(one_hot, slot_of[None, :], 0), axis=1)
    adv = jnp.sum(jnp.where(one_hot, seq_advantage[None, :], 0.0), axis=1)[:, None]
    half_width = HD // 2
    frequency = ROPE_BASE ** (-(2.0 * jnp.arange(half_width, dtype=f32)) / HD)
    angles = position.astype(f32)[:, None] * frequency[None, :]
    cos, sin = jnp.cos(angles), jnp.sin(angles)
    cos = jnp.concatenate([cos, cos], axis=1)
    sin = jnp.concatenate([-sin, sin], axis=1)

    start = row_start[:, None]
    arrived_rows = after(arrived_rows, cos, sin, start, adv)
    x_own = jnp.take(
        arrived_rows.reshape(sequence_count * max_len, local_features),
        row_slot * max_len + position,
        axis=0,
        mode="clip",
    )
    x_head, x_tail = x_own[: bounds[1], :], x_own[bounds[1] :, :]
    tail_near = gather_near(x_tail)
    head_near = gather_near(after(x_head, tail_near[0], g_far2))
    tail_far2 = gather_far((after(tail_near[0], g_rows), tail_near[1]), z)
    head_far2 = gather_far((after(head_near[0], tail_far2), head_near[1]), z)

    w_qkv = lax.all_gather(
        jnp.concatenate([w_q, w_k, w_v], axis=1), "fsdp", axis=0, tiled=True
    )
    w_o = lax.all_gather(w_o_t, "fsdp", axis=0, tiled=True)
    gain_f = gain.astype(f32)
    gain_shards = gain_f.reshape(4, 1, local_features)
    w_shards = (w_qkv.astype(f32) * gain_f[:, None]).astype(bf16)
    w_shards = w_shards.reshape(4, local_features, qkv_cols)
    w_k_parts = [lax.dynamic_index_in_dim(w_shards, z ^ k, 0, keepdims=False) for k in range(4)]

    def backward(i, raw, inv, prev):
        return attention(
            bounds[i], row_count, feature_count, raw, inv, ga[i], adv, cos, sin, start, prev
        )

    def input_terms(dqkv, scales, parts):
        return [
            (
                scales[:, 0:1] * times_trans(dqkv, w_k_parts[k])
                - parts[k].astype(f32) * scales[:, 1:2]
            ).astype(bf16)
            for k in range(4)
        ]

    tail_end = gather_end(after(tail_far2, g_end, *head_near))
    tail_shards = shards(x_tail, tail_near, tail_far2, tail_end, z)
    raw1, inv1 = project(tail_shards, w_k_parts, (), feature_count)
    head_end = gather_end(after(head_far2, tail_end))
    w_o = after(w_o, head_far2)
    o_shards = w_o.reshape(4, local_features, q_cols)
    ga = [
        matmul(g_rows, w_o),
        sum(
            matmul(g_shards[k], lax.dynamic_index_in_dim(o_shards, z ^ k, 0, keepdims=False))
            for k in range(4)
        ),
    ]
    head_shards = shards(x_head, head_near, head_far2, after(head_end, raw1, *ga), z)
    raw0, inv0 = project(head_shards, w_k_parts, (), feature_count)
    dqkv0, scaled0, scales0, out0, *carry = backward(0, raw0, inv0, ())
    final = dqkv0.shape[0]
    terms0 = input_terms(dqkv0, scales0, [x[:final] for x in head_shards])
    end0 = scatter_end(terms0)
    total0 = far_total(terms0, end0)
    step0 = scatter_far(total0)
    dx0 = scatter_near(terms0, step0, z)

    dqkv1, scaled1, scales1, out1 = backward(
        1, after(raw1, terms0[3]), inv1, carry
    )
    places = jnp.stack([z ^ j for j in range(4)]).astype(jnp.int32)
    weight_terms = weight_grads(
        places,
        head_shards,
        tail_shards,
        g_shards,
        g_rows,
        after(jnp.concatenate([scaled0, scaled1], axis=0), total0),
        jnp.concatenate([out0, out1], axis=0),
        gain_shards,
    )
    summed = lax.psum_scatter(weight_terms, "fsdp", scatter_dimension=0, tiled=True)

    terms1 = input_terms(
        after(dqkv1, weight_terms),
        scales1,
        [jnp.concatenate([x[final:], y], axis=0) for x, y in zip(head_shards, tail_shards)],
    )
    end1 = scatter_end([*terms1[:3], after(terms1[3], end0)])
    step1 = scatter_far(far_total(terms1, after(end1, *step0)))
    dx1 = scatter_near(terms1, (after(step1[0], dx0), step1[1]), z)
    dx = jnp.concatenate([dx0, dx1], axis=0)
    input_grad = (adv * log_prob_grad.astype(f32) + dx).astype(bf16)
    grad_q = summed[:, :q_cols]
    grad_k = summed[:, q_cols : q_cols + k_cols]
    grad_v = summed[:, q_cols + k_cols : qkv_cols]
    grad_o_t = summed[:, qkv_cols:]
    return (input_grad, grad_q, grad_k, grad_v, grad_o_t)


def solution(mesh):
    in_specs = (
        P("fsdp", None, "tp"),
        P("fsdp"),
        P("fsdp", None),
        P("fsdp"),
        P("fsdp", "tp"),
        P(),
        P("fsdp", "tp"),
        P("fsdp", "tp"),
        P("fsdp", "tp"),
        P("fsdp", "tp"),
    )
    out_specs = (
        P("fsdp", "tp"),
        P("fsdp", "tp"),
        P("fsdp", "tp"),
        P("fsdp", "tp"),
        P("fsdp", "tp"),
    )
    return jax.shard_map(
        per_device, mesh=mesh, in_specs=in_specs, out_specs=out_specs, check_vma=False
    )
```

```python
import functools

import jax
import jax.numpy as jnp
from jax import lax
from jax.experimental import pallas as pl
from jax.experimental.pallas import tpu as pltpu
from jax.sharding import PartitionSpec as P

KEY_VALUE_HEADS = 4
HD = 128
QUERY_HEADS = 16
GSIZE = 16
ROPE_BASE = 1000000.0
NORM_EPSILON = 1e-06
BLOCK = 128

UP = [(0, 1), (1, 2), (2, 3)]
DOWN = [(1, 0), (2, 1), (3, 2)]
UP_MID = [(1, 2), (2, 3)]
DOWN_MID = [(1, 0), (2, 1)]
TO_ENDS = [(2, 3), (1, 0)]
FROM_ENDS = [(3, 2), (0, 1)]
UP_IN = [(0, 1), (1, 2)]
DOWN_IN = [(3, 2), (2, 1)]


def contract_rows(left, right):
    return lax.dot_general(
        left, right, (((0,), (0,)), ((), ())), preferred_element_type=jnp.float32
    )


def times_trans(left, right):
    return lax.dot_general(
        left, right, (((1,), (1,)), ((), ())), preferred_element_type=jnp.float32
    )


def matmul(left, right):
    return jnp.dot(left, right, preferred_element_type=jnp.float32)


def gather_near(own):
    return lax.ppermute(own, "tp", UP), lax.ppermute(own, "tp", DOWN)


def gather_far(step1, z):
    up2 = lax.ppermute(step1[0], "tp", UP_MID)
    down2 = lax.ppermute(step1[1], "tp", DOWN_MID)
    return jnp.where(z >= 2, up2, down2)


def gather_end(far2):
    return lax.ppermute(far2, "tp", TO_ENDS)


def shards(own, step1, far2, far3, z):
    up1, down1 = step1
    near = jnp.where(z % 2 == 1, up1, down1)
    other = jnp.where(z == 1, down1, jnp.where(z == 2, up1, far3))
    return [own, near, far2, other]


def after(value, *earlier):
    return lax.optimization_barrier((value, *earlier))[0]


def scatter_end(parts):
    return lax.ppermute(parts[3], "tp", FROM_ENDS)


def far_total(parts, from_end):
    return (parts[2].astype(jnp.float32) + from_end.astype(jnp.float32)).astype(jnp.bfloat16)


def scatter_far(total2):
    return lax.ppermute(total2, "tp", UP_IN), lax.ppermute(total2, "tp", DOWN_IN)


def scatter_near(parts, step2, z):
    own, near, _, other = parts
    f32 = jnp.float32
    up2, down2 = step2
    go_up = jnp.where(z == 1, other, near).astype(f32) + up2.astype(f32)
    go_down = jnp.where(z == 2, other, near).astype(f32) + down2.astype(f32)
    up3 = lax.ppermute(go_up.astype(jnp.bfloat16), "tp", UP)
    down3 = lax.ppermute(go_down.astype(jnp.bfloat16), "tp", DOWN)
    return own.astype(f32) + up3.astype(f32) + down3.astype(f32)


def attention_kernel(*refs):
    raw_refs, inv_refs, ga_refs = refs[:2], refs[2:4], refs[4:6]
    adv_ref, cos_ref, sin_ref, start_ref = refs[6:10]
    dqkv_refs, scale_refs = refs[10:12], refs[12:14]
    dscaled_ref, out_ref, qkv_b, dq_b, dk_acc, dv_acc = refs[14:]
    heads = ga_refs[0].shape[1] // HD
    qw = heads * HD
    scale = HD ** (-0.5)
    f32, bf16 = jnp.float32, jnp.bfloat16
    blocks = adv_ref.shape[0] // BLOCK

    def span(block):
        return slice(block * BLOCK, (block + 1) * BLOCK)

    def piece(pair, block):
        first = pair[0].shape[0] // BLOCK
        return (pair[0], span(block)) if block < first else (pair[1], span(block - first))

    def read(pair, block, cols):
        ref, rows = piece(pair, block)
        return ref[rows, cols]

    def turn(value, cos, sin):
        return value * cos + pltpu.roll(value, HD // 2, 1) * sin

    def inverse(block):
        return read(inv_refs, block, slice(0, 1))

    qkv_b[span(0), :] = jnp.zeros((BLOCK, qkv_b.shape[1]), bf16)
    dk_acc[span(0), :] = jnp.zeros((BLOCK, HD), f32)
    dv_acc[span(0), :] = jnp.zeros((BLOCK, HD), f32)

    for block in range(blocks):
        here, after = span(block), span(block + 1)
        both = slice(block * BLOCK, (block + 2) * BLOCK)
        cos, sin = cos_ref[here, :], sin_ref[here, :]
        inv = inverse(block)
        for h in range(heads + 2):
            cols = slice(h * HD, (h + 1) * HD)
            linear = read(raw_refs, block, cols) * inv
            qkv_b[after, cols] = (turn(linear, cos, sin) if h <= heads else linear).astype(bf16)
        adv = adv_ref[here, :]
        qs = jnp.concatenate(
            [qkv_b[after, h * HD : (h + 1) * HD] for h in range(heads)], axis=0
        )
        gs = jnp.concatenate(
            [
                (read(ga_refs, block, slice(h * HD, (h + 1) * HD)) * adv).astype(bf16)
                for h in range(heads)
            ],
            axis=0,
        )
        ks = qkv_b[both, qw : qw + HD]
        vs = qkv_b[both, qw + HD : qw + 2 * HD]
        start = start_ref[here, :] - (block - 1) * BLOCK
        col = lax.broadcasted_iota(jnp.int32, (BLOCK, 2 * BLOCK), 1)
        row = lax.broadcasted_iota(jnp.int32, (BLOCK, 2 * BLOCK), 0) + BLOCK
        bias = jnp.where((col >= start) & (col <= row), 0.0, -1e30)
        bias = jnp.concatenate([bias] * heads, axis=0)
        scores = times_trans(qs, ks) * scale + bias
        top = jnp.max(scores, axis=-1, keepdims=True)
        weight = jnp.exp(scores - top)
        prob = weight / jnp.sum(weight, axis=-1, keepdims=True)
        prob_b = prob.astype(bf16)
        out = matmul(prob_b, vs)
        grad_prob = times_trans(gs, vs)
        delta = jnp.sum(prob * grad_prob, axis=-1, keepdims=True)
        ds = (prob * (grad_prob - delta) * scale).astype(bf16)
        dq = matmul(ds, ks)
        dk_acc[here, :] += contract_rows(ds[:, :BLOCK], qs)
        dk_acc[after, :] = contract_rows(ds[:, BLOCK:], qs)
        dv_acc[here, :] += contract_rows(prob_b[:, :BLOCK], gs)
        dv_acc[after, :] = contract_rows(prob_b[:, BLOCK:], gs)
        for h in range(heads):
            cols = slice(h * HD, (h + 1) * HD)
            out_ref[here, cols] = (out[span(h), :].astype(bf16).astype(f32) * adv).astype(bf16)
            dq_b[here, cols] = turn(dq[span(h), :], cos, -sin).astype(bf16)

    for block in range(blocks):
        here, after = span(block), span(block + 1)
        cos, sin = cos_ref[here, :], sin_ref[here, :]
        inv = inverse(block)
        dqkv_ref, to = piece(dqkv_refs, block)
        total = jnp.zeros((BLOCK, 1), f32)
        for h in range(heads + 2):
            cols = slice(h * HD, (h + 1) * HD)
            if h < heads:
                grad = dq_b[here, cols]
            elif h == heads:
                grad = turn(dk_acc[after, :], cos, -sin).astype(bf16)
            else:
                grad = dv_acc[after, :].astype(bf16)
            dqkv_ref[to, cols] = grad
            grad = grad.astype(f32) * inv
            dscaled_ref[here, cols] = grad.astype(bf16)
            total += jnp.sum(grad * read(raw_refs, block, cols), axis=-1, keepdims=True)
        scale_ref, to = piece(scale_refs, block)
        scale_ref[to, 0:1] = inv
        scale_ref[to, 1:2] = inv * inv * total


def attention(raw, inv, ga, adv, cos, sin, start):
    rows, width = adv.shape[0], raw[0].shape[1]
    qw = ga[0].shape[1]
    half = rows // (2 * BLOCK) * BLOCK
    f32, bf16 = jnp.float32, jnp.bfloat16
    out_shape = [
        jax.ShapeDtypeStruct((half, width), bf16),
        jax.ShapeDtypeStruct((rows - half, width), bf16),
        jax.ShapeDtypeStruct((half, 2), f32),
        jax.ShapeDtypeStruct((rows - half, 2), f32),
        jax.ShapeDtypeStruct((rows, width), bf16),
        jax.ShapeDtypeStruct((rows, qw), bf16),
    ]
    operands = [*raw, *inv, *ga, adv, cos, sin, start]
    vmem = pl.BlockSpec(memory_space=pltpu.VMEM)
    return pl.pallas_call(
        attention_kernel,
        out_shape=out_shape,
        in_specs=[vmem] * len(operands),
        out_specs=[vmem] * len(out_shape),
        scratch_shapes=[
            pltpu.VMEM((rows + BLOCK, width), bf16),
            pltpu.VMEM((rows, qw), bf16),
            pltpu.VMEM((rows + BLOCK, HD), f32),
            pltpu.VMEM((rows + BLOCK, HD), f32),
        ],
        compiler_params=pltpu.CompilerParams(vmem_limit_bytes=14 * 1024 * 1024),
        cost_estimate=pl.CostEstimate(
            flops=rows * 2 * BLOCK * HD * 12 * (qw // HD),
            bytes_accessed=rows * width * 8 + rows * qw * 6,
            transcendentals=rows * 2 * BLOCK * (qw // HD),
        ),
        name="attention",
    )(*operands)


def project_kernel(count, feature_count, *refs):
    x_refs, w_refs = refs[:count], refs[count : 2 * count]
    raw_ref, square_ref = refs[-2:]
    raw, squares = None, None
    if len(refs) > 2 * count + 2:
        raw, squares = refs[2 * count][...], refs[2 * count + 1][...]
    for x_ref, w_ref in zip(x_refs, w_refs):
        part = matmul(x_ref[...], w_ref[...])
        raw = part if raw is None else raw + part
        wide = x_ref[...].astype(jnp.float32)
        part = jnp.sum(wide * wide, axis=1, keepdims=True)
        squares = part if squares is None else squares + part
    raw_ref[...] = raw
    if feature_count:
        squares = lax.rsqrt(squares / feature_count + NORM_EPSILON)
    square_ref[...] = squares


def project(parts, weights, prior, feature_count):
    rows, width = parts[0].shape[0], weights[0].shape[1]
    operands = [*parts, *weights, *prior]
    vmem = pl.BlockSpec(memory_space=pltpu.VMEM)
    return pl.pallas_call(
        functools.partial(project_kernel, len(parts), feature_count),
        out_shape=[
            jax.ShapeDtypeStruct((rows, width), jnp.float32),
            jax.ShapeDtypeStruct((rows, 1), jnp.float32),
        ],
        in_specs=[vmem] * len(operands),
        out_specs=[vmem] * 2,
        compiler_params=pltpu.CompilerParams(vmem_limit_bytes=12 * 1024 * 1024),
        cost_estimate=pl.CostEstimate(
            flops=2 * len(parts) * rows * width * parts[0].shape[1],
            bytes_accessed=2 * len(parts) * parts[0].shape[1] * (rows + width) + 8 * rows * width,
            transcendentals=rows,
        ),
        name="project",
    )(*operands)


def weight_grad_kernel(place_ref, *refs):
    heads, tails, g_tails = refs[:4], refs[4:8], refs[8:12]
    g_ref, scaled_ref, out_ref, gain_ref, term_ref = refs[12:]
    width = scaled_ref.shape[1]
    gain = gain_ref[0]
    gain = jnp.transpose(jnp.broadcast_to(gain, (HD, gain.shape[1])))[:, 0:1]
    first = g_ref.shape[0]
    for k in range(4):

        @pl.when(place_ref[pl.program_id(0)] == k)
        def _():
            total = contract_rows(heads[k][...], scaled_ref[:first, :])
            total += contract_rows(tails[k][...], scaled_ref[first:, :])
            term_ref[:, :width] = (total * gain).astype(jnp.bfloat16)
            total = contract_rows(g_ref[...], out_ref[:first, :])
            total += contract_rows(g_tails[k][...], out_ref[first:, :])
            term_ref[:, width:] = total.astype(jnp.bfloat16)


def weight_grads(places, heads, tails, g_tails, g_rows, scaled, out, gain):
    features = gain.shape[2]
    width = scaled.shape[1] + out.shape[1]
    vmem = pl.BlockSpec(memory_space=pltpu.VMEM)
    return pl.pallas_call(
        weight_grad_kernel,
        out_shape=jax.ShapeDtypeStruct((4 * features, width), jnp.bfloat16),
        grid_spec=pltpu.PrefetchScalarGridSpec(
            num_scalar_prefetch=1,
            grid=(4,),
            in_specs=[vmem] * 12
            + [pl.BlockSpec((g_rows.shape[0], features), lambda j, place: (0, j))]
            + [vmem] * 2
            + [pl.BlockSpec((1, 1, features), lambda j, place: (j, 0, 0))],
            out_specs=pl.BlockSpec((features, width), lambda j, place: (j, 0)),
        ),
        compiler_params=pltpu.CompilerParams(vmem_limit_bytes=40 * 1024 * 1024),
        cost_estimate=pl.CostEstimate(
            flops=2 * scaled.shape[0] * 4 * features * width,
            bytes_accessed=4 * features * (4 * scaled.shape[0] + 2 * width),
            transcendentals=0,
        ),
        name="weight_grads",
    )(places, *heads, *tails, *g_tails, g_rows, scaled, out, gain)


def per_device(roll_rows, dest, lengths, clusters, log_prob_grad, gain, w_q, w_k, w_v, w_o_t):
    sequence_count = dest.shape[0]
    max_len, local_features = roll_rows.shape[1:]
    row_count = log_prob_grad.shape[0]
    replicas = lax.axis_size("fsdp")
    per_pair = sequence_count // replicas
    me = lax.axis_index("fsdp")
    z = lax.axis_index("tp")
    f32, bf16 = jnp.float32, jnp.bfloat16
    q_cols, k_cols = w_q.shape[1], w_k.shape[1]
    qkv_cols = q_cols + 2 * k_cols
    feature_count = gain.shape[0]

    bounds = [0, row_count - 2 * BLOCK, row_count]
    g_rows = lax.all_gather(log_prob_grad[: bounds[1], :], "tp", axis=1, tiled=True)
    g_tail = log_prob_grad[bounds[1] :, :]
    g_near = gather_near(g_tail)
    g_far2 = gather_far(g_near, z)
    g_end = gather_end(g_far2)
    g_shards = shards(g_tail, g_near, g_far2, g_end, z)

    slot_ids = jnp.arange(sequence_count, dtype=jnp.int32)
    earlier_dest = dest[None, :] < dest[:, None]
    send_block = jnp.sum(earlier_dest.astype(jnp.int32), axis=1)
    source = jnp.sum(
        jnp.where(send_block[None, :] == slot_ids[:, None], slot_ids[None, :], 0), axis=1
    )
    send_rows = jnp.take(roll_rows, source, axis=0, mode="clip")
    arrived_rows = lax.all_to_all(send_rows, "fsdp", split_axis=0, concat_axis=0, tiled=True)

    ballots = clusters.reshape(sequence_count // GSIZE, GSIZE)
    vote_share = jnp.mean((ballots[:, :, None] == ballots[:, None, :]).astype(f32), axis=2)
    advantage = (vote_share - jnp.mean(vote_share, axis=1, keepdims=True)).reshape(sequence_count)
    tags = jnp.stack([(dest % sequence_count).astype(f32), advantage], axis=1)
    picked = send_block[None, :] == slot_ids[:, None]
    tags = jnp.sum(jnp.where(picked[:, :, None], tags[None, :, :], 0.0), axis=1).astype(bf16)
    tags = lax.all_to_all(tags, "fsdp", split_axis=0, concat_axis=0, tiled=True).astype(f32)
    holder = tags[None, :, 0].astype(jnp.int32) == slot_ids[:, None]
    slot_of = jnp.sum(jnp.where(holder, slot_ids[None, :], 0), axis=1)
    seq_advantage = jnp.sum(jnp.where(holder, tags[None, :, 1], 0.0), axis=1)

    lengths_row = lengths.reshape(sequence_count)
    sequence_ends = jnp.cumsum(lengths_row)
    sequence_starts = sequence_ends - lengths_row
    row_index = jnp.arange(row_count, dtype=jnp.int32)
    one_hot = (sequence_ends[None, :] > row_index[:, None]) & (
        sequence_starts[None, :] <= row_index[:, None]
    )
    row_start = jnp.sum(jnp.where(one_hot, sequence_starts[None, :], 0), axis=1)
    position = row_index - row_start
    row_slot = jnp.sum(jnp.where(one_hot, slot_of[None, :], 0), axis=1)
    adv = jnp.sum(jnp.where(one_hot, seq_advantage[None, :], 0.0), axis=1)[:, None]
    half_width = HD // 2
    frequency = ROPE_BASE ** (-(2.0 * jnp.arange(half_width, dtype=f32)) / HD)
    angles = position.astype(f32)[:, None] * frequency[None, :]
    cos, sin = jnp.cos(angles), jnp.sin(angles)
    cos = jnp.concatenate([cos, cos], axis=1)
    sin = jnp.concatenate([-sin, sin], axis=1)

    start = row_start[:, None]
    arrived_rows = after(arrived_rows, cos, sin, start, adv)
    x_own = jnp.take(
        arrived_rows.reshape(sequence_count * max_len, local_features),
        row_slot * max_len + position,
        axis=0,
        mode="clip",
    )
    x_head, x_tail = x_own[: bounds[1], :], x_own[bounds[1] :, :]
    tail_near = gather_near(x_tail)
    head_near = gather_near(after(x_head, tail_near[0], g_far2))
    tail_far2 = gather_far((after(tail_near[0], g_rows), tail_near[1]), z)
    head_far2 = gather_far((after(head_near[0], tail_far2), head_near[1]), z)

    w_qkv = lax.all_gather(
        jnp.concatenate([w_q, w_k, w_v], axis=1), "fsdp", axis=0, tiled=True
    )
    w_o = lax.all_gather(w_o_t, "fsdp", axis=0, tiled=True)
    gain_f = gain.astype(f32)
    gain_shards = gain_f.reshape(4, 1, local_features)
    w_shards = (w_qkv.astype(f32) * gain_f[:, None]).astype(bf16)
    w_shards = w_shards.reshape(4, local_features, qkv_cols)
    w_k_parts = [lax.dynamic_index_in_dim(w_shards, z ^ k, 0, keepdims=False) for k in range(4)]

    def input_terms(dqkv, scales, parts):
        return [
            (
                scales[:, 0:1] * times_trans(dqkv, w_k_parts[k])
                - parts[k].astype(f32) * (scales[:, 1:2] / feature_count)
            ).astype(bf16)
            for k in range(4)
        ]

    tail_end = gather_end(after(tail_far2, g_end, *head_near))
    tail_shards = shards(x_tail, tail_near, tail_far2, tail_end, z)
    raw1, inv1 = project(tail_shards, w_k_parts, (), feature_count)
    head_end = gather_end(after(head_far2, tail_end))
    w_o = after(w_o, head_far2)
    o_shards = w_o.reshape(4, local_features, q_cols)
    ga = [
        matmul(g_rows, w_o),
        sum(
            matmul(g_shards[k], lax.dynamic_index_in_dim(o_shards, z ^ k, 0, keepdims=False))
            for k in range(4)
        ),
    ]
    head_shards = shards(x_head, head_near, head_far2, after(head_end, raw1, *ga), z)
    raw0, inv0 = project(head_shards, w_k_parts, (), feature_count)
    dqkv0, dqkv1, scales0, scales1, scaled, out = attention(
        (raw0, raw1), (inv0, inv1), ga, adv, cos, sin, start
    )
    half = dqkv0.shape[0]
    terms0 = input_terms(dqkv0, scales0, [x[:half] for x in head_shards])
    end0 = scatter_end(terms0)
    total0 = far_total(terms0, end0)
    step0 = scatter_far(total0)
    dx0 = scatter_near(terms0, step0, z)

    places = jnp.stack([z ^ j for j in range(4)]).astype(jnp.int32)
    weight_terms = weight_grads(
        places,
        head_shards,
        tail_shards,
        g_shards,
        g_rows,
        after(scaled, terms0[3]),
        out,
        gain_shards,
    )
    summed = lax.psum_scatter(after(weight_terms, end0), "fsdp", scatter_dimension=0, tiled=True)

    terms1 = input_terms(
        after(dqkv1, end0),
        scales1,
        [jnp.concatenate([x[half:], y], axis=0) for x, y in zip(head_shards, tail_shards)],
    )
    end1 = scatter_end([*terms1[:3], after(terms1[3], end0)])
    step1 = scatter_far(far_total(terms1, after(end1, *step0)))
    dx1 = scatter_near(terms1, (after(step1[0], dx0), step1[1]), z)
    dx = jnp.concatenate([dx0, dx1], axis=0)
    input_grad = (adv * log_prob_grad.astype(f32) + dx).astype(bf16)
    grad_q = summed[:, :q_cols]
    grad_k = summed[:, q_cols : q_cols + k_cols]
    grad_v = summed[:, q_cols + k_cols : qkv_cols]
    grad_o_t = summed[:, qkv_cols:]
    return (input_grad, grad_q, grad_k, grad_v, grad_o_t)


def solution(mesh):
    in_specs = (
        P("fsdp", None, "tp"),
        P("fsdp"),
        P("fsdp", None),
        P("fsdp"),
        P("fsdp", "tp"),
        P(),
        P("fsdp", "tp"),
        P("fsdp", "tp"),
        P("fsdp", "tp"),
        P("fsdp", "tp"),
    )
    out_specs = (
        P("fsdp", "tp"),
        P("fsdp", "tp"),
        P("fsdp", "tp"),
        P("fsdp", "tp"),
        P("fsdp", "tp"),
    )
    return jax.shard_map(
        per_device, mesh=mesh, in_specs=in_specs, out_specs=out_specs, check_vma=False
    )
```

```python
import functools

import jax
import jax.numpy as jnp
from jax import lax
from jax.experimental import pallas as pl
from jax.experimental.pallas import tpu as pltpu
from jax.sharding import PartitionSpec as P

KEY_VALUE_HEADS = 4
HD = 128
QUERY_HEADS = 16
GSIZE = 16
ROPE_BASE = 1000000.0
NORM_EPSILON = 1e-06
BLOCK = 128

UP = [(0, 1), (1, 2), (2, 3)]
DOWN = [(1, 0), (2, 1), (3, 2)]
UP_MID = [(1, 2), (2, 3)]
DOWN_MID = [(1, 0), (2, 1)]
TO_ENDS = [(2, 3), (1, 0)]
FROM_ENDS = [(3, 2), (0, 1)]
UP_IN = [(0, 1), (1, 2)]
DOWN_IN = [(3, 2), (2, 1)]


def contract_rows(left, right):
    return lax.dot_general(
        left, right, (((0,), (0,)), ((), ())), preferred_element_type=jnp.float32
    )


def times_trans(left, right):
    return lax.dot_general(
        left, right, (((1,), (1,)), ((), ())), preferred_element_type=jnp.float32
    )


def matmul(left, right):
    return jnp.dot(left, right, preferred_element_type=jnp.float32)


def gather_near(own):
    return lax.ppermute(own, "tp", UP), lax.ppermute(own, "tp", DOWN)


def gather_far(step1, z):
    up2 = lax.ppermute(step1[0], "tp", UP_MID)
    down2 = lax.ppermute(step1[1], "tp", DOWN_MID)
    return jnp.where(z >= 2, up2, down2)


def gather_end(far2):
    return lax.ppermute(far2, "tp", TO_ENDS)


def shards(own, step1, far2, far3, z):
    up1, down1 = step1
    near = jnp.where(z % 2 == 1, up1, down1)
    other = jnp.where(z == 1, down1, jnp.where(z == 2, up1, far3))
    return [own, near, far2, other]


def after(value, *earlier):
    return lax.optimization_barrier((value, *earlier))[0]


def scatter_end(parts):
    return lax.ppermute(parts[3], "tp", FROM_ENDS)


def far_total(parts, from_end):
    return (parts[2].astype(jnp.float32) + from_end.astype(jnp.float32)).astype(jnp.bfloat16)


def scatter_far(total2):
    return lax.ppermute(total2, "tp", UP_IN), lax.ppermute(total2, "tp", DOWN_IN)


def scatter_near(parts, step2, z):
    own, near, _, other = parts
    f32 = jnp.float32
    up2, down2 = step2
    go_up = jnp.where(z == 1, other, near).astype(f32) + up2.astype(f32)
    go_down = jnp.where(z == 2, other, near).astype(f32) + down2.astype(f32)
    up3 = lax.ppermute(go_up.astype(jnp.bfloat16), "tp", UP)
    down3 = lax.ppermute(go_down.astype(jnp.bfloat16), "tp", DOWN)
    return own.astype(f32) + up3.astype(f32) + down3.astype(f32)


def attention_kernel(*refs):
    raw_refs, inv_refs, ga_refs = refs[:2], refs[2:4], refs[4:6]
    adv_ref, cos_ref, sin_ref, start_ref = refs[6:10]
    dqkv_ref, scale_ref, dscaled_ref, out_ref, qkv_b, dk_acc, dv_acc = refs[10:]
    heads = ga_refs[0].shape[1] // HD
    qw = heads * HD
    scale = HD ** (-0.5)
    f32, bf16 = jnp.float32, jnp.bfloat16
    pieces = list(zip(raw_refs, inv_refs, ga_refs, (0, raw_refs[0].shape[0])))
    edge = pl.ds(0, BLOCK)
    qkv_b[edge, :] = jnp.zeros((BLOCK, qkv_b.shape[1]), bf16)
    dk_acc[edge, :] = jnp.zeros((BLOCK, HD), f32)
    dv_acc[edge, :] = jnp.zeros((BLOCK, HD), f32)

    def turn(value, cos, sin):
        return value * cos + pltpu.roll(value, HD // 2, 1) * sin

    def rows_of(block, first):
        base = pl.multiple_of(block * BLOCK, BLOCK)
        return base + first, pl.ds(base, BLOCK), pl.ds(base + first, BLOCK)

    def forward_and_back(raw_ref, inv_ref, ga_ref, first, block, carry):
        base, local, here = rows_of(block, first)
        after = pl.ds(base + BLOCK, BLOCK)
        both = pl.ds(base, 2 * BLOCK)
        cos, sin = cos_ref[here, :], sin_ref[here, :]
        inv = inv_ref[local, :]
        for h in range(heads + 2):
            cols = slice(h * HD, (h + 1) * HD)
            linear = raw_ref[local, cols] * inv
            qkv_b[after, cols] = (turn(linear, cos, sin) if h <= heads else linear).astype(bf16)
        adv = adv_ref[here, :]
        qs = jnp.concatenate(
            [qkv_b[after, h * HD : (h + 1) * HD] for h in range(heads)], axis=0
        )
        gs = jnp.concatenate(
            [(ga_ref[local, h * HD : (h + 1) * HD] * adv).astype(bf16) for h in range(heads)],
            axis=0,
        )
        ks = qkv_b[both, qw : qw + HD]
        vs = qkv_b[both, qw + HD : qw + 2 * HD]
        start = start_ref[here, :] - (base - BLOCK)
        col = lax.broadcasted_iota(jnp.int32, (BLOCK, 2 * BLOCK), 1)
        row = lax.broadcasted_iota(jnp.int32, (BLOCK, 2 * BLOCK), 0) + BLOCK
        bias = jnp.where((col >= start) & (col <= row), 0.0, -1e30)
        bias = jnp.concatenate([bias] * heads, axis=0)
        scores = times_trans(qs, ks) * scale + bias
        top = jnp.max(scores, axis=-1, keepdims=True)
        weight = jnp.exp(scores - top)
        prob = weight / jnp.sum(weight, axis=-1, keepdims=True)
        prob_b = prob.astype(bf16)
        out = matmul(prob_b, vs)
        grad_prob = times_trans(gs, vs)
        delta = jnp.sum(prob * grad_prob, axis=-1, keepdims=True)
        ds = (prob * (grad_prob - delta) * scale).astype(bf16)
        dq = matmul(ds, ks)
        dk_acc[here, :] += contract_rows(ds[:, :BLOCK], qs)
        dk_acc[after, :] = contract_rows(ds[:, BLOCK:], qs)
        dv_acc[here, :] += contract_rows(prob_b[:, :BLOCK], gs)
        dv_acc[after, :] = contract_rows(prob_b[:, BLOCK:], gs)
        for h in range(heads):
            cols = slice(h * HD, (h + 1) * HD)
            part = slice(h * BLOCK, (h + 1) * BLOCK)
            out_ref[here, cols] = (out[part, :].astype(bf16).astype(f32) * adv).astype(bf16)
            dqkv_ref[here, cols] = turn(dq[part, :], cos, -sin).astype(bf16)
        return carry

    def finish(raw_ref, inv_ref, ga_ref, first, block, carry):
        base, local, here = rows_of(block, first)
        after = pl.ds(base + BLOCK, BLOCK)
        inv = inv_ref[local, :]
        total = jnp.zeros((BLOCK, 1), f32)
        for h in range(heads + 2):
            cols = slice(h * HD, (h + 1) * HD)
            if h < heads:
                grad = dqkv_ref[here, cols]
            elif h == heads:
                grad = turn(dk_acc[after, :], cos_ref[here, :], -sin_ref[here, :]).astype(bf16)
                dqkv_ref[here, cols] = grad
            else:
                grad = dv_acc[after, :].astype(bf16)
                dqkv_ref[here, cols] = grad
            grad = grad.astype(f32) * inv
            dscaled_ref[here, cols] = grad.astype(bf16)
            total += jnp.sum(grad * raw_ref[local, cols], axis=-1, keepdims=True)
        scale_ref[here, 0:1] = inv
        scale_ref[here, 1:2] = inv * inv * total
        return carry

    for body in (forward_and_back, finish):
        for piece in pieces:
            lax.fori_loop(0, piece[0].shape[0] // BLOCK, functools.partial(body, *piece), 0)


def attention(raw, inv, ga, adv, cos, sin, start):
    rows, width = adv.shape[0], raw[0].shape[1]
    qw = ga[0].shape[1]
    f32, bf16 = jnp.float32, jnp.bfloat16
    out_shape = [
        jax.ShapeDtypeStruct((rows, width), bf16),
        jax.ShapeDtypeStruct((rows, 2), f32),
        jax.ShapeDtypeStruct((rows, width), bf16),
        jax.ShapeDtypeStruct((rows, qw), bf16),
    ]
    operands = [*raw, *inv, *ga, adv, cos, sin, start]
    vmem = pl.BlockSpec(memory_space=pltpu.VMEM)
    return pl.pallas_call(
        attention_kernel,
        out_shape=out_shape,
        in_specs=[vmem] * len(operands),
        out_specs=[vmem] * len(out_shape),
        scratch_shapes=[
            pltpu.VMEM((rows + BLOCK, width), bf16),
            pltpu.VMEM((rows + BLOCK, HD), f32),
            pltpu.VMEM((rows + BLOCK, HD), f32),
        ],
        compiler_params=pltpu.CompilerParams(vmem_limit_bytes=14 * 1024 * 1024),
        cost_estimate=pl.CostEstimate(
            flops=rows * 2 * BLOCK * HD * 12 * (qw // HD),
            bytes_accessed=rows * width * 8 + rows * qw * 6,
            transcendentals=rows * 2 * BLOCK * (qw // HD),
        ),
        name="attention",
    )(*operands)


def project_kernel(count, feature_count, *refs):
    x_refs, w_refs = refs[:count], refs[count : 2 * count]
    raw_ref, square_ref = refs[-2:]
    raw, squares = None, None
    if len(refs) > 2 * count + 2:
        raw, squares = refs[2 * count][...], refs[2 * count + 1][...]
    for x_ref, w_ref in zip(x_refs, w_refs):
        part = matmul(x_ref[...], w_ref[...])
        raw = part if raw is None else raw + part
        wide = x_ref[...].astype(jnp.float32)
        part = jnp.sum(wide * wide, axis=1, keepdims=True)
        squares = part if squares is None else squares + part
    raw_ref[...] = raw
    if feature_count:
        squares = lax.rsqrt(squares / feature_count + NORM_EPSILON)
    square_ref[...] = squares


def project(parts, weights, prior, feature_count):
    rows, width = parts[0].shape[0], weights[0].shape[1]
    operands = [*parts, *weights, *prior]
    vmem = pl.BlockSpec(memory_space=pltpu.VMEM)
    return pl.pallas_call(
        functools.partial(project_kernel, len(parts), feature_count),
        out_shape=[
            jax.ShapeDtypeStruct((rows, width), jnp.float32),
            jax.ShapeDtypeStruct((rows, 1), jnp.float32),
        ],
        in_specs=[vmem] * len(operands),
        out_specs=[vmem] * 2,
        compiler_params=pltpu.CompilerParams(vmem_limit_bytes=12 * 1024 * 1024),
        cost_estimate=pl.CostEstimate(
            flops=2 * len(parts) * rows * width * parts[0].shape[1],
            bytes_accessed=2 * len(parts) * parts[0].shape[1] * (rows + width) + 8 * rows * width,
            transcendentals=rows,
        ),
        name="project",
    )(*operands)


def weight_grad_kernel(place_ref, *refs):
    heads, tails, g_tails = refs[:4], refs[4:8], refs[8:12]
    g_ref, scaled_ref, out_ref, gain_ref, term_ref = refs[12:]
    width = scaled_ref.shape[1]
    gain = gain_ref[0]
    gain = jnp.transpose(jnp.broadcast_to(gain, (HD, gain.shape[1])))[:, 0:1]
    first = g_ref.shape[0]
    for k in range(4):

        @pl.when(place_ref[pl.program_id(0)] == k)
        def _():
            total = contract_rows(heads[k][...], scaled_ref[:first, :])
            total += contract_rows(tails[k][...], scaled_ref[first:, :])
            term_ref[:, :width] = (total * gain).astype(jnp.bfloat16)
            total = contract_rows(g_ref[...], out_ref[:first, :])
            total += contract_rows(g_tails[k][...], out_ref[first:, :])
            term_ref[:, width:] = total.astype(jnp.bfloat16)


def weight_grads(places, heads, tails, g_tails, g_rows, scaled, out, gain):
    features = gain.shape[2]
    width = scaled.shape[1] + out.shape[1]
    x_parts = [*heads, *tails, *g_tails]

    def once(o):
        return pl.BlockSpec(o.shape, lambda j, place: (0, 0), pipeline_mode=pl.Buffered(1))

    return pl.pallas_call(
        weight_grad_kernel,
        out_shape=jax.ShapeDtypeStruct((4 * features, width), jnp.bfloat16),
        grid_spec=pltpu.PrefetchScalarGridSpec(
            num_scalar_prefetch=1,
            grid=(4,),
            in_specs=[once(o) for o in x_parts]
            + [pl.BlockSpec((g_rows.shape[0], features), lambda j, place: (0, j))]
            + [once(scaled), once(out)]
            + [pl.BlockSpec((1, 1, features), lambda j, place: (j, 0, 0))],
            out_specs=pl.BlockSpec((features, width), lambda j, place: (j, 0)),
        ),
        compiler_params=pltpu.CompilerParams(vmem_limit_bytes=40 * 1024 * 1024),
        cost_estimate=pl.CostEstimate(
            flops=2 * scaled.shape[0] * 4 * features * width,
            bytes_accessed=4 * features * (4 * scaled.shape[0] + 2 * width),
            transcendentals=0,
        ),
        name="weight_grads",
    )(places, *x_parts, g_rows, scaled, out, gain)


def per_device(roll_rows, dest, lengths, clusters, log_prob_grad, gain, w_q, w_k, w_v, w_o_t):
    sequence_count = dest.shape[0]
    max_len, local_features = roll_rows.shape[1:]
    row_count = log_prob_grad.shape[0]
    replicas = lax.axis_size("fsdp")
    per_pair = sequence_count // replicas
    me = lax.axis_index("fsdp")
    z = lax.axis_index("tp")
    f32, bf16 = jnp.float32, jnp.bfloat16
    q_cols, k_cols = w_q.shape[1], w_k.shape[1]
    qkv_cols = q_cols + 2 * k_cols
    feature_count = gain.shape[0]

    bounds = [0, row_count - 2 * BLOCK, row_count]
    g_rows = lax.all_gather(log_prob_grad[: bounds[1], :], "tp", axis=1, tiled=True)
    g_tail = log_prob_grad[bounds[1] :, :]
    g_near = gather_near(g_tail)
    g_far2 = gather_far(g_near, z)
    g_end = gather_end(g_far2)
    g_shards = shards(g_tail, g_near, g_far2, g_end, z)

    slot_ids = jnp.arange(sequence_count, dtype=jnp.int32)
    earlier_dest = dest[None, :] < dest[:, None]
    send_block = jnp.sum(earlier_dest.astype(jnp.int32), axis=1)
    source = jnp.sum(
        jnp.where(send_block[None, :] == slot_ids[:, None], slot_ids[None, :], 0), axis=1
    )
    send_rows = jnp.take(roll_rows, source, axis=0, mode="clip")
    arrived_rows = lax.all_to_all(send_rows, "fsdp", split_axis=0, concat_axis=0, tiled=True)

    ballots = clusters.reshape(sequence_count // GSIZE, GSIZE)
    vote_share = jnp.mean((ballots[:, :, None] == ballots[:, None, :]).astype(f32), axis=2)
    advantage = (vote_share - jnp.mean(vote_share, axis=1, keepdims=True)).reshape(sequence_count)
    tags = jnp.stack([(dest % sequence_count).astype(f32), advantage], axis=1)
    picked = send_block[None, :] == slot_ids[:, None]
    tags = jnp.sum(jnp.where(picked[:, :, None], tags[None, :, :], 0.0), axis=1).astype(bf16)
    tags = lax.all_to_all(tags, "fsdp", split_axis=0, concat_axis=0, tiled=True).astype(f32)
    holder = tags[None, :, 0].astype(jnp.int32) == slot_ids[:, None]
    slot_of = jnp.sum(jnp.where(holder, slot_ids[None, :], 0), axis=1)
    seq_advantage = jnp.sum(jnp.where(holder, tags[None, :, 1], 0.0), axis=1)

    lengths_row = lengths.reshape(sequence_count)
    sequence_ends = jnp.cumsum(lengths_row)
    sequence_starts = sequence_ends - lengths_row
    row_index = jnp.arange(row_count, dtype=jnp.int32)
    one_hot = (sequence_ends[None, :] > row_index[:, None]) & (
        sequence_starts[None, :] <= row_index[:, None]
    )
    row_start = jnp.sum(jnp.where(one_hot, sequence_starts[None, :], 0), axis=1)
    position = row_index - row_start
    row_slot = jnp.sum(jnp.where(one_hot, slot_of[None, :], 0), axis=1)
    adv = jnp.sum(jnp.where(one_hot, seq_advantage[None, :], 0.0), axis=1)[:, None]
    half_width = HD // 2
    frequency = ROPE_BASE ** (-(2.0 * jnp.arange(half_width, dtype=f32)) / HD)
    angles = position.astype(f32)[:, None] * frequency[None, :]
    cos, sin = jnp.cos(angles), jnp.sin(angles)
    cos = jnp.concatenate([cos, cos], axis=1)
    sin = jnp.concatenate([-sin, sin], axis=1)

    start = row_start[:, None]
    arrived_rows = after(arrived_rows, cos, sin, start, adv)
    x_own = jnp.take(
        arrived_rows.reshape(sequence_count * max_len, local_features),
        row_slot * max_len + position,
        axis=0,
        mode="clip",
    )
    x_head, x_tail = x_own[: bounds[1], :], x_own[bounds[1] :, :]
    tail_near = gather_near(x_tail)
    head_near = gather_near(after(x_head, tail_near[0], g_far2))
    tail_far2 = gather_far((after(tail_near[0], g_rows), tail_near[1]), z)
    head_far2 = gather_far((after(head_near[0], tail_far2), head_near[1]), z)

    w_qkv = lax.all_gather(
        jnp.concatenate([w_q, w_k, w_v], axis=1), "fsdp", axis=0, tiled=True
    )
    w_o = lax.all_gather(w_o_t, "fsdp", axis=0, tiled=True)
    gain_f = gain.astype(f32)
    gain_shards = gain_f.reshape(4, 1, local_features)
    w_shards = (w_qkv.astype(f32) * gain_f[:, None]).astype(bf16)
    w_shards = w_shards.reshape(4, local_features, qkv_cols)
    w_k_parts = [lax.dynamic_index_in_dim(w_shards, z ^ k, 0, keepdims=False) for k in range(4)]

    def input_terms(dqkv, scales, parts):
        return [
            (
                scales[:, 0:1] * times_trans(dqkv, w_k_parts[k])
                - parts[k].astype(f32) * (scales[:, 1:2] / feature_count)
            ).astype(bf16)
            for k in range(4)
        ]

    tail_end = gather_end(after(tail_far2, g_end, *head_near))
    tail_shards = shards(x_tail, tail_near, tail_far2, tail_end, z)
    raw1, inv1 = project(tail_shards, w_k_parts, (), feature_count)
    head_end = gather_end(after(head_far2, tail_end))
    w_o = after(w_o, head_far2)
    o_shards = w_o.reshape(4, local_features, q_cols)
    ga = [
        matmul(g_rows, w_o),
        sum(
            matmul(g_shards[k], lax.dynamic_index_in_dim(o_shards, z ^ k, 0, keepdims=False))
            for k in range(4)
        ),
    ]
    head_shards = shards(x_head, head_near, head_far2, after(head_end, raw1, *ga), z)
    raw0, inv0 = project(head_shards, w_k_parts, (), feature_count)
    dqkv, scales, scaled, out = attention(
        (raw0, raw1), (inv0, inv1), ga, adv, cos, sin, start
    )
    half = row_count // (2 * BLOCK) * BLOCK
    terms0 = input_terms(dqkv[:half], scales[:half], [x[:half] for x in head_shards])
    end0 = scatter_end(terms0)
    total0 = far_total(terms0, end0)
    step0 = scatter_far(total0)
    dx0 = scatter_near(terms0, step0, z)

    places = jnp.stack([z ^ j for j in range(4)]).astype(jnp.int32)
    weight_terms = weight_grads(
        places,
        head_shards,
        tail_shards,
        g_shards,
        g_rows,
        after(scaled, terms0[3]),
        out,
        gain_shards,
    )
    summed = lax.psum_scatter(after(weight_terms, end0), "fsdp", scatter_dimension=0, tiled=True)

    terms1 = input_terms(
        after(dqkv[half:], end0),
        scales[half:],
        [jnp.concatenate([x[half:], y], axis=0) for x, y in zip(head_shards, tail_shards)],
    )
    end1 = scatter_end([*terms1[:3], after(terms1[3], end0)])
    step1 = scatter_far(far_total(terms1, after(end1, *step0)))
    dx1 = scatter_near(terms1, (after(step1[0], dx0), step1[1]), z)
    dx = jnp.concatenate([dx0, dx1], axis=0)
    input_grad = (adv * log_prob_grad.astype(f32) + dx).astype(bf16)
    grad_q = summed[:, :q_cols]
    grad_k = summed[:, q_cols : q_cols + k_cols]
    grad_v = summed[:, q_cols + k_cols : qkv_cols]
    grad_o_t = summed[:, qkv_cols:]
    return (input_grad, grad_q, grad_k, grad_v, grad_o_t)


def solution(mesh):
    in_specs = (
        P("fsdp", None, "tp"),
        P("fsdp"),
        P("fsdp", None),
        P("fsdp"),
        P("fsdp", "tp"),
        P(),
        P("fsdp", "tp"),
        P("fsdp", "tp"),
        P("fsdp", "tp"),
        P("fsdp", "tp"),
    )
    out_specs = (
        P("fsdp", "tp"),
        P("fsdp", "tp"),
        P("fsdp", "tp"),
        P("fsdp", "tp"),
        P("fsdp", "tp"),
    )
    return jax.shard_map(
        per_device, mesh=mesh, in_specs=in_specs, out_specs=out_specs, check_vma=False
    )
```

```python
import functools

import jax
import jax.numpy as jnp
from jax import lax
from jax.experimental import pallas as pl
from jax.experimental.pallas import tpu as pltpu
from jax.sharding import PartitionSpec as P

KEY_VALUE_HEADS = 4
HD = 128
QUERY_HEADS = 16
GSIZE = 16
ROPE_BASE = 1000000.0
NORM_EPSILON = 1e-06
BLOCK = 128

UP = [(0, 1), (1, 2), (2, 3)]
DOWN = [(1, 0), (2, 1), (3, 2)]
UP_MID = [(1, 2), (2, 3)]
DOWN_MID = [(1, 0), (2, 1)]
TO_ENDS = [(2, 3), (1, 0)]
FROM_ENDS = [(3, 2), (0, 1)]
UP_IN = [(0, 1), (1, 2)]
DOWN_IN = [(3, 2), (2, 1)]


def contract_rows(left, right):
    return lax.dot_general(
        left, right, (((0,), (0,)), ((), ())), preferred_element_type=jnp.float32
    )


def times_trans(left, right):
    return lax.dot_general(
        left, right, (((1,), (1,)), ((), ())), preferred_element_type=jnp.float32
    )


def matmul(left, right):
    return jnp.dot(left, right, preferred_element_type=jnp.float32)


def gather_near(own):
    return lax.ppermute(own, "tp", UP), lax.ppermute(own, "tp", DOWN)


def gather_far(step1, z):
    up2 = lax.ppermute(step1[0], "tp", UP_MID)
    down2 = lax.ppermute(step1[1], "tp", DOWN_MID)
    return jnp.where(z >= 2, up2, down2)


def gather_end(far2):
    return lax.ppermute(far2, "tp", TO_ENDS)


def shards(own, step1, far2, far3, z):
    up1, down1 = step1
    near = jnp.where(z % 2 == 1, up1, down1)
    other = jnp.where(z == 1, down1, jnp.where(z == 2, up1, far3))
    return [own, near, far2, other]


def after(value, *earlier):
    return lax.optimization_barrier((value, *earlier))[0]


def scatter_end(parts):
    return lax.ppermute(parts[3], "tp", FROM_ENDS)


def far_total(parts, from_end):
    return (parts[2].astype(jnp.float32) + from_end.astype(jnp.float32)).astype(jnp.bfloat16)


def scatter_far(total2):
    return lax.ppermute(total2, "tp", UP_IN), lax.ppermute(total2, "tp", DOWN_IN)


def scatter_near(parts, step2, z):
    own, near, _, other = parts
    f32 = jnp.float32
    up2, down2 = step2
    go_up = jnp.where(z == 1, other, near).astype(f32) + up2.astype(f32)
    go_down = jnp.where(z == 2, other, near).astype(f32) + down2.astype(f32)
    up3 = lax.ppermute(go_up.astype(jnp.bfloat16), "tp", UP)
    down3 = lax.ppermute(go_down.astype(jnp.bfloat16), "tp", DOWN)
    return own.astype(f32) + up3.astype(f32) + down3.astype(f32)


def attention_kernel(*refs):
    raw_refs, inv_refs, ga_refs = refs[:2], refs[2:4], refs[4:6]
    adv_ref, cos_ref, sin_ref, start_ref = refs[6:10]
    dqkv_ref, scale_ref, dscaled_ref, out_ref, qkv_b, dk_acc, dv_acc = refs[10:]
    heads = ga_refs[0].shape[1] // HD
    qw = heads * HD
    scale = HD ** (-0.5)
    f32, bf16 = jnp.float32, jnp.bfloat16
    pieces = list(zip(raw_refs, inv_refs, ga_refs, (0, raw_refs[0].shape[0])))
    edge = pl.ds(0, BLOCK)
    qkv_b[edge, :] = jnp.zeros((BLOCK, qkv_b.shape[1]), bf16)
    dk_acc[edge, :] = jnp.zeros((BLOCK, HD), f32)
    dv_acc[edge, :] = jnp.zeros((BLOCK, HD), f32)

    def turn(value, cos, sin):
        return value * cos + pltpu.roll(value, HD // 2, 1) * sin

    def rows_of(block, first):
        base = pl.multiple_of(block * BLOCK, BLOCK)
        return base + first, pl.ds(base, BLOCK), pl.ds(base + first, BLOCK)

    def forward_and_back(raw_ref, inv_ref, ga_ref, first, block, carry):
        base, local, here = rows_of(block, first)
        after = pl.ds(base + BLOCK, BLOCK)
        both = pl.ds(base, 2 * BLOCK)
        cos, sin = cos_ref[here, :], sin_ref[here, :]
        inv = inv_ref[local, :]
        for h in range(heads + 2):
            cols = slice(h * HD, (h + 1) * HD)
            linear = raw_ref[local, cols] * inv
            qkv_b[after, cols] = (turn(linear, cos, sin) if h <= heads else linear).astype(bf16)
        adv = adv_ref[here, :]
        qs = jnp.concatenate(
            [qkv_b[after, h * HD : (h + 1) * HD] for h in range(heads)], axis=0
        )
        gs = jnp.concatenate(
            [(ga_ref[local, h * HD : (h + 1) * HD] * adv).astype(bf16) for h in range(heads)],
            axis=0,
        )
        ks = qkv_b[both, qw : qw + HD]
        vs = qkv_b[both, qw + HD : qw + 2 * HD]
        start = start_ref[here, :] - (base - BLOCK)
        col = lax.broadcasted_iota(jnp.int32, (BLOCK, 2 * BLOCK), 1)
        row = lax.broadcasted_iota(jnp.int32, (BLOCK, 2 * BLOCK), 0) + BLOCK
        bias = jnp.where((col >= start) & (col <= row), 0.0, -1e30)
        bias = jnp.concatenate([bias] * heads, axis=0)
        scores = times_trans(qs, ks) * scale + bias
        top = jnp.max(scores, axis=-1, keepdims=True)
        weight = jnp.exp(scores - top)
        prob = weight / jnp.sum(weight, axis=-1, keepdims=True)
        prob_b = prob.astype(bf16)
        out = matmul(prob_b, vs)
        grad_prob = times_trans(gs, vs)
        delta = jnp.sum(prob * grad_prob, axis=-1, keepdims=True)
        ds = (prob * (grad_prob - delta) * scale).astype(bf16)
        dq = matmul(ds, ks)
        dk_acc[here, :] += contract_rows(ds[:, :BLOCK], qs)
        dk_acc[after, :] = contract_rows(ds[:, BLOCK:], qs)
        dv_acc[here, :] += contract_rows(prob_b[:, :BLOCK], gs)
        dv_acc[after, :] = contract_rows(prob_b[:, BLOCK:], gs)
        for h in range(heads):
            cols = slice(h * HD, (h + 1) * HD)
            part = slice(h * BLOCK, (h + 1) * BLOCK)
            out_ref[here, cols] = (out[part, :].astype(bf16).astype(f32) * adv).astype(bf16)
            dqkv_ref[here, cols] = turn(dq[part, :], cos, -sin).astype(bf16)
        return carry

    def finish(raw_ref, inv_ref, ga_ref, first, block, carry):
        base, local, here = rows_of(block, first)
        after = pl.ds(base + BLOCK, BLOCK)
        inv = inv_ref[local, :]
        total = jnp.zeros((BLOCK, 1), f32)
        for h in range(heads + 2):
            cols = slice(h * HD, (h + 1) * HD)
            if h < heads:
                grad = dqkv_ref[here, cols]
            elif h == heads:
                grad = turn(dk_acc[after, :], cos_ref[here, :], -sin_ref[here, :]).astype(bf16)
                dqkv_ref[here, cols] = grad
            else:
                grad = dv_acc[after, :].astype(bf16)
                dqkv_ref[here, cols] = grad
            grad = grad.astype(f32) * inv
            dscaled_ref[here, cols] = grad.astype(bf16)
            total += jnp.sum(grad * raw_ref[local, cols], axis=-1, keepdims=True)
        scale_ref[here, 0:1] = inv
        scale_ref[here, 1:2] = inv * inv * total
        return carry

    for body in (forward_and_back, finish):
        for piece in pieces:
            lax.fori_loop(0, piece[0].shape[0] // BLOCK, functools.partial(body, *piece), 0)


def attention(raw, inv, ga, adv, cos, sin, start):
    rows, width = adv.shape[0], raw[0].shape[1]
    qw = ga[0].shape[1]
    f32, bf16 = jnp.float32, jnp.bfloat16
    out_shape = [
        jax.ShapeDtypeStruct((rows, width), bf16),
        jax.ShapeDtypeStruct((rows, 2), f32),
        jax.ShapeDtypeStruct((rows, width), bf16),
        jax.ShapeDtypeStruct((rows, qw), bf16),
    ]
    operands = [*raw, *inv, *ga, adv, cos, sin, start]
    vmem = pl.BlockSpec(memory_space=pltpu.VMEM)
    return pl.pallas_call(
        attention_kernel,
        out_shape=out_shape,
        in_specs=[vmem] * len(operands),
        out_specs=[vmem] * len(out_shape),
        scratch_shapes=[
            pltpu.VMEM((rows + BLOCK, width), bf16),
            pltpu.VMEM((rows + BLOCK, HD), f32),
            pltpu.VMEM((rows + BLOCK, HD), f32),
        ],
        compiler_params=pltpu.CompilerParams(vmem_limit_bytes=14 * 1024 * 1024),
        cost_estimate=pl.CostEstimate(
            flops=rows * 2 * BLOCK * HD * 12 * (qw // HD),
            bytes_accessed=rows * width * 8 + rows * qw * 6,
            transcendentals=rows * 2 * BLOCK * (qw // HD),
        ),
        name="attention",
    )(*operands)


def project_kernel(count, feature_count, *refs):
    x_refs, w_refs = refs[:count], refs[count : 2 * count]
    raw_ref, square_ref = refs[-2:]
    raw, squares = None, None
    if len(refs) > 2 * count + 2:
        raw, squares = refs[2 * count][...], refs[2 * count + 1][...]
    for x_ref, w_ref in zip(x_refs, w_refs):
        part = matmul(x_ref[...], w_ref[...])
        raw = part if raw is None else raw + part
        wide = x_ref[...].astype(jnp.float32)
        part = jnp.sum(wide * wide, axis=1, keepdims=True)
        squares = part if squares is None else squares + part
    raw_ref[...] = raw
    if feature_count:
        squares = lax.rsqrt(squares / feature_count + NORM_EPSILON)
    square_ref[...] = squares


def project(parts, weights, prior, feature_count):
    rows, width = parts[0].shape[0], weights[0].shape[1]
    operands = [*parts, *weights, *prior]
    vmem = pl.BlockSpec(memory_space=pltpu.VMEM)
    return pl.pallas_call(
        functools.partial(project_kernel, len(parts), feature_count),
        out_shape=[
            jax.ShapeDtypeStruct((rows, width), jnp.float32),
            jax.ShapeDtypeStruct((rows, 1), jnp.float32),
        ],
        in_specs=[vmem] * len(operands),
        out_specs=[vmem] * 2,
        compiler_params=pltpu.CompilerParams(vmem_limit_bytes=12 * 1024 * 1024),
        cost_estimate=pl.CostEstimate(
            flops=2 * len(parts) * rows * width * parts[0].shape[1],
            bytes_accessed=2 * len(parts) * parts[0].shape[1] * (rows + width) + 8 * rows * width,
            transcendentals=rows,
        ),
        name="project",
    )(*operands)


def weight_grad_kernel(place_ref, *refs):
    heads, tails, g_tails = refs[:4], refs[4:8], refs[8:12]
    g_ref, scaled_ref, out_ref, gain_ref, term_ref = refs[12:]
    width = scaled_ref.shape[1]
    gain = gain_ref[0]
    gain = jnp.transpose(jnp.broadcast_to(gain, (HD, gain.shape[1])))[:, 0:1]
    first = g_ref.shape[0]
    for k in range(4):

        @pl.when(place_ref[pl.program_id(0)] == k)
        def _():
            total = contract_rows(heads[k][...], scaled_ref[:first, :])
            total += contract_rows(tails[k][...], scaled_ref[first:, :])
            term_ref[:, :width] = (total * gain).astype(jnp.bfloat16)
            total = contract_rows(g_ref[...], out_ref[:first, :])
            total += contract_rows(g_tails[k][...], out_ref[first:, :])
            term_ref[:, width:] = total.astype(jnp.bfloat16)


def weight_grads(places, heads, tails, g_tails, g_rows, scaled, out, gain):
    features = gain.shape[2]
    width = scaled.shape[1] + out.shape[1]
    x_parts = [*heads, *tails, *g_tails]

    def once(o):
        return pl.BlockSpec(o.shape, lambda j, place: (0, 0), pipeline_mode=pl.Buffered(1))

    return pl.pallas_call(
        weight_grad_kernel,
        out_shape=jax.ShapeDtypeStruct((4 * features, width), jnp.bfloat16),
        grid_spec=pltpu.PrefetchScalarGridSpec(
            num_scalar_prefetch=1,
            grid=(4,),
            in_specs=[once(o) for o in x_parts]
            + [pl.BlockSpec((g_rows.shape[0], features), lambda j, place: (0, j))]
            + [once(scaled), once(out)]
            + [pl.BlockSpec((1, 1, features), lambda j, place: (j, 0, 0))],
            out_specs=pl.BlockSpec((features, width), lambda j, place: (j, 0)),
        ),
        compiler_params=pltpu.CompilerParams(vmem_limit_bytes=58 * 1024 * 1024),
        cost_estimate=pl.CostEstimate(
            flops=2 * scaled.shape[0] * 4 * features * width,
            bytes_accessed=4 * features * (4 * scaled.shape[0] + 2 * width),
            transcendentals=0,
        ),
        name="weight_grads",
    )(places, *x_parts, g_rows, scaled, out, gain)


def per_device(roll_rows, dest, lengths, clusters, log_prob_grad, gain, w_q, w_k, w_v, w_o_t):
    sequence_count = dest.shape[0]
    max_len, local_features = roll_rows.shape[1:]
    row_count = log_prob_grad.shape[0]
    replicas = lax.axis_size("fsdp")
    per_pair = sequence_count // replicas
    me = lax.axis_index("fsdp")
    z = lax.axis_index("tp")
    f32, bf16 = jnp.float32, jnp.bfloat16
    q_cols, k_cols = w_q.shape[1], w_k.shape[1]
    qkv_cols = q_cols + 2 * k_cols
    feature_count = gain.shape[0]

    bounds = [0, row_count - 2 * BLOCK, row_count]
    g_rows = lax.all_gather(log_prob_grad[: bounds[1], :], "tp", axis=1, tiled=True)
    g_tail = log_prob_grad[bounds[1] :, :]
    g_near = gather_near(g_tail)
    g_far2 = gather_far(g_near, z)
    g_end = gather_end(g_far2)
    g_shards = shards(g_tail, g_near, g_far2, g_end, z)

    slot_ids = jnp.arange(sequence_count, dtype=jnp.int32)
    earlier_dest = dest[None, :] < dest[:, None]
    send_block = jnp.sum(earlier_dest.astype(jnp.int32), axis=1)
    source = jnp.sum(
        jnp.where(send_block[None, :] == slot_ids[:, None], slot_ids[None, :], 0), axis=1
    )
    send_rows = jnp.take(roll_rows, source, axis=0, mode="clip")
    arrived_rows = lax.all_to_all(send_rows, "fsdp", split_axis=0, concat_axis=0, tiled=True)

    ballots = clusters.reshape(sequence_count // GSIZE, GSIZE)
    vote_share = jnp.mean((ballots[:, :, None] == ballots[:, None, :]).astype(f32), axis=2)
    advantage = (vote_share - jnp.mean(vote_share, axis=1, keepdims=True)).reshape(sequence_count)
    tags = jnp.stack([(dest % sequence_count).astype(f32), advantage], axis=1)
    picked = send_block[None, :] == slot_ids[:, None]
    tags = jnp.sum(jnp.where(picked[:, :, None], tags[None, :, :], 0.0), axis=1).astype(bf16)
    tags = lax.all_to_all(tags, "fsdp", split_axis=0, concat_axis=0, tiled=True).astype(f32)
    holder = tags[None, :, 0].astype(jnp.int32) == slot_ids[:, None]
    slot_of = jnp.sum(jnp.where(holder, slot_ids[None, :], 0), axis=1)
    seq_advantage = jnp.sum(jnp.where(holder, tags[None, :, 1], 0.0), axis=1)

    lengths_row = lengths.reshape(sequence_count)
    sequence_ends = jnp.cumsum(lengths_row)
    sequence_starts = sequence_ends - lengths_row
    row_index = jnp.arange(row_count, dtype=jnp.int32)
    one_hot = (sequence_ends[None, :] > row_index[:, None]) & (
        sequence_starts[None, :] <= row_index[:, None]
    )
    row_start = jnp.sum(jnp.where(one_hot, sequence_starts[None, :], 0), axis=1)
    position = row_index - row_start
    row_slot = jnp.sum(jnp.where(one_hot, slot_of[None, :], 0), axis=1)
    adv = jnp.sum(jnp.where(one_hot, seq_advantage[None, :], 0.0), axis=1)[:, None]
    half_width = HD // 2
    frequency = ROPE_BASE ** (-(2.0 * jnp.arange(half_width, dtype=f32)) / HD)
    angles = position.astype(f32)[:, None] * frequency[None, :]
    cos, sin = jnp.cos(angles), jnp.sin(angles)
    cos = jnp.concatenate([cos, cos], axis=1)
    sin = jnp.concatenate([-sin, sin], axis=1)

    start = row_start[:, None]
    arrived_rows = after(arrived_rows, cos, sin, start, adv)
    x_own = jnp.take(
        arrived_rows.reshape(sequence_count * max_len, local_features),
        row_slot * max_len + position,
        axis=0,
        mode="clip",
    )
    x_head, x_tail = x_own[: bounds[1], :], x_own[bounds[1] :, :]
    tail_near = gather_near(x_tail)
    head_near = gather_near(after(x_head, tail_near[0], g_far2))
    tail_far2 = gather_far((after(tail_near[0], g_rows), tail_near[1]), z)
    head_far2 = gather_far((after(head_near[0], tail_far2), head_near[1]), z)

    w_qkv = lax.all_gather(
        jnp.concatenate([w_q, w_k, w_v], axis=1), "fsdp", axis=0, tiled=True
    )
    w_o = lax.all_gather(w_o_t, "fsdp", axis=0, tiled=True)
    gain_f = gain.astype(f32)
    gain_shards = gain_f.reshape(4, 1, local_features)
    w_shards = (w_qkv.astype(f32) * gain_f[:, None]).astype(bf16)
    w_shards = w_shards.reshape(4, local_features, qkv_cols)
    w_k_parts = [lax.dynamic_index_in_dim(w_shards, z ^ k, 0, keepdims=False) for k in range(4)]

    def input_terms(dqkv, scales, parts):
        return [
            (
                scales[:, 0:1] * times_trans(dqkv, w_k_parts[k])
                - parts[k].astype(f32) * (scales[:, 1:2] / feature_count)
            ).astype(bf16)
            for k in range(4)
        ]

    tail_end = gather_end(after(tail_far2, g_end, *head_near))
    tail_shards = shards(x_tail, tail_near, tail_far2, tail_end, z)
    raw1, inv1 = project(tail_shards, w_k_parts, (), feature_count)
    head_end = gather_end(after(head_far2, tail_end))
    w_o = after(w_o, head_far2)
    o_shards = w_o.reshape(4, local_features, q_cols)
    ga = [
        matmul(g_rows, w_o),
        sum(
            matmul(g_shards[k], lax.dynamic_index_in_dim(o_shards, z ^ k, 0, keepdims=False))
            for k in range(4)
        ),
    ]
    near = jnp.where(z % 2 == 1, *head_near)
    early = project([x_head, near, head_far2], w_k_parts[:3], (), 0)
    head_shards = shards(x_head, head_near, head_far2, after(head_end, raw1, *early, *ga), z)
    head_shards[1] = near
    raw0, inv0 = project(head_shards[3:], w_k_parts[3:], early, feature_count)
    dqkv, scales, scaled, out = attention(
        (raw0, raw1), (inv0, inv1), ga, adv, cos, sin, start
    )
    half = row_count // (2 * BLOCK) * BLOCK
    terms0 = input_terms(dqkv[:half], scales[:half], [x[:half] for x in head_shards])
    end0 = scatter_end(terms0)
    total0 = far_total(terms0, end0)
    step0 = scatter_far(total0)
    dx0 = scatter_near(terms0, step0, z)

    places = jnp.stack([z ^ j for j in range(4)]).astype(jnp.int32)
    weight_terms = weight_grads(
        places,
        head_shards,
        tail_shards,
        g_shards,
        g_rows,
        after(scaled, terms0[3]),
        out,
        gain_shards,
    )
    summed = lax.psum_scatter(after(weight_terms, end0), "fsdp", scatter_dimension=0, tiled=True)

    terms1 = input_terms(
        after(dqkv[half:], total0),
        scales[half:],
        [jnp.concatenate([x[half:], y], axis=0) for x, y in zip(head_shards, tail_shards)],
    )
    end1 = scatter_end([*terms1[:3], after(terms1[3], end0)])
    step1 = scatter_far(far_total(terms1, after(end1, *step0)))
    dx1 = scatter_near(terms1, (after(step1[0], dx0), step1[1]), z)
    dx = jnp.concatenate([dx0, dx1], axis=0)
    input_grad = (adv * log_prob_grad.astype(f32) + dx).astype(bf16)
    grad_q = summed[:, :q_cols]
    grad_k = summed[:, q_cols : q_cols + k_cols]
    grad_v = summed[:, q_cols + k_cols : qkv_cols]
    grad_o_t = summed[:, qkv_cols:]
    return (input_grad, grad_q, grad_k, grad_v, grad_o_t)


def solution(mesh):
    in_specs = (
        P("fsdp", None, "tp"),
        P("fsdp"),
        P("fsdp", None),
        P("fsdp"),
        P("fsdp", "tp"),
        P(),
        P("fsdp", "tp"),
        P("fsdp", "tp"),
        P("fsdp", "tp"),
        P("fsdp", "tp"),
    )
    out_specs = (
        P("fsdp", "tp"),
        P("fsdp", "tp"),
        P("fsdp", "tp"),
        P("fsdp", "tp"),
        P("fsdp", "tp"),
    )
    return jax.shard_map(
        per_device, mesh=mesh, in_specs=in_specs, out_specs=out_specs, check_vma=False
    )
```

```python
import functools

import jax
import jax.numpy as jnp
from jax import lax
from jax.experimental import pallas as pl
from jax.experimental.pallas import tpu as pltpu
from jax.sharding import PartitionSpec as P

KEY_VALUE_HEADS = 4
HD = 128
QUERY_HEADS = 16
GSIZE = 16
ROPE_BASE = 1000000.0
NORM_EPSILON = 1e-06
BLOCK = 128

UP = [(0, 1), (1, 2), (2, 3)]
DOWN = [(1, 0), (2, 1), (3, 2)]
UP_MID = [(1, 2), (2, 3)]
DOWN_MID = [(1, 0), (2, 1)]
TO_ENDS = [(2, 3), (1, 0)]
FROM_ENDS = [(3, 2), (0, 1)]
UP_IN = [(0, 1), (1, 2)]
DOWN_IN = [(3, 2), (2, 1)]


def contract_rows(left, right):
    return lax.dot_general(
        left, right, (((0,), (0,)), ((), ())), preferred_element_type=jnp.float32
    )


def times_trans(left, right):
    return lax.dot_general(
        left, right, (((1,), (1,)), ((), ())), preferred_element_type=jnp.float32
    )


def matmul(left, right):
    return jnp.dot(left, right, preferred_element_type=jnp.float32)


def gather_near(own):
    return lax.ppermute(own, "tp", UP), lax.ppermute(own, "tp", DOWN)


def gather_far(step1, z):
    up2 = lax.ppermute(step1[0], "tp", UP_MID)
    down2 = lax.ppermute(step1[1], "tp", DOWN_MID)
    return jnp.where(z >= 2, up2, down2)


def gather_end(far2):
    return lax.ppermute(far2, "tp", TO_ENDS)


def shards(own, step1, far2, far3, z):
    up1, down1 = step1
    near = jnp.where(z % 2 == 1, up1, down1)
    other = jnp.where(z == 1, down1, jnp.where(z == 2, up1, far3))
    return [own, near, far2, other]


def after(value, *earlier):
    return lax.optimization_barrier((value, *earlier))[0]


def scatter_end(parts):
    return lax.ppermute(parts[3], "tp", FROM_ENDS)


def far_total(parts, from_end):
    return (parts[2].astype(jnp.float32) + from_end.astype(jnp.float32)).astype(jnp.bfloat16)


def scatter_far(total2):
    return lax.ppermute(total2, "tp", UP_IN), lax.ppermute(total2, "tp", DOWN_IN)


def scatter_near(parts, step2, z):
    own, near, _, other = parts
    f32 = jnp.float32
    up2, down2 = step2
    go_up = jnp.where(z == 1, other, near).astype(f32) + up2.astype(f32)
    go_down = jnp.where(z == 2, other, near).astype(f32) + down2.astype(f32)
    up3 = lax.ppermute(go_up.astype(jnp.bfloat16), "tp", UP)
    down3 = lax.ppermute(go_down.astype(jnp.bfloat16), "tp", DOWN)
    return own.astype(f32) + up3.astype(f32) + down3.astype(f32)


def attention_kernel(*refs):
    raw_refs, inv_refs = refs[:2], refs[2:4]
    ga_ref, adv_ref, cos_ref, sin_ref, start_ref = refs[4:9]
    dqkv_ref, scale_ref, dscaled_ref, out_ref, qkv_b, dk_acc, dv_acc = refs[9:]
    heads = ga_ref.shape[1] // HD
    qw = heads * HD
    scale = HD ** (-0.5)
    f32, bf16 = jnp.float32, jnp.bfloat16
    pieces = list(zip(raw_refs, inv_refs, (0, raw_refs[0].shape[0])))
    edge = pl.ds(0, BLOCK)
    qkv_b[edge, :] = jnp.zeros((BLOCK, qkv_b.shape[1]), bf16)
    dk_acc[edge, :] = jnp.zeros((BLOCK, HD), f32)
    dv_acc[edge, :] = jnp.zeros((BLOCK, HD), f32)

    def turn(value, cos, sin):
        return value * cos + pltpu.roll(value, HD // 2, 1) * sin

    def rows_of(block, first):
        base = pl.multiple_of(block * BLOCK, BLOCK)
        return base + first, pl.ds(base, BLOCK), pl.ds(base + first, BLOCK)

    def forward_and_back(raw_ref, inv_ref, first, block, carry):
        base, local, here = rows_of(block, first)
        after = pl.ds(base + BLOCK, BLOCK)
        both = pl.ds(base, 2 * BLOCK)
        cos, sin = cos_ref[here, :], sin_ref[here, :]
        inv = inv_ref[local, :]
        for h in range(heads + 2):
            cols = slice(h * HD, (h + 1) * HD)
            linear = raw_ref[local, cols] * inv
            qkv_b[after, cols] = (turn(linear, cos, sin) if h <= heads else linear).astype(bf16)
        adv = adv_ref[here, :]
        qs = jnp.concatenate(
            [qkv_b[after, h * HD : (h + 1) * HD] for h in range(heads)], axis=0
        )
        gs = jnp.concatenate(
            [(ga_ref[here, h * HD : (h + 1) * HD] * adv).astype(bf16) for h in range(heads)],
            axis=0,
        )
        ks = qkv_b[both, qw : qw + HD]
        vs = qkv_b[both, qw + HD : qw + 2 * HD]
        start = start_ref[here, :] - (base - BLOCK)
        col = lax.broadcasted_iota(jnp.int32, (BLOCK, 2 * BLOCK), 1)
        row = lax.broadcasted_iota(jnp.int32, (BLOCK, 2 * BLOCK), 0) + BLOCK
        bias = jnp.where((col >= start) & (col <= row), 0.0, -1e30)
        bias = jnp.concatenate([bias] * heads, axis=0)
        scores = times_trans(qs, ks) * scale + bias
        top = jnp.max(scores, axis=-1, keepdims=True)
        weight = jnp.exp(scores - top)
        prob = weight / jnp.sum(weight, axis=-1, keepdims=True)
        prob_b = prob.astype(bf16)
        out = matmul(prob_b, vs)
        grad_prob = times_trans(gs, vs)
        delta = jnp.sum(prob * grad_prob, axis=-1, keepdims=True)
        ds = (prob * (grad_prob - delta) * scale).astype(bf16)
        dq = matmul(ds, ks)
        dk_acc[here, :] += contract_rows(ds[:, :BLOCK], qs)
        dk_acc[after, :] = contract_rows(ds[:, BLOCK:], qs)
        dv_acc[here, :] += contract_rows(prob_b[:, :BLOCK], gs)
        dv_acc[after, :] = contract_rows(prob_b[:, BLOCK:], gs)
        for h in range(heads):
            cols = slice(h * HD, (h + 1) * HD)
            part = slice(h * BLOCK, (h + 1) * BLOCK)
            out_ref[here, cols] = (out[part, :].astype(bf16).astype(f32) * adv).astype(bf16)
            dqkv_ref[here, cols] = turn(dq[part, :], cos, -sin).astype(bf16)
        return carry

    def finish(raw_ref, inv_ref, first, block, carry):
        base, local, here = rows_of(block, first)
        after = pl.ds(base + BLOCK, BLOCK)
        inv = inv_ref[local, :]
        total = jnp.zeros((BLOCK, 1), f32)
        for h in range(heads + 2):
            cols = slice(h * HD, (h + 1) * HD)
            if h < heads:
                grad = dqkv_ref[here, cols]
            elif h == heads:
                grad = turn(dk_acc[after, :], cos_ref[here, :], -sin_ref[here, :]).astype(bf16)
                dqkv_ref[here, cols] = grad
            else:
                grad = dv_acc[after, :].astype(bf16)
                dqkv_ref[here, cols] = grad
            grad = grad.astype(f32) * inv
            dscaled_ref[here, cols] = grad.astype(bf16)
            total += jnp.sum(grad * raw_ref[local, cols], axis=-1, keepdims=True)
        scale_ref[here, 0:1] = inv
        scale_ref[here, 1:2] = inv * inv * total
        return carry

    for body in (forward_and_back, finish):
        for piece in pieces:
            lax.fori_loop(0, piece[0].shape[0] // BLOCK, functools.partial(body, *piece), 0)


def attention(raw, inv, ga, adv, cos, sin, start):
    rows, width = adv.shape[0], raw[0].shape[1]
    qw = ga.shape[1]
    f32, bf16 = jnp.float32, jnp.bfloat16
    out_shape = [
        jax.ShapeDtypeStruct((rows, width), bf16),
        jax.ShapeDtypeStruct((rows, 2), f32),
        jax.ShapeDtypeStruct((rows, width), bf16),
        jax.ShapeDtypeStruct((rows, qw), bf16),
    ]
    operands = [*raw, *inv, ga, adv, cos, sin, start]
    vmem = pl.BlockSpec(memory_space=pltpu.VMEM)
    return pl.pallas_call(
        attention_kernel,
        out_shape=out_shape,
        in_specs=[vmem] * len(operands),
        out_specs=[vmem] * len(out_shape),
        scratch_shapes=[
            pltpu.VMEM((rows + BLOCK, width), bf16),
            pltpu.VMEM((rows + BLOCK, HD), f32),
            pltpu.VMEM((rows + BLOCK, HD), f32),
        ],
        compiler_params=pltpu.CompilerParams(vmem_limit_bytes=14 * 1024 * 1024),
        cost_estimate=pl.CostEstimate(
            flops=rows * 2 * BLOCK * HD * 12 * (qw // HD),
            bytes_accessed=rows * width * 8 + rows * qw * 6,
            transcendentals=rows * 2 * BLOCK * (qw // HD),
        ),
        name="attention",
    )(*operands)


def project_kernel(count, feature_count, *refs):
    x_refs, w_refs = refs[:count], refs[count : 2 * count]
    raw_ref, square_ref = refs[-2:]
    raw, squares = None, None
    if len(refs) > 2 * count + 2:
        raw, squares = refs[2 * count][...], refs[2 * count + 1][...]
    for x_ref, w_ref in zip(x_refs, w_refs):
        part = matmul(x_ref[...], w_ref[...])
        raw = part if raw is None else raw + part
        wide = x_ref[...].astype(jnp.float32)
        part = jnp.sum(wide * wide, axis=1, keepdims=True)
        squares = part if squares is None else squares + part
    raw_ref[...] = raw
    if feature_count:
        squares = lax.rsqrt(squares / feature_count + NORM_EPSILON)
    square_ref[...] = squares


def project(parts, weights, prior, feature_count):
    rows, width = parts[0].shape[0], weights[0].shape[1]
    operands = [*parts, *weights, *prior]
    vmem = pl.BlockSpec(memory_space=pltpu.VMEM)
    return pl.pallas_call(
        functools.partial(project_kernel, len(parts), feature_count),
        out_shape=[
            jax.ShapeDtypeStruct((rows, width), jnp.float32),
            jax.ShapeDtypeStruct((rows, 1), jnp.float32),
        ],
        in_specs=[vmem] * len(operands),
        out_specs=[vmem] * 2,
        compiler_params=pltpu.CompilerParams(vmem_limit_bytes=12 * 1024 * 1024),
        cost_estimate=pl.CostEstimate(
            flops=2 * len(parts) * rows * width * parts[0].shape[1],
            bytes_accessed=2 * len(parts) * parts[0].shape[1] * (rows + width) + 8 * rows * width,
            transcendentals=rows,
        ),
        name="project",
    )(*operands)


def weight_grad_kernel(place_ref, *refs):
    heads, tails, g_tails = refs[:4], refs[4:8], refs[8:12]
    g_ref, scaled_ref, out_ref, gain_ref, term_ref = refs[12:]
    width = scaled_ref.shape[1]
    gain = gain_ref[0]
    gain = jnp.transpose(jnp.broadcast_to(gain, (HD, gain.shape[1])))[:, 0:1]
    first, g_first = heads[0].shape[0], g_ref.shape[0]
    for k in range(4):

        @pl.when(place_ref[pl.program_id(0)] == k)
        def _():
            total = contract_rows(heads[k][...], scaled_ref[:first, :])
            total += contract_rows(tails[k][...], scaled_ref[first:, :])
            term_ref[:, :width] = (total * gain).astype(jnp.bfloat16)
            total = contract_rows(g_ref[...], out_ref[:g_first, :])
            total += contract_rows(g_tails[k][...], out_ref[g_first:, :])
            term_ref[:, width:] = total.astype(jnp.bfloat16)


def weight_grads(places, heads, tails, g_tails, g_rows, scaled, out, gain):
    features = gain.shape[2]
    width = scaled.shape[1] + out.shape[1]
    x_parts = [*heads, *tails, *g_tails]

    def once(o):
        return pl.BlockSpec(o.shape, lambda j, place: (0, 0), pipeline_mode=pl.Buffered(1))

    return pl.pallas_call(
        weight_grad_kernel,
        out_shape=jax.ShapeDtypeStruct((4 * features, width), jnp.bfloat16),
        grid_spec=pltpu.PrefetchScalarGridSpec(
            num_scalar_prefetch=1,
            grid=(4,),
            in_specs=[once(o) for o in x_parts]
            + [pl.BlockSpec((g_rows.shape[0], features), lambda j, place: (0, j))]
            + [once(scaled), once(out)]
            + [pl.BlockSpec((1, 1, features), lambda j, place: (j, 0, 0))],
            out_specs=pl.BlockSpec((features, width), lambda j, place: (j, 0)),
        ),
        compiler_params=pltpu.CompilerParams(vmem_limit_bytes=58 * 1024 * 1024),
        cost_estimate=pl.CostEstimate(
            flops=2 * scaled.shape[0] * 4 * features * width,
            bytes_accessed=4 * features * (4 * scaled.shape[0] + 2 * width),
            transcendentals=0,
        ),
        name="weight_grads",
    )(places, *x_parts, g_rows, scaled, out, gain)


def per_device(roll_rows, dest, lengths, clusters, log_prob_grad, gain, w_q, w_k, w_v, w_o_t):
    sequence_count = dest.shape[0]
    max_len, local_features = roll_rows.shape[1:]
    row_count = log_prob_grad.shape[0]
    replicas = lax.axis_size("fsdp")
    per_pair = sequence_count // replicas
    me = lax.axis_index("fsdp")
    z = lax.axis_index("tp")
    f32, bf16 = jnp.float32, jnp.bfloat16
    q_cols, k_cols = w_q.shape[1], w_k.shape[1]
    qkv_cols = q_cols + 2 * k_cols
    feature_count = gain.shape[0]

    bounds = [0, row_count - 2 * BLOCK, row_count]
    g_rows = lax.all_gather(log_prob_grad[: bounds[1], :], "tp", axis=1, tiled=True)
    g_tail = log_prob_grad[bounds[1] :, :]
    g_near = gather_near(g_tail)
    g_far2 = gather_far(g_near, z)
    g_end = gather_end(g_far2)
    g_shards = shards(g_tail, g_near, g_far2, g_end, z)

    slot_ids = jnp.arange(sequence_count, dtype=jnp.int32)
    earlier_dest = dest[None, :] < dest[:, None]
    send_block = jnp.sum(earlier_dest.astype(jnp.int32), axis=1)
    source = jnp.sum(
        jnp.where(send_block[None, :] == slot_ids[:, None], slot_ids[None, :], 0), axis=1
    )
    send_rows = jnp.take(roll_rows, source, axis=0, mode="clip")
    arrived_rows = lax.all_to_all(send_rows, "fsdp", split_axis=0, concat_axis=0, tiled=True)

    ballots = clusters.reshape(sequence_count // GSIZE, GSIZE)
    vote_share = jnp.mean((ballots[:, :, None] == ballots[:, None, :]).astype(f32), axis=2)
    advantage = (vote_share - jnp.mean(vote_share, axis=1, keepdims=True)).reshape(sequence_count)
    tags = jnp.stack([(dest % sequence_count).astype(f32), advantage], axis=1)
    picked = send_block[None, :] == slot_ids[:, None]
    tags = jnp.sum(jnp.where(picked[:, :, None], tags[None, :, :], 0.0), axis=1).astype(bf16)
    tags = lax.all_to_all(tags, "fsdp", split_axis=0, concat_axis=0, tiled=True).astype(f32)
    holder = tags[None, :, 0].astype(jnp.int32) == slot_ids[:, None]
    slot_of = jnp.sum(jnp.where(holder, slot_ids[None, :], 0), axis=1)
    seq_advantage = jnp.sum(jnp.where(holder, tags[None, :, 1], 0.0), axis=1)

    lengths_row = lengths.reshape(sequence_count)
    sequence_ends = jnp.cumsum(lengths_row)
    sequence_starts = sequence_ends - lengths_row
    row_index = jnp.arange(row_count, dtype=jnp.int32)
    one_hot = (sequence_ends[None, :] > row_index[:, None]) & (
        sequence_starts[None, :] <= row_index[:, None]
    )
    row_start = jnp.sum(jnp.where(one_hot, sequence_starts[None, :], 0), axis=1)
    position = row_index - row_start
    row_slot = jnp.sum(jnp.where(one_hot, slot_of[None, :], 0), axis=1)
    adv = jnp.sum(jnp.where(one_hot, seq_advantage[None, :], 0.0), axis=1)[:, None]
    half_width = HD // 2
    frequency = ROPE_BASE ** (-(2.0 * jnp.arange(half_width, dtype=f32)) / HD)
    angles = position.astype(f32)[:, None] * frequency[None, :]
    cos, sin = jnp.cos(angles), jnp.sin(angles)
    cos = jnp.concatenate([cos, cos], axis=1)
    sin = jnp.concatenate([-sin, sin], axis=1)

    start = row_start[:, None]
    arrived_rows = after(arrived_rows, cos, sin, start, adv)
    x_own = jnp.take(
        arrived_rows.reshape(sequence_count * max_len, local_features),
        row_slot * max_len + position,
        axis=0,
        mode="clip",
    )
    half = row_count // (2 * BLOCK) * BLOCK
    x_head, x_tail = x_own[:half, :], x_own[half:, :]
    tail_near = gather_near(x_tail)
    head_near = gather_near(after(x_head, tail_near[0], g_far2))
    tail_far2 = gather_far((after(tail_near[0], g_rows), tail_near[1]), z)
    head_far2 = gather_far((after(head_near[0], tail_far2), head_near[1]), z)

    w_qkv = lax.all_gather(
        jnp.concatenate([w_q, w_k, w_v], axis=1), "fsdp", axis=0, tiled=True
    )
    w_o = lax.all_gather(w_o_t, "fsdp", axis=0, tiled=True)
    gain_f = gain.astype(f32)
    gain_shards = gain_f.reshape(4, 1, local_features)
    w_shards = (w_qkv.astype(f32) * gain_f[:, None]).astype(bf16)
    w_shards = w_shards.reshape(4, local_features, qkv_cols)
    w_k_parts = [lax.dynamic_index_in_dim(w_shards, z ^ k, 0, keepdims=False) for k in range(4)]

    def input_terms(dqkv, scales, parts):
        return [
            (
                scales[:, 0:1] * times_trans(dqkv, w_k_parts[k])
                - parts[k].astype(f32) * (scales[:, 1:2] / feature_count)
            ).astype(bf16)
            for k in range(4)
        ]

    tail_end = gather_end(after(tail_far2, g_end, *head_near))
    tail_shards = shards(x_tail, tail_near, tail_far2, tail_end, z)
    raw1, inv1 = project(tail_shards, w_k_parts, (), feature_count)
    head_end = gather_end(head_far2)
    w_o = after(w_o, head_far2)
    o_shards = w_o.reshape(4, local_features, q_cols)
    ga_tail = sum(
        matmul(g_shards[k], lax.dynamic_index_in_dim(o_shards, z ^ k, 0, keepdims=False))
        for k in range(4)
    )
    ga = jnp.concatenate([matmul(g_rows, w_o), ga_tail], axis=0)
    near = jnp.where(z % 2 == 1, *head_near)
    early = project([x_head, near, head_far2], w_k_parts[:3], (), 0)
    head_shards = shards(x_head, head_near, head_far2, after(head_end, raw1, *early, ga), z)
    head_shards[1] = near
    raw0, inv0 = project(head_shards[3:], w_k_parts[3:], early, feature_count)
    dqkv, scales, scaled, out = attention(
        (raw0, raw1), (inv0, inv1), ga, adv, cos, sin, start
    )
    terms0 = input_terms(dqkv[:half], scales[:half], head_shards)
    end0 = scatter_end(terms0)
    total0 = far_total(terms0, end0)
    step0 = scatter_far(total0)
    dx0 = scatter_near(terms0, step0, z)

    places = jnp.stack([z ^ j for j in range(4)]).astype(jnp.int32)
    weight_terms = weight_grads(
        places,
        head_shards,
        tail_shards,
        g_shards,
        g_rows,
        after(scaled, terms0[3]),
        out,
        gain_shards,
    )
    summed = lax.psum_scatter(after(weight_terms, end0), "fsdp", scatter_dimension=0, tiled=True)

    terms1 = input_terms(after(dqkv[half:], total0), scales[half:], tail_shards)
    end1 = scatter_end([*terms1[:3], after(terms1[3], end0)])
    step1 = scatter_far(far_total(terms1, after(end1, *step0)))
    dx1 = scatter_near(terms1, (after(step1[0], dx0), step1[1]), z)
    dx = jnp.concatenate([dx0, dx1], axis=0)
    input_grad = (adv * log_prob_grad.astype(f32) + dx).astype(bf16)
    grad_q = summed[:, :q_cols]
    grad_k = summed[:, q_cols : q_cols + k_cols]
    grad_v = summed[:, q_cols + k_cols : qkv_cols]
    grad_o_t = summed[:, qkv_cols:]
    return (input_grad, grad_q, grad_k, grad_v, grad_o_t)


def solution(mesh):
    in_specs = (
        P("fsdp", None, "tp"),
        P("fsdp"),
        P("fsdp", None),
        P("fsdp"),
        P("fsdp", "tp"),
        P(),
        P("fsdp", "tp"),
        P("fsdp", "tp"),
        P("fsdp", "tp"),
        P("fsdp", "tp"),
    )
    out_specs = (
        P("fsdp", "tp"),
        P("fsdp", "tp"),
        P("fsdp", "tp"),
        P("fsdp", "tp"),
        P("fsdp", "tp"),
    )
    return jax.shard_map(
        per_device, mesh=mesh, in_specs=in_specs, out_specs=out_specs, check_vma=False
    )
```

```python
import functools

import jax
import jax.numpy as jnp
from jax import lax
from jax.experimental import pallas as pl
from jax.experimental.pallas import tpu as pltpu
from jax.sharding import PartitionSpec as P

KEY_VALUE_HEADS = 4
HD = 128
QUERY_HEADS = 16
GSIZE = 16
ROPE_BASE = 1000000.0
NORM_EPSILON = 1e-06
BLOCK = 128

UP = [(0, 1), (1, 2), (2, 3)]
DOWN = [(1, 0), (2, 1), (3, 2)]
UP_MID = [(1, 2), (2, 3)]
DOWN_MID = [(1, 0), (2, 1)]
TO_ENDS = [(2, 3), (1, 0)]
FROM_ENDS = [(3, 2), (0, 1)]
UP_IN = [(0, 1), (1, 2)]
DOWN_IN = [(3, 2), (2, 1)]


def contract_rows(left, right):
    return lax.dot_general(
        left, right, (((0,), (0,)), ((), ())), preferred_element_type=jnp.float32
    )


def times_trans(left, right):
    return lax.dot_general(
        left, right, (((1,), (1,)), ((), ())), preferred_element_type=jnp.float32
    )


def matmul(left, right):
    return jnp.dot(left, right, preferred_element_type=jnp.float32)


def gather_near(own):
    return lax.ppermute(own, "tp", UP), lax.ppermute(own, "tp", DOWN)


def gather_far(step1, z):
    up2 = lax.ppermute(step1[0], "tp", UP_MID)
    down2 = lax.ppermute(step1[1], "tp", DOWN_MID)
    return jnp.where(z >= 2, up2, down2)


def gather_end(far2):
    return lax.ppermute(far2, "tp", TO_ENDS)


def shards(own, step1, far2, far3, z):
    up1, down1 = step1
    near = jnp.where(z % 2 == 1, up1, down1)
    other = jnp.where(z == 1, down1, jnp.where(z == 2, up1, far3))
    return [own, near, far2, other]


def after(value, *earlier):
    return lax.optimization_barrier((value, *earlier))[0]


def scatter_end(parts):
    return lax.ppermute(parts[3], "tp", FROM_ENDS)


def far_total(parts, from_end):
    return (parts[2].astype(jnp.float32) + from_end.astype(jnp.float32)).astype(jnp.bfloat16)


def scatter_far(total2):
    return lax.ppermute(total2, "tp", UP_IN), lax.ppermute(total2, "tp", DOWN_IN)


def scatter_near(parts, step2, z):
    own, near, _, other = parts
    f32 = jnp.float32
    up2, down2 = step2
    go_up = jnp.where(z == 1, other, near).astype(f32) + up2.astype(f32)
    go_down = jnp.where(z == 2, other, near).astype(f32) + down2.astype(f32)
    up3 = lax.ppermute(go_up.astype(jnp.bfloat16), "tp", UP)
    down3 = lax.ppermute(go_down.astype(jnp.bfloat16), "tp", DOWN)
    return own.astype(f32) + up3.astype(f32) + down3.astype(f32)


def attention_kernel(*refs):
    raw_refs, inv_refs = refs[:2], refs[2:4]
    ga_ref, adv_ref, cos_ref, sin_ref, start_ref = refs[4:9]
    dqkv_ref, scale_ref, dscaled_ref, out_ref, qkv_b, dk_acc, dv_acc = refs[9:]
    heads = ga_ref.shape[1] // HD
    qw = heads * HD
    scale = HD ** (-0.5)
    f32, bf16 = jnp.float32, jnp.bfloat16
    pieces = list(zip(raw_refs, inv_refs, (0, raw_refs[0].shape[0])))
    edge = pl.ds(0, BLOCK)
    qkv_b[edge, :] = jnp.zeros((BLOCK, qkv_b.shape[1]), bf16)
    dk_acc[edge, :] = jnp.zeros((BLOCK, HD), f32)
    dv_acc[edge, :] = jnp.zeros((BLOCK, HD), f32)

    def turn(value, cos, sin):
        return value * cos + pltpu.roll(value, HD // 2, 1) * sin

    def rows_of(block, first):
        base = pl.multiple_of(block * BLOCK, BLOCK)
        return base + first, pl.ds(base, BLOCK), pl.ds(base + first, BLOCK)

    def forward_and_back(raw_ref, inv_ref, first, block, carry):
        base, local, here = rows_of(block, first)
        after = pl.ds(base + BLOCK, BLOCK)
        both = pl.ds(base, 2 * BLOCK)
        cos, sin = cos_ref[here, :], sin_ref[here, :]
        inv = inv_ref[local, :]
        for h in range(heads + 2):
            cols = slice(h * HD, (h + 1) * HD)
            linear = raw_ref[local, cols] * inv
            qkv_b[after, cols] = (turn(linear, cos, sin) if h <= heads else linear).astype(bf16)
        adv = adv_ref[here, :]
        qs = jnp.concatenate(
            [qkv_b[after, h * HD : (h + 1) * HD] for h in range(heads)], axis=0
        )
        gs = jnp.concatenate(
            [(ga_ref[here, h * HD : (h + 1) * HD] * adv).astype(bf16) for h in range(heads)],
            axis=0,
        )
        ks = qkv_b[both, qw : qw + HD]
        vs = qkv_b[both, qw + HD : qw + 2 * HD]
        start = start_ref[here, :] - (base - BLOCK)
        col = lax.broadcasted_iota(jnp.int32, (BLOCK, 2 * BLOCK), 1)
        row = lax.broadcasted_iota(jnp.int32, (BLOCK, 2 * BLOCK), 0) + BLOCK
        bias = jnp.where((col >= start) & (col <= row), 0.0, -1e30)
        bias = jnp.concatenate([bias] * heads, axis=0)
        scores = times_trans(qs, ks) * scale + bias
        top = jnp.max(scores, axis=-1, keepdims=True)
        weight = jnp.exp(scores - top)
        prob = weight / jnp.sum(weight, axis=-1, keepdims=True)
        prob_b = prob.astype(bf16)
        out = matmul(prob_b, vs)
        grad_prob = times_trans(gs, vs)
        delta = jnp.sum(prob * grad_prob, axis=-1, keepdims=True)
        ds = (prob * (grad_prob - delta) * scale).astype(bf16)
        dq = matmul(ds, ks)
        dk_acc[here, :] += contract_rows(ds[:, :BLOCK], qs)
        dk_acc[after, :] = contract_rows(ds[:, BLOCK:], qs)
        dv_acc[here, :] += contract_rows(prob_b[:, :BLOCK], gs)
        dv_acc[after, :] = contract_rows(prob_b[:, BLOCK:], gs)
        for h in range(heads):
            cols = slice(h * HD, (h + 1) * HD)
            part = slice(h * BLOCK, (h + 1) * BLOCK)
            out_ref[here, cols] = (out[part, :].astype(bf16).astype(f32) * adv).astype(bf16)
            dqkv_ref[here, cols] = turn(dq[part, :], cos, -sin).astype(bf16)
        return carry

    def finish(raw_ref, inv_ref, first, block, carry):
        base, local, here = rows_of(block, first)
        after = pl.ds(base + BLOCK, BLOCK)
        inv = inv_ref[local, :]
        total = jnp.zeros((BLOCK, 1), f32)
        for h in range(heads + 2):
            cols = slice(h * HD, (h + 1) * HD)
            if h < heads:
                grad = dqkv_ref[here, cols]
            elif h == heads:
                grad = turn(dk_acc[after, :], cos_ref[here, :], -sin_ref[here, :]).astype(bf16)
                dqkv_ref[here, cols] = grad
            else:
                grad = dv_acc[after, :].astype(bf16)
                dqkv_ref[here, cols] = grad
            grad = grad.astype(f32) * inv
            dscaled_ref[here, cols] = grad.astype(bf16)
            total += jnp.sum(grad * raw_ref[local, cols], axis=-1, keepdims=True)
        scale_ref[here, 0:1] = inv
        scale_ref[here, 1:2] = inv * inv * total
        return carry

    for body in (forward_and_back, finish):
        for piece in pieces:
            lax.fori_loop(0, piece[0].shape[0] // BLOCK, functools.partial(body, *piece), 0)


def attention(raw, inv, ga, adv, cos, sin, start):
    rows, width = adv.shape[0], raw[0].shape[1]
    qw = ga.shape[1]
    f32, bf16 = jnp.float32, jnp.bfloat16
    out_shape = [
        jax.ShapeDtypeStruct((rows, width), bf16),
        jax.ShapeDtypeStruct((rows, 2), f32),
        jax.ShapeDtypeStruct((rows, width), bf16),
        jax.ShapeDtypeStruct((rows, qw), bf16),
    ]
    operands = [*raw, *inv, ga, adv, cos, sin, start]
    vmem = pl.BlockSpec(memory_space=pltpu.VMEM)
    return pl.pallas_call(
        attention_kernel,
        out_shape=out_shape,
        in_specs=[vmem] * len(operands),
        out_specs=[vmem] * len(out_shape),
        scratch_shapes=[
            pltpu.VMEM((rows + BLOCK, width), bf16),
            pltpu.VMEM((rows + BLOCK, HD), f32),
            pltpu.VMEM((rows + BLOCK, HD), f32),
        ],
        compiler_params=pltpu.CompilerParams(vmem_limit_bytes=14 * 1024 * 1024),
        cost_estimate=pl.CostEstimate(
            flops=rows * 2 * BLOCK * HD * 12 * (qw // HD),
            bytes_accessed=rows * width * 8 + rows * qw * 6,
            transcendentals=rows * 2 * BLOCK * (qw // HD),
        ),
        name="attention",
    )(*operands)


def project_kernel(count, feature_count, *refs):
    x_refs, w_refs = refs[:count], refs[count : 2 * count]
    raw_ref, square_ref = refs[-2:]
    raw, squares = None, None
    if len(refs) > 2 * count + 2:
        raw, squares = refs[2 * count][...], refs[2 * count + 1][...]
    for x_ref, w_ref in zip(x_refs, w_refs):
        part = matmul(x_ref[...], w_ref[...])
        raw = part if raw is None else raw + part
        wide = x_ref[...].astype(jnp.float32)
        part = jnp.sum(wide * wide, axis=1, keepdims=True)
        squares = part if squares is None else squares + part
    raw_ref[...] = raw
    if feature_count:
        squares = lax.rsqrt(squares / feature_count + NORM_EPSILON)
    square_ref[...] = squares


def project(parts, weights, prior, feature_count):
    rows, width = parts[0].shape[0], weights[0].shape[1]
    operands = [*parts, *weights, *prior]
    vmem = pl.BlockSpec(memory_space=pltpu.VMEM)
    return pl.pallas_call(
        functools.partial(project_kernel, len(parts), feature_count),
        out_shape=[
            jax.ShapeDtypeStruct((rows, width), jnp.float32),
            jax.ShapeDtypeStruct((rows, 1), jnp.float32),
        ],
        in_specs=[vmem] * len(operands),
        out_specs=[vmem] * 2,
        compiler_params=pltpu.CompilerParams(vmem_limit_bytes=12 * 1024 * 1024),
        cost_estimate=pl.CostEstimate(
            flops=2 * len(parts) * rows * width * parts[0].shape[1],
            bytes_accessed=2 * len(parts) * parts[0].shape[1] * (rows + width) + 8 * rows * width,
            transcendentals=rows,
        ),
        name="project",
    )(*operands)


def weight_grad_kernel(place_ref, *refs):
    heads, tails, g_tails = refs[:4], refs[4:8], refs[8:12]
    g_ref, scaled_ref, out_ref, gain_ref, term_ref = refs[12:]
    width = scaled_ref.shape[1]
    gain = gain_ref[0]
    gain = jnp.transpose(jnp.broadcast_to(gain, (HD, gain.shape[1])))[:, 0:1]
    first, g_first = heads[0].shape[0], g_ref.shape[0]
    for k in range(4):

        @pl.when(place_ref[pl.program_id(0)] == k)
        def _():
            total = contract_rows(heads[k][...], scaled_ref[:first, :])
            total += contract_rows(tails[k][...], scaled_ref[first:, :])
            term_ref[:, :width] = (total * gain).astype(jnp.bfloat16)
            total = contract_rows(g_ref[...], out_ref[:g_first, :])
            total += contract_rows(g_tails[k][...], out_ref[g_first:, :])
            term_ref[:, width:] = total.astype(jnp.bfloat16)


def weight_grads(places, heads, tails, g_tails, g_rows, scaled, out, gain):
    features = gain.shape[2]
    width = scaled.shape[1] + out.shape[1]
    x_parts = [*heads, *tails, *g_tails]

    def once(o):
        return pl.BlockSpec(o.shape, lambda j, place: (0, 0), pipeline_mode=pl.Buffered(1))

    return pl.pallas_call(
        weight_grad_kernel,
        out_shape=jax.ShapeDtypeStruct((4 * features, width), jnp.bfloat16),
        grid_spec=pltpu.PrefetchScalarGridSpec(
            num_scalar_prefetch=1,
            grid=(4,),
            in_specs=[once(o) for o in x_parts]
            + [pl.BlockSpec((g_rows.shape[0], features), lambda j, place: (0, j))]
            + [once(scaled), once(out)]
            + [pl.BlockSpec((1, 1, features), lambda j, place: (j, 0, 0))],
            out_specs=pl.BlockSpec((features, width), lambda j, place: (j, 0)),
        ),
        compiler_params=pltpu.CompilerParams(vmem_limit_bytes=58 * 1024 * 1024),
        cost_estimate=pl.CostEstimate(
            flops=2 * scaled.shape[0] * 4 * features * width,
            bytes_accessed=4 * features * (4 * scaled.shape[0] + 2 * width),
            transcendentals=0,
        ),
        name="weight_grads",
    )(places, *x_parts, g_rows, scaled, out, gain)


def per_device(roll_rows, dest, lengths, clusters, log_prob_grad, gain, w_q, w_k, w_v, w_o_t):
    sequence_count = dest.shape[0]
    max_len, local_features = roll_rows.shape[1:]
    row_count = log_prob_grad.shape[0]
    replicas = lax.axis_size("fsdp")
    per_pair = sequence_count // replicas
    me = lax.axis_index("fsdp")
    z = lax.axis_index("tp")
    f32, bf16 = jnp.float32, jnp.bfloat16
    q_cols, k_cols = w_q.shape[1], w_k.shape[1]
    qkv_cols = q_cols + 2 * k_cols
    feature_count = gain.shape[0]

    bounds = [0, row_count - 2 * BLOCK, row_count]
    g_rows = lax.all_gather(log_prob_grad[: bounds[1], :], "tp", axis=1, tiled=True)
    g_tail = log_prob_grad[bounds[1] :, :]
    g_near = gather_near(g_tail)
    g_far2 = gather_far(g_near, z)
    g_end = gather_end(g_far2)
    g_shards = shards(g_tail, g_near, g_far2, g_end, z)

    slot_ids = jnp.arange(sequence_count, dtype=jnp.int32)
    earlier_dest = dest[None, :] < dest[:, None]
    send_block = jnp.sum(earlier_dest.astype(jnp.int32), axis=1)
    source = jnp.sum(
        jnp.where(send_block[None, :] == slot_ids[:, None], slot_ids[None, :], 0), axis=1
    )
    send_rows = jnp.take(roll_rows, source, axis=0, mode="clip")
    arrived_rows = lax.all_to_all(send_rows, "fsdp", split_axis=0, concat_axis=0, tiled=True)

    ballots = clusters.reshape(sequence_count // GSIZE, GSIZE)
    vote_share = jnp.mean((ballots[:, :, None] == ballots[:, None, :]).astype(f32), axis=2)
    advantage = (vote_share - jnp.mean(vote_share, axis=1, keepdims=True)).reshape(sequence_count)
    tags = jnp.stack([(dest % sequence_count).astype(f32), advantage], axis=1)
    picked = send_block[None, :] == slot_ids[:, None]
    tags = jnp.sum(jnp.where(picked[:, :, None], tags[None, :, :], 0.0), axis=1).astype(bf16)
    tags = lax.all_to_all(tags, "fsdp", split_axis=0, concat_axis=0, tiled=True).astype(f32)
    holder = tags[None, :, 0].astype(jnp.int32) == slot_ids[:, None]
    slot_of = jnp.sum(jnp.where(holder, slot_ids[None, :], 0), axis=1)
    seq_advantage = jnp.sum(jnp.where(holder, tags[None, :, 1], 0.0), axis=1)

    lengths_row = lengths.reshape(sequence_count)
    sequence_ends = jnp.cumsum(lengths_row)
    sequence_starts = sequence_ends - lengths_row
    row_index = jnp.arange(row_count, dtype=jnp.int32)
    one_hot = (sequence_ends[None, :] > row_index[:, None]) & (
        sequence_starts[None, :] <= row_index[:, None]
    )
    row_start = jnp.sum(jnp.where(one_hot, sequence_starts[None, :], 0), axis=1)
    position = row_index - row_start
    row_slot = jnp.sum(jnp.where(one_hot, slot_of[None, :], 0), axis=1)
    adv = jnp.sum(jnp.where(one_hot, seq_advantage[None, :], 0.0), axis=1)[:, None]
    half_width = HD // 2
    frequency = ROPE_BASE ** (-(2.0 * jnp.arange(half_width, dtype=f32)) / HD)
    angles = position.astype(f32)[:, None] * frequency[None, :]
    cos, sin = jnp.cos(angles), jnp.sin(angles)
    cos = jnp.concatenate([cos, cos], axis=1)
    sin = jnp.concatenate([-sin, sin], axis=1)

    start = row_start[:, None]
    arrived_rows = after(arrived_rows, cos, sin, start, adv)
    x_own = jnp.take(
        arrived_rows.reshape(sequence_count * max_len, local_features),
        row_slot * max_len + position,
        axis=0,
        mode="clip",
    )
    half = row_count // (2 * BLOCK) * BLOCK
    x_head, x_tail = x_own[:half, :], x_own[half:, :]
    tail_near = gather_near(x_tail)
    head_near = gather_near(after(x_head, tail_near[0], g_far2))
    tail_far2 = gather_far((after(tail_near[0], g_rows), tail_near[1]), z)
    head_far2 = gather_far((after(head_near[0], tail_far2), head_near[1]), z)

    own_qkv = jnp.concatenate([w_q, w_k, w_v], axis=1)
    w_qkv = lax.all_gather(own_qkv, "fsdp", axis=0, tiled=True)
    w_o = lax.all_gather(after(w_o_t, own_qkv), "fsdp", axis=0, tiled=True)
    gain_f = gain.astype(f32)
    gain_shards = gain_f.reshape(4, 1, local_features)
    w_shards = (w_qkv.astype(f32) * gain_f[:, None]).astype(bf16)
    w_shards = w_shards.reshape(4, local_features, qkv_cols)
    w_k_parts = [lax.dynamic_index_in_dim(w_shards, z ^ k, 0, keepdims=False) for k in range(4)]

    def input_terms(dqkv, scales, parts):
        return [
            (
                scales[:, 0:1] * times_trans(dqkv, w_k_parts[k])
                - parts[k].astype(f32) * (scales[:, 1:2] / feature_count)
            ).astype(bf16)
            for k in range(4)
        ]

    tail_end = gather_end(after(tail_far2, g_end, *head_near))
    near = jnp.where(z % 2 == 1, *head_near)
    early = project([x_head, near, head_far2], w_k_parts[:3], (), 0)
    tail_shards = shards(x_tail, tail_near, tail_far2, after(tail_end, early[0]), z)
    raw1, inv1 = project(tail_shards, w_k_parts, (), feature_count)
    head_end = gather_end(head_far2)
    w_o = after(w_o, early[0])
    o_shards = w_o.reshape(4, local_features, q_cols)
    ga_tail = sum(
        matmul(g_shards[k], lax.dynamic_index_in_dim(o_shards, z ^ k, 0, keepdims=False))
        for k in range(4)
    )
    ga = jnp.concatenate([matmul(g_rows, w_o), ga_tail], axis=0)
    head_shards = shards(x_head, head_near, head_far2, after(head_end, raw1, *early, ga), z)
    head_shards[1] = near
    raw0, inv0 = project(head_shards[3:], w_k_parts[3:], early, feature_count)
    dqkv, scales, scaled, out = attention(
        (raw0, raw1), (inv0, inv1), ga, adv, cos, sin, start
    )
    terms0 = input_terms(dqkv[:half], scales[:half], head_shards)
    end0 = scatter_end(terms0)
    total0 = far_total(terms0, end0)
    step0 = scatter_far(total0)
    dx0 = scatter_near(terms0, step0, z)

    places = jnp.stack([z ^ j for j in range(4)]).astype(jnp.int32)
    weight_terms = weight_grads(
        places,
        head_shards,
        tail_shards,
        g_shards,
        g_rows,
        after(scaled, terms0[3]),
        out,
        gain_shards,
    )
    summed = lax.psum_scatter(after(weight_terms, end0), "fsdp", scatter_dimension=0, tiled=True)

    terms1 = input_terms(after(dqkv[half:], total0), scales[half:], tail_shards)
    end1 = scatter_end([*terms1[:3], after(terms1[3], end0)])
    step1 = scatter_far(far_total(terms1, after(end1, *step0)))
    dx1 = scatter_near(terms1, (after(step1[0], dx0), step1[1]), z)
    dx = jnp.concatenate([dx0, dx1], axis=0)
    input_grad = (adv * log_prob_grad.astype(f32) + dx).astype(bf16)
    grad_q = summed[:, :q_cols]
    grad_k = summed[:, q_cols : q_cols + k_cols]
    grad_v = summed[:, q_cols + k_cols : qkv_cols]
    grad_o_t = summed[:, qkv_cols:]
    return (input_grad, grad_q, grad_k, grad_v, grad_o_t)


def solution(mesh):
    in_specs = (
        P("fsdp", None, "tp"),
        P("fsdp"),
        P("fsdp", None),
        P("fsdp"),
        P("fsdp", "tp"),
        P(),
        P("fsdp", "tp"),
        P("fsdp", "tp"),
        P("fsdp", "tp"),
        P("fsdp", "tp"),
    )
    out_specs = (
        P("fsdp", "tp"),
        P("fsdp", "tp"),
        P("fsdp", "tp"),
        P("fsdp", "tp"),
        P("fsdp", "tp"),
    )
    return jax.shard_map(
        per_device, mesh=mesh, in_specs=in_specs, out_specs=out_specs, check_vma=False
    )
```

```python
import functools

import jax
import jax.numpy as jnp
from jax import lax
from jax.experimental import pallas as pl
from jax.experimental.pallas import tpu as pltpu
from jax.sharding import PartitionSpec as P

KEY_VALUE_HEADS = 4
HD = 128
QUERY_HEADS = 16
GSIZE = 16
ROPE_BASE = 1000000.0
NORM_EPSILON = 1e-06
BLOCK = 128

UP = [(0, 1), (1, 2), (2, 3)]
DOWN = [(1, 0), (2, 1), (3, 2)]
UP_MID = [(1, 2), (2, 3)]
DOWN_MID = [(1, 0), (2, 1)]
TO_ENDS = [(2, 3), (1, 0)]
FROM_ENDS = [(3, 2), (0, 1)]
UP_IN = [(0, 1), (1, 2)]
DOWN_IN = [(3, 2), (2, 1)]


def contract_rows(left, right):
    return lax.dot_general(
        left, right, (((0,), (0,)), ((), ())), preferred_element_type=jnp.float32
    )


def times_trans(left, right):
    return lax.dot_general(
        left, right, (((1,), (1,)), ((), ())), preferred_element_type=jnp.float32
    )


def matmul(left, right):
    return jnp.dot(left, right, preferred_element_type=jnp.float32)


def gather_near(own):
    return lax.ppermute(own, "tp", UP), lax.ppermute(own, "tp", DOWN)


def gather_far(step1, z):
    up2 = lax.ppermute(step1[0], "tp", UP_MID)
    down2 = lax.ppermute(step1[1], "tp", DOWN_MID)
    return jnp.where(z >= 2, up2, down2)


def gather_end(far2):
    return lax.ppermute(far2, "tp", TO_ENDS)


def shards(own, step1, far2, far3, z):
    up1, down1 = step1
    near = jnp.where(z % 2 == 1, up1, down1)
    other = jnp.where(z == 1, down1, jnp.where(z == 2, up1, far3))
    return [own, near, far2, other]


def after(value, *earlier):
    return lax.optimization_barrier((value, *earlier))[0]


def scatter_end(parts):
    return lax.ppermute(parts[3], "tp", FROM_ENDS)


def far_total(parts, from_end):
    return (parts[2].astype(jnp.float32) + from_end.astype(jnp.float32)).astype(jnp.bfloat16)


def scatter_far(total2):
    return lax.ppermute(total2, "tp", UP_IN), lax.ppermute(total2, "tp", DOWN_IN)


def scatter_near(parts, step2, z):
    own, near, _, other = parts
    f32 = jnp.float32
    up2, down2 = step2
    go_up = jnp.where(z == 1, other, near).astype(f32) + up2.astype(f32)
    go_down = jnp.where(z == 2, other, near).astype(f32) + down2.astype(f32)
    up3 = lax.ppermute(go_up.astype(jnp.bfloat16), "tp", UP)
    down3 = lax.ppermute(go_down.astype(jnp.bfloat16), "tp", DOWN)
    return own.astype(f32) + up3.astype(f32) + down3.astype(f32)


def attention_kernel(*refs):
    raw_refs, inv_refs = refs[:2], refs[2:4]
    ga_ref, adv_ref, cos_ref, sin_ref, start_ref = refs[4:9]
    dqkv_ref, scale_ref, dscaled_ref, out_ref, qkv_b, dk_acc, dv_acc = refs[9:]
    heads = ga_ref.shape[1] // HD
    qw = heads * HD
    scale = HD ** (-0.5)
    f32, bf16 = jnp.float32, jnp.bfloat16
    pieces = list(zip(raw_refs, inv_refs, (0, raw_refs[0].shape[0])))
    edge = pl.ds(0, BLOCK)
    qkv_b[edge, :] = jnp.zeros((BLOCK, qkv_b.shape[1]), bf16)
    dk_acc[edge, :] = jnp.zeros((BLOCK, HD), f32)
    dv_acc[edge, :] = jnp.zeros((BLOCK, HD), f32)

    def turn(value, cos, sin):
        return value * cos + pltpu.roll(value, HD // 2, 1) * sin

    def rows_of(block, first):
        base = pl.multiple_of(block * BLOCK, BLOCK)
        return base + first, pl.ds(base, BLOCK), pl.ds(base + first, BLOCK)

    def forward_and_back(raw_ref, inv_ref, first, block, carry):
        base, local, here = rows_of(block, first)
        after = pl.ds(base + BLOCK, BLOCK)
        both = pl.ds(base, 2 * BLOCK)
        cos, sin = cos_ref[here, :], sin_ref[here, :]
        inv = inv_ref[local, :]
        for h in range(heads + 2):
            cols = slice(h * HD, (h + 1) * HD)
            linear = raw_ref[local, cols] * inv
            qkv_b[after, cols] = (turn(linear, cos, sin) if h <= heads else linear).astype(bf16)
        adv = adv_ref[here, :]
        qs = jnp.concatenate(
            [qkv_b[after, h * HD : (h + 1) * HD] for h in range(heads)], axis=0
        )
        gs = jnp.concatenate(
            [(ga_ref[here, h * HD : (h + 1) * HD] * adv).astype(bf16) for h in range(heads)],
            axis=0,
        )
        ks = qkv_b[both, qw : qw + HD]
        vs = qkv_b[both, qw + HD : qw + 2 * HD]
        start = start_ref[here, :] - (base - BLOCK)
        col = lax.broadcasted_iota(jnp.int32, (BLOCK, 2 * BLOCK), 1)
        row = lax.broadcasted_iota(jnp.int32, (BLOCK, 2 * BLOCK), 0) + BLOCK
        bias = jnp.where((col >= start) & (col <= row), 0.0, -1e30)
        bias = jnp.concatenate([bias] * heads, axis=0)
        scores = times_trans(qs, ks) * scale + bias
        top = jnp.max(scores, axis=-1, keepdims=True)
        weight = jnp.exp(scores - top)
        prob = weight / jnp.sum(weight, axis=-1, keepdims=True)
        prob_b = prob.astype(bf16)
        out = matmul(prob_b, vs)
        grad_prob = times_trans(gs, vs)
        delta = jnp.sum(prob * grad_prob, axis=-1, keepdims=True)
        ds = (prob * (grad_prob - delta) * scale).astype(bf16)
        dq = matmul(ds, ks)
        dk_acc[here, :] += contract_rows(ds[:, :BLOCK], qs)
        dk_acc[after, :] = contract_rows(ds[:, BLOCK:], qs)
        dv_acc[here, :] += contract_rows(prob_b[:, :BLOCK], gs)
        dv_acc[after, :] = contract_rows(prob_b[:, BLOCK:], gs)
        for h in range(heads):
            cols = slice(h * HD, (h + 1) * HD)
            part = slice(h * BLOCK, (h + 1) * BLOCK)
            out_ref[here, cols] = (out[part, :].astype(bf16).astype(f32) * adv).astype(bf16)
            dqkv_ref[here, cols] = turn(dq[part, :], cos, -sin).astype(bf16)
        return carry

    def finish(raw_ref, inv_ref, first, block, carry):
        base, local, here = rows_of(block, first)
        after = pl.ds(base + BLOCK, BLOCK)
        inv = inv_ref[local, :]
        total = jnp.zeros((BLOCK, 1), f32)
        for h in range(heads + 2):
            cols = slice(h * HD, (h + 1) * HD)
            if h < heads:
                grad = dqkv_ref[here, cols]
            elif h == heads:
                grad = turn(dk_acc[after, :], cos_ref[here, :], -sin_ref[here, :]).astype(bf16)
                dqkv_ref[here, cols] = grad
            else:
                grad = dv_acc[after, :].astype(bf16)
                dqkv_ref[here, cols] = grad
            grad = grad.astype(f32) * inv
            dscaled_ref[here, cols] = grad.astype(bf16)
            total += jnp.sum(grad * raw_ref[local, cols], axis=-1, keepdims=True)
        scale_ref[here, 0:1] = inv
        scale_ref[here, 1:2] = inv * inv * total
        return carry

    for body in (forward_and_back, finish):
        for piece in pieces:
            lax.fori_loop(0, piece[0].shape[0] // BLOCK, functools.partial(body, *piece), 0)


def attention(raw, inv, ga, adv, cos, sin, start):
    rows, width = adv.shape[0], raw[0].shape[1]
    qw = ga.shape[1]
    f32, bf16 = jnp.float32, jnp.bfloat16
    out_shape = [
        jax.ShapeDtypeStruct((rows, width), bf16),
        jax.ShapeDtypeStruct((rows, 2), f32),
        jax.ShapeDtypeStruct((rows, width), bf16),
        jax.ShapeDtypeStruct((rows, qw), bf16),
    ]
    operands = [*raw, *inv, ga, adv, cos, sin, start]
    vmem = pl.BlockSpec(memory_space=pltpu.VMEM)
    return pl.pallas_call(
        attention_kernel,
        out_shape=out_shape,
        in_specs=[vmem] * len(operands),
        out_specs=[vmem] * len(out_shape),
        scratch_shapes=[
            pltpu.VMEM((rows + BLOCK, width), bf16),
            pltpu.VMEM((rows + BLOCK, HD), f32),
            pltpu.VMEM((rows + BLOCK, HD), f32),
        ],
        compiler_params=pltpu.CompilerParams(vmem_limit_bytes=14 * 1024 * 1024),
        cost_estimate=pl.CostEstimate(
            flops=rows * 2 * BLOCK * HD * 12 * (qw // HD),
            bytes_accessed=rows * width * 8 + rows * qw * 6,
            transcendentals=rows * 2 * BLOCK * (qw // HD),
        ),
        name="attention",
    )(*operands)


def project_kernel(count, feature_count, *refs):
    x_refs, w_refs = refs[:count], refs[count : 2 * count]
    raw_ref, square_ref = refs[-2:]
    raw, squares = None, None
    if len(refs) > 2 * count + 2:
        raw, squares = refs[2 * count][...], refs[2 * count + 1][...]
    for x_ref, w_ref in zip(x_refs, w_refs):
        part = matmul(x_ref[...], w_ref[...])
        raw = part if raw is None else raw + part
        wide = x_ref[...].astype(jnp.float32)
        part = jnp.sum(wide * wide, axis=1, keepdims=True)
        squares = part if squares is None else squares + part
    raw_ref[...] = raw
    if feature_count:
        squares = lax.rsqrt(squares / feature_count + NORM_EPSILON)
    square_ref[...] = squares


def project(parts, weights, prior, feature_count):
    rows, width = parts[0].shape[0], weights[0].shape[1]
    operands = [*parts, *weights, *prior]
    vmem = pl.BlockSpec(memory_space=pltpu.VMEM)
    return pl.pallas_call(
        functools.partial(project_kernel, len(parts), feature_count),
        out_shape=[
            jax.ShapeDtypeStruct((rows, width), jnp.float32),
            jax.ShapeDtypeStruct((rows, 1), jnp.float32),
        ],
        in_specs=[vmem] * len(operands),
        out_specs=[vmem] * 2,
        compiler_params=pltpu.CompilerParams(vmem_limit_bytes=12 * 1024 * 1024),
        cost_estimate=pl.CostEstimate(
            flops=2 * len(parts) * rows * width * parts[0].shape[1],
            bytes_accessed=2 * len(parts) * parts[0].shape[1] * (rows + width) + 8 * rows * width,
            transcendentals=rows,
        ),
        name="project",
    )(*operands)


def weight_grad_kernel(place_ref, *refs):
    heads, tails, g_tails = refs[:4], refs[4:8], refs[8:12]
    g_ref, scaled_ref, out_ref, gain_ref, term_ref = refs[12:]
    width = scaled_ref.shape[1]
    gain = gain_ref[0]
    gain = jnp.transpose(jnp.broadcast_to(gain, (HD, gain.shape[1])))[:, 0:1]
    first, g_first = heads[0].shape[0], g_ref.shape[0]
    for k in range(4):

        @pl.when(place_ref[pl.program_id(0)] == k)
        def _():
            total = contract_rows(heads[k][...], scaled_ref[:first, :])
            total += contract_rows(tails[k][...], scaled_ref[first:, :])
            term_ref[:, :width] = (total * gain).astype(jnp.bfloat16)
            total = contract_rows(g_ref[...], out_ref[:g_first, :])
            total += contract_rows(g_tails[k][...], out_ref[g_first:, :])
            term_ref[:, width:] = total.astype(jnp.bfloat16)


def weight_grads(places, heads, tails, g_tails, g_rows, scaled, out, gain):
    features = gain.shape[2]
    width = scaled.shape[1] + out.shape[1]
    x_parts = [*heads, *tails, *g_tails]

    def once(o):
        return pl.BlockSpec(o.shape, lambda j, place: (0, 0), pipeline_mode=pl.Buffered(1))

    return pl.pallas_call(
        weight_grad_kernel,
        out_shape=jax.ShapeDtypeStruct((4 * features, width), jnp.bfloat16),
        grid_spec=pltpu.PrefetchScalarGridSpec(
            num_scalar_prefetch=1,
            grid=(4,),
            in_specs=[once(o) for o in x_parts]
            + [pl.BlockSpec((g_rows.shape[0], features), lambda j, place: (0, j))]
            + [once(scaled), once(out)]
            + [pl.BlockSpec((1, 1, features), lambda j, place: (j, 0, 0))],
            out_specs=pl.BlockSpec((features, width), lambda j, place: (j, 0)),
        ),
        compiler_params=pltpu.CompilerParams(vmem_limit_bytes=58 * 1024 * 1024),
        cost_estimate=pl.CostEstimate(
            flops=2 * scaled.shape[0] * 4 * features * width,
            bytes_accessed=4 * features * (4 * scaled.shape[0] + 2 * width),
            transcendentals=0,
        ),
        name="weight_grads",
    )(places, *x_parts, g_rows, scaled, out, gain)


def per_device(roll_rows, dest, lengths, clusters, log_prob_grad, gain, w_q, w_k, w_v, w_o_t):
    sequence_count = dest.shape[0]
    max_len, local_features = roll_rows.shape[1:]
    row_count = log_prob_grad.shape[0]
    replicas = lax.axis_size("fsdp")
    per_pair = sequence_count // replicas
    me = lax.axis_index("fsdp")
    z = lax.axis_index("tp")
    f32, bf16 = jnp.float32, jnp.bfloat16
    q_cols, k_cols = w_q.shape[1], w_k.shape[1]
    qkv_cols = q_cols + 2 * k_cols
    feature_count = gain.shape[0]

    bounds = [0, row_count - 2 * BLOCK, row_count]
    g_rows = lax.all_gather(log_prob_grad[: bounds[1], :], "tp", axis=1, tiled=True)
    g_tail = log_prob_grad[bounds[1] :, :]
    g_near = gather_near(g_tail)
    g_far2 = gather_far(g_near, z)
    g_end = gather_end(g_far2)
    g_shards = shards(g_tail, g_near, g_far2, g_end, z)

    slot_ids = jnp.arange(sequence_count, dtype=jnp.int32)
    earlier_dest = dest[None, :] < dest[:, None]
    send_block = jnp.sum(earlier_dest.astype(jnp.int32), axis=1)
    source = jnp.sum(
        jnp.where(send_block[None, :] == slot_ids[:, None], slot_ids[None, :], 0), axis=1
    )
    send_rows = jnp.take(roll_rows, source, axis=0, mode="clip")
    arrived_rows = lax.all_to_all(send_rows, "fsdp", split_axis=0, concat_axis=0, tiled=True)

    ballots = clusters.reshape(sequence_count // GSIZE, GSIZE)
    vote_share = jnp.mean((ballots[:, :, None] == ballots[:, None, :]).astype(f32), axis=2)
    advantage = (vote_share - jnp.mean(vote_share, axis=1, keepdims=True)).reshape(sequence_count)
    tags = jnp.stack([(dest % sequence_count).astype(f32), advantage], axis=1)
    picked = send_block[None, :] == slot_ids[:, None]
    tags = jnp.sum(jnp.where(picked[:, :, None], tags[None, :, :], 0.0), axis=1).astype(bf16)
    tags = lax.all_to_all(tags, "fsdp", split_axis=0, concat_axis=0, tiled=True).astype(f32)
    holder = tags[None, :, 0].astype(jnp.int32) == slot_ids[:, None]
    slot_of = jnp.sum(jnp.where(holder, slot_ids[None, :], 0), axis=1)
    seq_advantage = jnp.sum(jnp.where(holder, tags[None, :, 1], 0.0), axis=1)

    lengths_row = lengths.reshape(sequence_count)
    sequence_ends = jnp.cumsum(lengths_row)
    sequence_starts = sequence_ends - lengths_row
    row_index = jnp.arange(row_count, dtype=jnp.int32)
    one_hot = (sequence_ends[None, :] > row_index[:, None]) & (
        sequence_starts[None, :] <= row_index[:, None]
    )
    row_start = jnp.sum(jnp.where(one_hot, sequence_starts[None, :], 0), axis=1)
    position = row_index - row_start
    row_slot = jnp.sum(jnp.where(one_hot, slot_of[None, :], 0), axis=1)
    adv = jnp.sum(jnp.where(one_hot, seq_advantage[None, :], 0.0), axis=1)[:, None]
    half_width = HD // 2
    frequency = ROPE_BASE ** (-(2.0 * jnp.arange(half_width, dtype=f32)) / HD)
    angles = position.astype(f32)[:, None] * frequency[None, :]
    cos, sin = jnp.cos(angles), jnp.sin(angles)
    cos = jnp.concatenate([cos, cos], axis=1)
    sin = jnp.concatenate([-sin, sin], axis=1)

    start = row_start[:, None]
    arrived_rows = after(arrived_rows, cos, sin, start, adv)
    x_own = jnp.take(
        arrived_rows.reshape(sequence_count * max_len, local_features),
        row_slot * max_len + position,
        axis=0,
        mode="clip",
    )
    half = row_count // (2 * BLOCK) * BLOCK
    x_head, x_tail = x_own[:half, :], x_own[half:, :]
    tail_near = gather_near(x_tail)
    head_near = gather_near(after(x_head, tail_near[0], g_far2))
    tail_far2 = gather_far((after(tail_near[0], g_rows), tail_near[1]), z)
    head_far2 = gather_far((after(head_near[0], tail_far2), head_near[1]), z)

    gain_f = gain.astype(f32)
    own_gain = lax.dynamic_slice_in_dim(gain_f, me * w_q.shape[0], w_q.shape[0], 0)
    own_qkv = jnp.concatenate([w_q, w_k, w_v], axis=1).astype(f32) * own_gain[:, None]
    w_qkv = lax.all_gather(own_qkv.astype(bf16), "fsdp", axis=0, tiled=True)
    w_o = lax.all_gather(w_o_t, "fsdp", axis=0, tiled=True)
    gain_shards = gain_f.reshape(4, 1, local_features)
    w_shards = w_qkv.reshape(4, local_features, qkv_cols)
    w_k_parts = [lax.dynamic_index_in_dim(w_shards, z ^ k, 0, keepdims=False) for k in range(4)]

    def input_terms(dqkv, scales, parts):
        return [
            (
                scales[:, 0:1] * times_trans(dqkv, w_k_parts[k])
                - parts[k].astype(f32) * (scales[:, 1:2] / feature_count)
            ).astype(bf16)
            for k in range(4)
        ]

    tail_end = gather_end(after(tail_far2, g_end, *head_near))
    tail_shards = shards(x_tail, tail_near, tail_far2, tail_end, z)
    raw1, inv1 = project(tail_shards, w_k_parts, (), feature_count)
    head_end = gather_end(head_far2)
    w_o = after(w_o, head_far2)
    o_shards = w_o.reshape(4, local_features, q_cols)
    ga_tail = sum(
        matmul(g_shards[k], lax.dynamic_index_in_dim(o_shards, z ^ k, 0, keepdims=False))
        for k in range(4)
    )
    ga = jnp.concatenate([matmul(g_rows, w_o), ga_tail], axis=0)
    near = jnp.where(z % 2 == 1, *head_near)
    early = project([x_head, near, head_far2], w_k_parts[:3], (), 0)
    head_shards = shards(x_head, head_near, head_far2, after(head_end, raw1, *early, ga), z)
    head_shards[1] = near
    raw0, inv0 = project(head_shards[3:], w_k_parts[3:], early, feature_count)
    dqkv, scales, scaled, out = attention(
        (raw0, raw1), (inv0, inv1), ga, adv, cos, sin, start
    )
    terms0 = input_terms(dqkv[:half], scales[:half], head_shards)
    end0 = scatter_end(terms0)
    total0 = far_total(terms0, end0)
    step0 = scatter_far(total0)
    dx0 = scatter_near(terms0, step0, z)

    places = jnp.stack([z ^ j for j in range(4)]).astype(jnp.int32)
    weight_terms = weight_grads(
        places,
        head_shards,
        tail_shards,
        g_shards,
        g_rows,
        after(scaled, terms0[3]),
        out,
        gain_shards,
    )
    summed = lax.psum_scatter(after(weight_terms, end0), "fsdp", scatter_dimension=0, tiled=True)

    terms1 = input_terms(after(dqkv[half:], total0), scales[half:], tail_shards)
    end1 = scatter_end([*terms1[:3], after(terms1[3], end0)])
    step1 = scatter_far(far_total(terms1, after(end1, *step0)))
    dx1 = scatter_near(terms1, (after(step1[0], dx0), step1[1]), z)
    dx = jnp.concatenate([dx0, dx1], axis=0)
    input_grad = (adv * log_prob_grad.astype(f32) + dx).astype(bf16)
    grad_q = summed[:, :q_cols]
    grad_k = summed[:, q_cols : q_cols + k_cols]
    grad_v = summed[:, q_cols + k_cols : qkv_cols]
    grad_o_t = summed[:, qkv_cols:]
    return (input_grad, grad_q, grad_k, grad_v, grad_o_t)


def solution(mesh):
    in_specs = (
        P("fsdp", None, "tp"),
        P("fsdp"),
        P("fsdp", None),
        P("fsdp"),
        P("fsdp", "tp"),
        P(),
        P("fsdp", "tp"),
        P("fsdp", "tp"),
        P("fsdp", "tp"),
        P("fsdp", "tp"),
    )
    out_specs = (
        P("fsdp", "tp"),
        P("fsdp", "tp"),
        P("fsdp", "tp"),
        P("fsdp", "tp"),
        P("fsdp", "tp"),
    )
    return jax.shard_map(
        per_device, mesh=mesh, in_specs=in_specs, out_specs=out_specs, check_vma=False
    )
```
